32 devices in a mesh: dp: 4 (over z), seq: 4 (over y, x), heads: 2 (over core).
Axes of the slice: x: 2, y: 2, z: 4, core: 2. Of those that a mesh axis runs over, the one named last changes fastest.
Arguments:
- hidden_in: bfloat16 [4, 3072, 2048], P('dp', ('seq', 'heads')), may hold values from -6 to 6
- out_cotangent: bfloat16 [4, 3072, 2048], P('dp', ('seq', 'heads')), may hold values from -6 to 6
- lengths: int32 [4, 2], P('dp'), may hold values from 1024 to 2048, as said below
- norm_gain: float32 [2048], replicated, may hold values from 0.5 to 1.5
- q_weight: bfloat16 [2048, 2048], P(None, 'heads'), may hold values from -0.125 to 0.125
- k_weight: bfloat16 [2048, 2048], P(None, 'heads'), may hold values from -0.125 to 0.125
- v_weight: bfloat16 [2048, 4096], P(None, 'heads'), may hold values from -0.125 to 0.125
- gate_weight: bfloat16 [2048, 4096], P(None, 'heads'), may hold values from -0.125 to 0.125
- decay_weight: bfloat16 [2048, 16], P(None, 'heads'), may hold values from -0.125 to 0.125
- beta_weight: bfloat16 [2048, 16], P(None, 'heads'), may hold values from -0.125 to 0.125
- conv_q: float32 [4, 2048], P(None, 'heads'), may hold values from -3 to 3
- conv_k: float32 [4, 2048], P(None, 'heads'), may hold values from -3 to 3
- conv_v: float32 [4, 4096], P(None, 'heads'), may hold values from -3 to 3
- decay_log: float32 [16], P('heads'), may hold values from -7 to -3.5
- decay_bias: float32 [16], P('heads'), may hold values from -1 to 1
- out_gain: float32 [256], replicated, may hold values from 0.5 to 1.5
- out_weight: bfloat16 [4096, 2048], P('heads'), may hold values from -0.1875 to 0.1875
- ffn_gain: float32 [2048], replicated, may hold values from 0.5 to 1.5
- ffn_gate: bfloat16 [2048, 5632], P(None, 'heads'), may hold values from -0.125 to 0.125
- ffn_up: bfloat16 [2048, 5632], P(None, 'heads'), may hold values from -0.125 to 0.125
- ffn_down: bfloat16 [5632, 2048], P('heads'), may hold values from -0.15625 to 0.15625
Outputs:
- output: bfloat16 [4, 3072, 2048], P('dp', ('seq', 'heads'))
- input_grad: float32 [4, 3072, 2048], P('dp', ('seq', 'heads'))
- norm_gain_grad: float32 [2048], replicated
- q_weight_grad: float32 [2048, 2048], P(('dp', 'seq'), 'heads')
- k_weight_grad: float32 [2048, 2048], P(('dp', 'seq'), 'heads')
- v_weight_grad: float32 [2048, 4096], P(('dp', 'seq'), 'heads')
- gate_weight_grad: float32 [2048, 4096], P(('dp', 'seq'), 'heads')
- decay_weight_grad: float32 [2048, 16], P(('dp', 'seq'), 'heads')
- beta_weight_grad: float32 [2048, 16], P(('dp', 'seq'), 'heads')
- conv_q_grad: float32 [4, 2048], replicated
- conv_k_grad: float32 [4, 2048], replicated
- conv_v_grad: float32 [4, 4096], replicated
- decay_log_grad: float32 [16], replicated
- decay_bias_grad: float32 [16], replicated
- out_gain_grad: float32 [256], replicated
- out_weight_grad: float32 [4096, 2048], P('heads', ('dp', 'seq'))
- ffn_gain_grad: float32 [2048], replicated
- ffn_gate_grad: float32 [2048, 5632], P(('dp', 'seq'), 'heads')
- ffn_up_grad: float32 [2048, 5632], P(('dp', 'seq'), 'heads')
- ffn_down_grad: float32 [5632, 2048], P('heads', ('dp', 'seq'))
The draws below stay inside these ranges and needn't reach their ends.
Inputs may be any that keep to these rules, and one draw needn't show every extreme that they name: Row b holds the lengths of batch index b's two sequences in order: one of 1024 tokens and one of 2048 tokens, in either order.
All inputs are finite; a program needn't handle non-finite values.
Results may differ from the reference program's by a relative error of at most 0.02.
Values may be sent and summed in bfloat16 or wider, within the bound.
A program may use at most 448 MiB of HBM per device.

```python
import jax
import jax.numpy as jnp
from jax import lax

D = 2048
HEADS = 16
DK = 128
DV = 256
FF = 5632
GROUP = 64
KCONV = 4
SHORT = 1024
SEQLEN = 3072
BATCH = 4


def draw_lengths(key, part):
    flips = jax.random.randint(key, (BATCH,), 0, 2)
    first = SHORT + flips * SHORT
    second = 3 * SHORT - first
    return jnp.stack([first, second], axis=1).astype(jnp.int32)


def levels(own_key, dims, shards, smallest, high):
    factor_of = 1.0
    for dim, blocks in shards:
        heights = jax.random.uniform(jax.random.fold_in(jax.random.fold_in(own_key, 6), dim), (blocks,), jnp.float32, smallest / len(shards), high / len(shards))
        factor_of = factor_of * jnp.repeat(jnp.exp(heights), dims[dim] // blocks).reshape((-1,) + (1,) * (len(dims) - 1 - dim))
    return factor_of


def gaussian(own_key, extent, scale, bound, shards=(), held_as=jnp.bfloat16):
    drawn = jax.random.normal(own_key, extent, jnp.float32) * scale
    if len(shards) > 0:
        drawn = levels(own_key, extent, shards, -0.22, 0.18) * drawn
    return jnp.clip(drawn, min=-bound, max=bound).astype(held_as)


def setup_inputs(seed: int = 0) -> dict:
    seeds = jax.random.split(jax.random.key(seed), 22)
    hidden_in = gaussian(seeds[0], (BATCH, SEQLEN, D), 1.0, 6.0, ((0, 4), (1, 8)))
    out_cotangent = gaussian(seeds[1], (BATCH, SEQLEN, D), 1.0, 6.0, ((0, 4), (1, 8)))
    lengths = draw_lengths(jax.random.fold_in(seeds[21], 71), 0)
    norm_gain = jnp.clip(1.0 + 0.1 * jax.random.normal(seeds[3], (D,), jnp.float32), 0.5, 1.5)
    q_weight = gaussian(seeds[4], (D, HEADS * DK), D ** -0.5, 0.125, ((1, 2),))
    k_weight = gaussian(seeds[5], (D, HEADS * DK), D ** -0.5, 0.125, ((1, 2),))
    v_weight = gaussian(seeds[6], (D, HEADS * DV), D ** -0.5, 0.125, ((1, 2),))
    gate_weight = gaussian(seeds[7], (D, HEADS * DV), D ** -0.5, 0.125, ((1, 2),))
    decay_weight = gaussian(seeds[8], (D, HEADS), D ** -0.5, 0.125, ((1, 2),))
    beta_weight = gaussian(seeds[9], (D, HEADS), D ** -0.5, 0.125, ((1, 2),))
    conv_q = gaussian(seeds[10], (KCONV, HEADS * DK), 0.5, 3.0, ((1, 2),), jnp.float32)
    conv_k = gaussian(seeds[11], (KCONV, HEADS * DK), 0.5, 3.0, ((1, 2),), jnp.float32)
    conv_v = gaussian(seeds[12], (KCONV, HEADS * DV), 0.5, 3.0, ((1, 2),), jnp.float32)
    decay_log = jnp.clip(-7.0 + 3.5 * jax.random.uniform(seeds[13], (HEADS,), jnp.float32) ** levels(seeds[13], (HEADS,), ((0, 2),), -0.2, 0.2), -7.0, -3.5)
    decay_bias = jnp.clip(jax.random.uniform(seeds[14], (HEADS,), jnp.float32, -1.0, 1.0) * levels(seeds[14], (HEADS,), ((0, 2),), -0.4, 0.0), -1.0, 1.0)
    out_gain = jnp.clip(1.0 + 0.1 * jax.random.normal(seeds[15], (DV,), jnp.float32), 0.5, 1.5)
    out_weight = gaussian(seeds[16], (HEADS * DV, D), (HEADS * DV // 4) ** -0.5, 0.1875, ((0, 2),))
    ffn_gain = jnp.clip(1.0 + 0.1 * jax.random.normal(seeds[17], (D,), jnp.float32), 0.5, 1.5)
    ffn_gate = gaussian(seeds[18], (D, FF), D ** -0.5, 0.125, ((1, 2),))
    ffn_up = gaussian(seeds[19], (D, FF), D ** -0.5, 0.125, ((1, 2),))
    ffn_down = gaussian(seeds[20], (FF, D), (FF // 4) ** -0.5, 0.15625, ((0, 2),))
    return dict(hidden_in=hidden_in, out_cotangent=out_cotangent, lengths=lengths, norm_gain=norm_gain, q_weight=q_weight, k_weight=k_weight, v_weight=v_weight, gate_weight=gate_weight, decay_weight=decay_weight, beta_weight=beta_weight, conv_q=conv_q, conv_k=conv_k, conv_v=conv_v, decay_log=decay_log, decay_bias=decay_bias, out_gain=out_gain, out_weight=out_weight, ffn_gain=ffn_gain, ffn_gate=ffn_gate, ffn_up=ffn_up, ffn_down=ffn_down)


@jax.custom_vjp
def low(v):
    return lax.optimization_barrier(v.astype(jnp.bfloat16)).astype(jnp.float32)

@jax.custom_vjp
def low_back(v):
    return v

def low_keep(v):
    return (low(v), None)

def low_pass(kept, grad):
    return (grad,)

def back_keep(v):
    return (v, None)

def back_low(kept, grad):
    return (low(grad),)
low.defvjp(low_keep, low_pass)
low_back.defvjp(back_keep, back_low)
EPS = 1e-06
PRECISE_MODE = lax.Precision.HIGHEST

def matmul(left, right):
    return jnp.dot(left, right, precision=PRECISE_MODE)

def rms_scale(values, gain):
    return values * lax.rsqrt(lax.optimization_barrier(jnp.mean(values * values, axis=-1, keepdims=True)) + EPS) * gain

def unit_rows(values):
    return values * lax.rsqrt(lax.optimization_barrier(jnp.sum(values * values, axis=-1, keepdims=True)) + EPS)

def short_conv(padded, weight, valid):
    taps = weight.shape[0]
    count = padded.shape[0] - taps + 1
    total = padded[0:count] * weight[0] * valid[:, 0:1]
    for tap in range(1, taps):
        total = total + padded[tap:tap + count] * weight[tap] * valid[:, tap:tap + 1]
    return jax.nn.silu(total)

def prepare(q_ext, k_ext, v_ext, decay_proj, beta_proj, conv_q, conv_k, conv_v, decay_log, decay_bias, valid):
    count = decay_proj.shape[0]
    heads = decay_proj.shape[1]
    query_vector = unit_rows(short_conv(q_ext, conv_q, valid).reshape(count, heads, -1))
    query_vector = query_vector * query_vector.shape[-1] ** (-0.5)
    key_vector = unit_rows(short_conv(k_ext, conv_k, valid).reshape(count, heads, -1))
    value = short_conv(v_ext, conv_v, valid).reshape(count, heads, -1)
    log_decay = -jnp.exp(decay_log) * jax.nn.softplus(decay_proj + decay_bias)
    beta = jax.nn.sigmoid(beta_proj)
    return (query_vector, key_vector, value, log_decay, beta)

def group_local(query_vector, key_vector, value, log_decay, beta):
    size = log_decay.shape[-1]
    cumul = jnp.cumsum(log_decay, axis=-1)
    order = jnp.arange(size)
    below = (order[:, None] > order[None, :]).astype(log_decay.dtype)
    within = (order[:, None] >= order[None, :]).astype(log_decay.dtype)
    spread = jnp.exp((cumul[..., :, None] - cumul[..., None, :]) * within) * within
    keys = jnp.einsum('nhik,nhjk->nhij', key_vector, key_vector, precision=PRECISE_MODE)
    unit = jnp.eye(size, dtype=log_decay.dtype) + beta[..., :, None] * keys * spread * below
    growth_factor = jnp.exp(cumul)
    right = jnp.concatenate([beta[..., None] * value, (beta * growth_factor)[..., None] * key_vector], axis=-1)
    solved_system = jax.scipy.linalg.solve_triangular(unit, right, lower=True, unit_diagonal=True)
    value_width = value.shape[-1]
    scores = jnp.einsum('nhik,nhjk->nhij', query_vector, key_vector, precision=PRECISE_MODE) * spread
    tail_tokens = jnp.exp(cumul[..., -1:] - cumul)
    return (solved_system[..., :value_width], solved_system[..., value_width:], scores, growth_factor[..., None] * query_vector, tail_tokens[..., None] * key_vector, jnp.exp(cumul[..., -1]))

def group_state(memory_state, u_part, w_part, scores, grown_query, tail_key, last_growth, keep):
    memory_state = memory_state * keep
    delta_update = u_part - jnp.einsum('lwo,loq->lwq', w_part, memory_state, precision=PRECISE_MODE)
    output_rows = jnp.einsum('lwo,loq->lwq', grown_query, memory_state, precision=PRECISE_MODE)
    output_rows = output_rows + jnp.einsum('hij,hjv->hiv', scores, delta_update, precision=PRECISE_MODE)
    updated_state = last_growth[:, None, None] * memory_state
    updated_state = updated_state + jnp.einsum('biw,bir->bwr', tail_key, delta_update, precision=PRECISE_MODE)
    return (updated_state, output_rows)

def run_span(memory_state, query_vector, key_vector, value, log_decay, beta, keep):
    count, heads = log_decay.shape
    blocks = keep.shape[0]
    size = count // blocks

    def split(values):
        shaped = values.reshape((blocks, size, heads) + values.shape[2:])
        return jnp.swapaxes(shaped, 1, 2)
    local = group_local(split(query_vector), split(key_vector), split(value), split(log_decay), split(beta))
    step_fn = jax.checkpoint(group_state)

    def advance(carry, items):
        return step_fn(carry, *items)
    final, outs = lax.scan(advance, memory_state, local + (keep,))
    outs = jnp.swapaxes(outs, 1, 2).reshape(count, heads, -1)
    return (final, outs)

def gate_piece(mixed, gate_proj, out_gain):
    count, heads, width = mixed.shape
    gates = jax.nn.silu(gate_proj.reshape(count, heads, width))
    return (rms_scale(mixed, out_gain) * gates).reshape(count, heads * width)

def forward_row(row, params, lens):
    norm_gain, q_weight, k_weight, v_weight, gate_weight, decay_weight, beta_weight, conv_q, conv_k, conv_v, decay_log, decay_bias, out_gain, out_weight, ffn_gain, ffn_gate, ffn_up, ffn_down = params
    count = row.shape[0]
    first = lens[0]
    index = jnp.arange(count, dtype=jnp.int32)
    place = index - jnp.where(index >= first, first, 0)
    taps = conv_q.shape[0]
    valid = jnp.stack([place >= taps - 1 - tap for tap in range(taps)], axis=1).astype(row.dtype)
    starts = jnp.arange(count // GROUP, dtype=jnp.int32) * GROUP
    keep = ((starts != 0) & (starts != first)).astype(row.dtype)
    normed = low(rms_scale(row, norm_gain))
    q_proj = low_back(matmul(normed, q_weight))
    k_proj = low_back(matmul(normed, k_weight))
    v_proj = low_back(matmul(normed, v_weight))
    gate_proj = low_back(matmul(normed, gate_weight))
    decay_proj = low_back(matmul(normed, decay_weight))
    beta_proj = low_back(matmul(normed, beta_weight))

    def extend(values):
        return jnp.concatenate([jnp.zeros((taps - 1, values.shape[1]), row.dtype), values], axis=0)
    query_vector, key_vector, value, log_decay, beta = prepare(extend(q_proj), extend(k_proj), extend(v_proj), decay_proj, beta_proj, conv_q, conv_k, conv_v, decay_log, decay_bias, valid)
    heads = log_decay.shape[1]
    start = jnp.zeros((heads, key_vector.shape[2], value.shape[2]), row.dtype)
    final, mixed = run_span(start, query_vector, key_vector, value, log_decay, beta, keep)
    gated = low(gate_piece(mixed, gate_proj, out_gain))
    middle = row + low_back(matmul(gated, out_weight))
    ffn_in = low(rms_scale(middle, ffn_gain))
    gate_ffn = low_back(matmul(ffn_in, ffn_gate))
    up_ffn = low_back(matmul(ffn_in, ffn_up))
    act = low(jax.nn.silu(gate_ffn) * up_ffn)
    return middle + matmul(act, ffn_down)

def reference(hidden_in, out_cotangent, lengths, norm_gain, q_weight, k_weight, v_weight, gate_weight, decay_weight, beta_weight, conv_q, conv_k, conv_v, decay_log, decay_bias, out_gain, out_weight, ffn_gain, ffn_gate, ffn_up, ffn_down):
    params = tuple((p.astype(jnp.float32) for p in (norm_gain, q_weight, k_weight, v_weight, gate_weight, decay_weight, beta_weight, conv_q, conv_k, conv_v, decay_log, decay_bias, out_gain, out_weight, ffn_gain, ffn_gate, ffn_up, ffn_down)))

    def row_grads(carry, item):
        row, cot, lens = item

        def apply(row_in, pars):
            return forward_row(row_in, pars, lens)
        result, pull = jax.vjp(apply, row.astype(jnp.float32), params)
        d_row, d_pars = pull(cot.astype(jnp.float32))
        carry = jax.tree.map(jnp.add, carry, d_pars)
        return (carry, (result.astype(jnp.bfloat16), d_row))
    init = tuple((jnp.zeros_like(p) for p in params))
    grads, (output, input_grad) = lax.scan(row_grads, init, (hidden_in, out_cotangent, lengths))
    return (output, input_grad, grads[0], grads[1], grads[2], grads[3], grads[4], grads[5], grads[6], grads[7], grads[8], grads[9], grads[10], grads[11], grads[12], grads[13], grads[14], grads[15], grads[16], grads[17])
```

```python
import jax
import jax.numpy as jnp
import numpy as np
from jax import lax
from jax.sharding import PartitionSpec as P

HEADS = 16
DK = 128
DV = 256
GROUP = 64


EPS = 1e-06
PRECISE_MODE = lax.Precision.HIGHEST


def shifted(value, axis, steps):
    count = lax.axis_size(axis)
    leading, last = (max(0, -steps), min(count, count - steps))
    return lax.ppermute(value, axis, [(source, source + steps) for source in range(leading, last)])


def prefix(array, axis, combine, identity):
    size, mine = (lax.axis_size(axis), lax.axis_index(axis))
    everything = jax.tree.map(lambda part: lax.all_gather(part, axis), array)
    start = jax.tree.map(
        lambda part, zero: jnp.broadcast_to(jnp.asarray(zero, part.dtype), part.shape),
        array,
        identity,
    )

    def hop(k, before):
        reached = k < mine
        new = combine(before, jax.tree.map(lambda part: part[k], everything))
        return jax.tree.map(lambda a, b: jnp.where(reached, a, b), new, before)

    return lax.fori_loop(0, size, hop, start)


def prefix_2(array, axis, join, neutral):
    count = lax.axis_size(axis)
    place = lax.axis_index(axis)
    ahead = count - 1 - place
    gathered = jax.tree.map(
        lambda a, kind: lax.all_gather(a.astype(kind), axis),
        array,
        jax.tree.map(lambda a: jnp.bfloat16 if a.dtype == jnp.float32 else a.dtype, array),
    )
    state = jax.tree.map(lambda a, e: jnp.zeros_like(a) + jnp.asarray(e, a.dtype), array, neutral)

    def one(hop, state):
        source = count - 1 - hop
        return join(
            state,
            jax.tree.map(
                lambda a, own: lax.dynamic_index_in_dim(a, source, 0, False).astype(own.dtype),
                gathered,
                array,
            ),
        )

    return lax.fori_loop(0, ahead, one, state)


def rms_scale(values, gain):
    return values * lax.rsqrt(jnp.mean(values * values, axis=-1, keepdims=True) + EPS) * gain


def unit_rows(values):
    return values * lax.rsqrt(jnp.sum(values * values, axis=-1, keepdims=True) + EPS)


def short_conv(padded, weight, valid):
    taps = weight.shape[0]
    count = padded.shape[0] - taps + 1
    total = padded[0:count] * weight[0] * valid[:, 0:1]
    for tap in range(1, taps):
        total = total + padded[tap : tap + count] * weight[tap] * valid[:, tap : tap + 1]
    return jax.nn.silu(total)


def prepare(
    q_ext, k_ext, v_ext, decay_proj, beta_proj, conv_q, conv_k, conv_v, decay_log, decay_bias, valid
):
    count = decay_proj.shape[0]
    heads = decay_proj.shape[1]
    query_vector = unit_rows(short_conv(q_ext, conv_q, valid).reshape(count, heads, -1))
    query_vector = query_vector * query_vector.shape[-1] ** (-0.5)
    key_vector = unit_rows(short_conv(k_ext, conv_k, valid).reshape(count, heads, -1))
    value = short_conv(v_ext, conv_v, valid).reshape(count, heads, -1)
    log_decay = -jnp.exp(decay_log) * jax.nn.softplus(decay_proj + decay_bias)
    beta = jax.nn.sigmoid(beta_proj)
    return (query_vector, key_vector, value, log_decay, beta)


def group_local(query_vector, key_vector, value, log_decay, beta):
    size = log_decay.shape[-1]
    cumul = jnp.cumsum(log_decay, axis=-1)
    order = jnp.arange(size)
    below = (order[:, None] > order[None, :]).astype(log_decay.dtype)
    within = (order[:, None] >= order[None, :]).astype(log_decay.dtype)
    spread = jnp.exp((cumul[..., :, None] - cumul[..., None, :]) * within) * within
    keys = jnp.einsum("nhik,nhjk->nhij", key_vector, key_vector, precision=PRECISE_MODE)
    unit = jnp.eye(size, dtype=log_decay.dtype) + beta[..., :, None] * keys * spread * below
    growth_factor = jnp.exp(cumul)
    right = jnp.concatenate(
        [beta[..., None] * value, (beta * growth_factor)[..., None] * key_vector], axis=-1
    )
    solved_system = jax.scipy.linalg.solve_triangular(unit, right, lower=True, unit_diagonal=True)
    value_width = value.shape[-1]
    scores = (
        jnp.einsum("nhik,nhjk->nhij", query_vector, key_vector, precision=PRECISE_MODE) * spread
    )
    tail_tokens = jnp.exp(cumul[..., -1:] - cumul)
    return (
        solved_system[..., :value_width],
        solved_system[..., value_width:],
        scores,
        growth_factor[..., None] * query_vector,
        tail_tokens[..., None] * key_vector,
        jnp.exp(cumul[..., -1]),
    )


def group_state(memory_state, u_part, w_part, scores, grown_query, tail_key, last_growth, keep):
    memory_state = memory_state * keep
    delta_update = u_part - jnp.einsum("lwo,loq->lwq", w_part, memory_state, precision=PRECISE_MODE)
    output_rows = jnp.einsum("lwo,loq->lwq", grown_query, memory_state, precision=PRECISE_MODE)
    output_rows = output_rows + jnp.einsum(
        "hij,hjv->hiv", scores, delta_update, precision=PRECISE_MODE
    )
    updated_state = last_growth[:, None, None] * memory_state
    updated_state = updated_state + jnp.einsum(
        "biw,bir->bwr", tail_key, delta_update, precision=PRECISE_MODE
    )
    return (updated_state, output_rows)


def run_span(memory_state, query_vector, key_vector, value, log_decay, beta, keep):
    count, heads = log_decay.shape
    blocks = keep.shape[0]
    size = count // blocks

    def split(values):
        shaped = values.reshape((blocks, size, heads) + values.shape[2:])
        return jnp.swapaxes(shaped, 1, 2)

    local = group_local(
        split(query_vector), split(key_vector), split(value), split(log_decay), split(beta)
    )
    step_fn = jax.checkpoint(group_state)

    def advance(carry, items):
        return step_fn(carry, *items)

    final, outs = lax.scan(advance, memory_state, local + (keep,))
    outs = jnp.swapaxes(outs, 1, 2).reshape(count, heads, -1)
    return (final, outs)


def gate_piece(mixed, gate_proj, out_gain):
    count, heads, width = mixed.shape
    gates = jax.nn.silu(gate_proj.reshape(count, heads, width))
    return (rms_scale(mixed, out_gain) * gates).reshape(count, heads * width)


def swish_product(gate_ffn, up_ffn):
    return jax.nn.silu(gate_ffn) * up_ffn


def compose(early, late):
    first_map = jnp.einsum("hij,hjk->hik", late[0], early[0], precision=PRECISE_MODE)
    second_map = jnp.einsum("hij,hjv->hiv", late[0], early[1], precision=PRECISE_MODE) + late[1]
    return (first_map, second_map)


def project(rows, weight):
    return jnp.dot(rows, weight, preferred_element_type=jnp.float32)


def rows_product(left, right):
    return jnp.dot(left, right, preferred_element_type=jnp.float32)


def rows_back(left, weight):
    return jnp.einsum("tc,dc->td", left, weight, preferred_element_type=jnp.float32)


def weight_grad(rows, grads):
    return jnp.einsum("td,tc->dc", rows, grads, preferred_element_type=jnp.float32)


STAGES = {"x": ("seq", 0, 1), "y": ("seq", 1, 2), "l": ("dp", 0, 4), "h": ("dp", 1, 8)}


def trade(value, stage):
    axis, bit, _ = STAGES[stage]
    count = lax.axis_size(axis)
    return lax.ppermute(value, axis, [(place, place ^ (1 << bit)) for place in range(count)])


def relative_order(rows, order):
    own = lax.axis_index("dp") * lax.axis_size("seq") + lax.axis_index("seq")
    width = rows.shape[1] // 16
    parts = []
    for place in range(16):
        mask = sum(STAGES[stage][2] for k, stage in enumerate(order) if place >> (3 - k) & 1)
        parts.append(lax.dynamic_slice_in_dim(rows, (own ^ mask) * width, width, 1))
    return jnp.concatenate(parts, axis=1)


def low(value):
    return value.astype(jnp.bfloat16)


def high(value):
    return value.astype(jnp.float32)


def scattered_grad(rows, grads, order):
    width = rows.shape[1] // 16
    first = trade(low(weight_grad(rows[:, 8 * width :], grads)), order[0])
    second = trade(
        low(weight_grad(rows[:, 4 * width : 8 * width], grads) + high(first[4 * width :])), order[1]
    )
    rest = weight_grad(rows[:, : 4 * width], grads) + high(first[: 4 * width])
    third = trade(low(rest[2 * width :] + high(second[2 * width :])), order[2])
    rest = rest[: 2 * width] + high(second[: 2 * width])
    fourth = trade(low(rest[width:] + high(third[width:])), order[3])
    return rest[:width] + high(third[:width]) + high(fourth)


def sum_all(value):
    for stage in "xylh":
        value = value + trade(value, stage)
    return value


def heads_gather(rows):
    count = lax.axis_size("heads")
    own = lax.axis_index("heads")
    step = 1
    while step < count:
        other = lax.ppermute(rows, "heads", [(place, place ^ step) for place in range(count)])
        size = rows.shape[0]
        upper = lax.rem(own // step, 2)
        both = jnp.zeros((2 * size,) + rows.shape[1:], rows.dtype)
        both = lax.dynamic_update_slice_in_dim(both, rows, upper * size, 0)
        rows = lax.dynamic_update_slice_in_dim(both, other, (1 - upper) * size, 0)
        step *= 2
    return rows


def heads_sum(compute, count, kind):
    if lax.axis_size("heads") != 2:
        whole = compute(lambda rows: rows).astype(kind)
        return high(lax.psum_scatter(whole, "heads", scatter_dimension=0, tiled=True))
    own = lax.axis_index("heads")
    half = count // 2

    def part(which):
        return compute(lambda rows: lax.dynamic_slice_in_dim(rows, which * half, half, 0))

    got = lax.ppermute(part(1 - own).astype(kind), "heads", [(0, 1), (1, 0)])
    return part(own) + high(got)


ORDERS = ("xylh", "ylxh", "lxyh")


def body(
    hidden_in,
    out_cotangent,
    lengths,
    norm_gain,
    q_weight,
    k_weight,
    v_weight,
    gate_weight,
    decay_weight,
    beta_weight,
    conv_q,
    conv_k,
    conv_v,
    decay_log,
    decay_bias,
    out_gain,
    out_weight,
    ffn_gain,
    ffn_gate,
    ffn_up,
    ffn_down,
):
    resid = hidden_in[0].astype(jnp.float32)
    normed_own = rms_scale(resid, norm_gain).astype(jnp.bfloat16)
    normed, cotangent = (
        heads_gather(normed_own),
        heads_gather(out_cotangent[0]),
    )
    span = normed.shape[0]
    taps = conv_q.shape[0]
    halo = taps - 1
    q_proj = project(normed, q_weight)
    k_proj = project(normed, k_weight)
    v_proj = project(normed, v_weight)
    gate_proj = project(normed, gate_weight)
    decay_proj = project(normed, decay_weight)
    beta_proj = project(normed, beta_weight)
    seq_index = lax.axis_index("seq")
    first = lengths[0, 0]
    index = seq_index * span + jnp.arange(span, dtype=jnp.int32)
    place = index - jnp.where(index >= first, first, 0)
    valid = jnp.stack([place >= taps - 1 - tap for tap in range(taps)], axis=1).astype(jnp.float32)
    starts = seq_index * span + jnp.arange(span // GROUP, dtype=jnp.int32) * GROUP
    keep = ((starts != 0) & (starts != first)).astype(jnp.float32)
    rim = shifted((q_proj[span - halo :], k_proj[span - halo :], v_proj[span - halo :]), "seq", 1)
    q_ext = jnp.concatenate([rim[0], q_proj], axis=0)
    k_ext = jnp.concatenate([rim[1], k_proj], axis=0)
    v_ext = jnp.concatenate([rim[2], v_proj], axis=0)

    def features(
        q_in, k_in, v_in, decay_in, beta_in, conv_qin, conv_kin, conv_vin, log_in, bias_in
    ):
        return prepare(
            q_in,
            k_in,
            v_in,
            decay_in,
            beta_in,
            conv_qin,
            conv_kin,
            conv_vin,
            log_in,
            bias_in,
            valid,
        )

    feats, feat_pull = jax.vjp(
        features,
        q_ext,
        k_ext,
        v_ext,
        decay_proj,
        beta_proj,
        conv_q,
        conv_k,
        conv_v,
        decay_log,
        decay_bias,
    )
    query_vector, key_vector, value, log_decay, beta = feats
    heads = log_decay.shape[1]
    width_k = key_vector.shape[2]
    value_width = value.shape[2]
    identity = jnp.broadcast_to(jnp.eye(width_k, dtype=jnp.float32), (heads, width_k, width_k))
    empty = jnp.zeros((heads, width_k, value_width), jnp.float32)
    transfer, _ = run_span(
        identity, query_vector, key_vector, jnp.zeros_like(query_vector), log_decay, beta, keep
    )
    offset, _ = run_span(empty, query_vector, key_vector, value, log_decay, beta, keep)
    earlier = prefix((transfer, offset), "seq", compose, (identity, empty))
    start_state = earlier[1]

    def span_fn(state_in, query_in, key_in, value_in, decay_in, beta_in):
        return run_span(state_in, query_in, key_in, value_in, decay_in, beta_in, keep)

    (end_state, mixed), span_pull = jax.vjp(
        span_fn, start_state, query_vector, key_vector, value, log_decay, beta
    )
    gated, gate_pull = jax.vjp(gate_piece, mixed, gate_proj, out_gain)
    gated_low = gated.astype(jnp.bfloat16)
    mixer = heads_sum(
        lambda pick: rows_product(pick(gated_low), out_weight), span, jnp.float32
    )
    resid_mid = resid + mixer
    ffn_own = rms_scale(resid_mid, ffn_gain).astype(jnp.bfloat16)
    ffn_in = heads_gather(ffn_own)
    gate_ffn = project(ffn_in, ffn_gate)
    up_ffn = project(ffn_in, ffn_up)
    act, act_pull = jax.vjp(swish_product, gate_ffn, up_ffn)
    act_low = act.astype(jnp.bfloat16)
    ffn_out = heads_sum(lambda pick: rows_product(pick(act_low), ffn_down), span, jnp.bfloat16)
    output = (resid_mid + ffn_out).astype(jnp.bfloat16)
    d_act = jnp.einsum("td,fd->tf", cotangent, ffn_down, preferred_element_type=jnp.float32)
    d_gate_ffn, d_up_ffn = act_pull(d_act)
    d_gate_low = d_gate_ffn.astype(jnp.bfloat16)
    d_up_low = d_up_ffn.astype(jnp.bfloat16)
    ffn_rel = {order: relative_order(ffn_in, order) for order in ORDERS[:2]}
    cotangent_rel = relative_order(cotangent, ORDERS[2])
    grad_gate = scattered_grad(ffn_rel[ORDERS[0]], d_gate_low, ORDERS[0])
    grad_up = scattered_grad(ffn_rel[ORDERS[1]], d_up_low, ORDERS[1])
    grad_down = scattered_grad(cotangent_rel, act_low, ORDERS[2]).T
    d_ffn = heads_sum(
        lambda pick: rows_back(pick(d_gate_low), ffn_gate) + rows_back(pick(d_up_low), ffn_up),
        span,
        jnp.float32,
    )
    _, ffn_norm_pull = jax.vjp(rms_scale, resid_mid, ffn_gain)
    d_mid_norm, d_ffn_gain = ffn_norm_pull(d_ffn)
    d_mid = out_cotangent[0].astype(jnp.float32) + d_mid_norm
    d_mid_all = heads_gather(low(d_mid))
    grad_out = scattered_grad(relative_order(d_mid_all, ORDERS[2]), gated_low, ORDERS[2]).T
    d_gated = jnp.einsum("td,cd->tc", d_mid_all, out_weight, preferred_element_type=jnp.float32)
    d_mixed, d_gate_proj, d_out_gain = gate_pull(d_gated)
    local_back = span_pull((jnp.zeros_like(end_state), d_mixed))[0]
    flipped = jnp.swapaxes(transfer, 1, 2)
    later = prefix_2((flipped, local_back), "seq", compose, (identity, empty))
    span_grads = span_pull((later[1], d_mixed))
    ext_grads = feat_pull(span_grads[1:])
    passed = shifted((ext_grads[0][:halo], ext_grads[1][:halo], ext_grads[2][:halo]), "seq", -1)
    d_q_low = ext_grads[0][halo:].at[span - halo :].add(passed[0]).astype(jnp.bfloat16)
    d_k_low = ext_grads[1][halo:].at[span - halo :].add(passed[1]).astype(jnp.bfloat16)
    d_v_low = ext_grads[2][halo:].at[span - halo :].add(passed[2]).astype(jnp.bfloat16)
    d_decay_low = ext_grads[3].astype(jnp.bfloat16)
    d_beta_low = ext_grads[4].astype(jnp.bfloat16)
    d_gate_low_mix = d_gate_proj.astype(jnp.bfloat16)
    normed_rel = {order: relative_order(normed, order) for order in ORDERS}
    grad_gate_mix = jnp.concatenate(
        [
            scattered_grad(normed_rel[ORDERS[0]], d_gate_low_mix[:, : d_gate_low_mix.shape[1] // 2], ORDERS[0]),
            scattered_grad(normed_rel[ORDERS[1]], d_gate_low_mix[:, d_gate_low_mix.shape[1] // 2 :], ORDERS[1]),
        ],
        axis=1,
    )
    mix_low = jnp.concatenate([d_q_low, d_k_low, d_v_low, d_decay_low, d_beta_low], axis=1)
    width_q = d_q_low.shape[1]
    width_v = d_v_low.shape[1]
    cuts = (0, 4 * width_q // 3 // 128 * 128, 8 * width_q // 3 // 128 * 128, mix_low.shape[1])
    grad_mix = jnp.concatenate(
        [
            scattered_grad(normed_rel[order], mix_low[:, cuts[k] : cuts[k + 1]], order)
            for k, order in enumerate(ORDERS)
        ],
        axis=1,
    )
    heads_here = d_decay_low.shape[1]
    ends = (width_q, 2 * width_q, 2 * width_q + width_v, 2 * width_q + width_v + heads_here)
    grad_q, grad_k, grad_v, grad_decay, grad_beta = jnp.split(grad_mix, ends, axis=1)
    pairs = (
        (d_q_low, q_weight),
        (d_k_low, k_weight),
        (d_v_low, v_weight),
        (d_gate_low_mix, gate_weight),
        (d_decay_low, decay_weight),
        (d_beta_low, beta_weight),
    )
    d_normed = heads_sum(
        lambda pick: sum(rows_back(pick(rows), weight) for rows, weight in pairs),
        span,
        jnp.bfloat16,
    )
    _, in_norm_pull = jax.vjp(rms_scale, resid, norm_gain)
    d_in_norm, d_norm_gain = in_norm_pull(d_normed)
    input_grad = d_mid + d_in_norm
    shared = (d_norm_gain, d_ffn_gain, d_out_gain)
    owned = (
        ext_grads[8],
        ext_grads[9],
        ext_grads[5].reshape(-1),
        ext_grads[6].reshape(-1),
        ext_grads[7].reshape(-1),
    )
    flat = sum_all(jnp.concatenate(shared + owned))
    everyone = heads_gather(flat[None])
    marks = np.cumsum([part.size for part in shared + owned])
    pieces = jnp.split(everyone, marks[:-1], axis=1)
    small = [piece.sum(0) for piece in pieces[:3]] + [pieces[3].reshape(-1), pieces[4].reshape(-1)]
    for piece in pieces[5:]:
        small.append(
            jnp.swapaxes(piece.reshape(piece.shape[0], taps, -1), 0, 1).reshape(taps, -1)
        )
    return (
        output[None],
        input_grad[None],
        small[0],
        grad_q,
        grad_k,
        grad_v,
        grad_gate_mix,
        grad_decay,
        grad_beta,
        small[5],
        small[6],
        small[7],
        small[3],
        small[4],
        small[2],
        grad_out,
        small[1],
        grad_gate,
        grad_up,
        grad_down,
    )


def solution(mesh):
    in_specs = (
        P("dp", ("seq", "heads"), None),
        P("dp", ("seq", "heads"), None),
        P("dp", None),
        P(),
        P(None, "heads"),
        P(None, "heads"),
        P(None, "heads"),
        P(None, "heads"),
        P(None, "heads"),
        P(None, "heads"),
        P(None, "heads"),
        P(None, "heads"),
        P(None, "heads"),
        P("heads"),
        P("heads"),
        P(),
        P("heads", None),
        P(),
        P(None, "heads"),
        P(None, "heads"),
        P("heads", None),
    )
    out_specs = (
        P("dp", ("seq", "heads"), None),
        P("dp", ("seq", "heads"), None),
        P(),
        P(("dp", "seq"), "heads"),
        P(("dp", "seq"), "heads"),
        P(("dp", "seq"), "heads"),
        P(("dp", "seq"), "heads"),
        P(("dp", "seq"), "heads"),
        P(("dp", "seq"), "heads"),
        P(),
        P(),
        P(),
        P(),
        P(),
        P(),
        P("heads", ("dp", "seq")),
        P(),
        P(("dp", "seq"), "heads"),
        P(("dp", "seq"), "heads"),
        P("heads", ("dp", "seq")),
    )
    return jax.shard_map(body, mesh=mesh, in_specs=in_specs, out_specs=out_specs, check_vma=False)
```

```python
import functools

import jax
import jax.numpy as jnp
import numpy as np
from jax import lax
from jax.experimental import pallas as pl
from jax.experimental.pallas import tpu as pltpu
from jax.sharding import PartitionSpec as P

HEADS = 16
DK = 128
DV = 256
GROUP = 64
EPS = 1e-06
PAIR = 2 * GROUP
RIM = 8
VMEM_BYTES = 56 * 1024 * 1024


def mm(left, right):
    return lax.dot_general(
        left, right, (((1,), (0,)), ((), ())), preferred_element_type=jnp.float32
    )


def mm_nt(left, right):
    return lax.dot_general(
        left, right, (((1,), (1,)), ((), ())), preferred_element_type=jnp.float32
    )


def mm_tn(left, right):
    return lax.dot_general(
        left, right, (((0,), (0,)), ((), ())), preferred_element_type=jnp.float32
    )


def low(value):
    return value.astype(jnp.bfloat16)


def high(value):
    return value.astype(jnp.float32)


def grid_masks():
    row = lax.broadcasted_iota(jnp.int32, (PAIR, PAIR), 0)
    col = lax.broadcasted_iota(jnp.int32, (PAIR, PAIR), 1)
    same = (row // GROUP) == (col // GROUP)
    return row, col, same & (row >= col), same & (row > col)


def unit_inverse(lower, row, col):
    inverse = jnp.where(row == col, 1.0, 0.0)
    size = 1
    while size < GROUP:
        here = ((row // (2 * size)) == (col // (2 * size))) & ((row // size) > (col // size))
        part = jnp.where(here, lower, 0.0)
        if size == 1:
            inverse = inverse - part
        else:
            inv_low = low(inverse)
            inverse = inverse - mm(inv_low, low(mm(low(part), inv_low)))
        size *= 2
    return inverse


def ranges(base, first, count):
    token = base + lax.broadcasted_iota(jnp.int32, (count, 1), 0)
    return token - jnp.where(token >= first, first, 0)


def conv_sum(ext, width, weight, place, taps):
    count = place.shape[0]
    total = None
    for tap in range(taps):
        rows = ext[RIM - taps + 1 + tap : RIM - taps + 1 + tap + count, :width]
        if tap < taps - 1:
            rows = jnp.where(place >= taps - 1 - tap, rows, 0.0)
        term = rows * weight[tap : tap + 1, :]
        total = term if total is None else total + term
    return total


def silu(value):
    return value * jax.nn.sigmoid(value)


def unit_scale(value):
    return lax.rsqrt(jnp.sum(value * value, axis=-1, keepdims=True) + EPS)


def column(table, head):
    lane = lax.broadcasted_iota(jnp.int32, table.shape, 1)
    return jnp.sum(jnp.where(lane == head, table, 0.0), axis=1, keepdims=True)


def fill_ext(ext, rim, body, width):
    ext[0:RIM, :width] = rim
    ext[RIM : RIM + body.shape[0], :width] = body


def decay_tables(decay_ref, beta_ref, log_ref, bias_ref, cum_ref, rate_ref):
    count = decay_ref.shape[0]
    shifted_in = decay_ref[...] + bias_ref[...]
    soft = jnp.maximum(shifted_in, 0.0) + jnp.log1p(jnp.exp(-jnp.abs(shifted_in)))
    log_decay = -jnp.exp(log_ref[...]) * soft
    _, _, within, _ = grid_masks()
    ones = jnp.where(within, 1.0, 0.0)
    for pair in range(count // PAIR):
        rows = slice(pair * PAIR, (pair + 1) * PAIR)
        cum_ref[rows, :] = lax.dot_general(
            ones,
            log_decay[rows, :],
            (((1,), (0,)), ((), ())),
            precision=lax.Precision.HIGHEST,
            preferred_element_type=jnp.float32,
        )
    rate_ref[...] = jax.nn.sigmoid(beta_ref[...])
    return log_decay, shifted_in


def state_kernel(
    taps,
    per_step,
    spot,
    q_ref,
    k_ref,
    v_ref,
    q_rim,
    k_rim,
    v_rim,
    conv_q,
    conv_k,
    conv_v,
    decay_ref,
    beta_ref,
    log_ref,
    bias_ref,
    mixed_ref,
    reach_ref,
    map_ref,
    add_ref,
    inverse_ref,
    cum_ref,
    rate_ref,
    ext,
    query,
    key,
    value,
    cum,
    rate,
    u_part,
    w_part,
    score,
    tail,
    delta,
    states,
):
    step = pl.program_id(0)
    count = q_ref.shape[0]
    pairs = count // PAIR
    blocks = count // GROUP
    first, base = spot[0], spot[1]

    @pl.when(step == 0)
    def _():
        decay_tables(decay_ref, beta_ref, log_ref, bias_ref, cum_ref, rate_ref)

    place = ranges(base, first, count)
    for j in range(per_step):
        cols = slice(j * DK, (j + 1) * DK)
        wide = slice(j * DV, (j + 1) * DV)
        fill_ext(ext, q_rim[:, cols], q_ref[:, cols], DK)
        c = silu(conv_sum(ext, DK, conv_q[:, cols], place, taps))
        query[j] = c * (unit_scale(c) * DK**-0.5)
        fill_ext(ext, k_rim[:, cols], k_ref[:, cols], DK)
        c = silu(conv_sum(ext, DK, conv_k[:, cols], place, taps))
        key[j] = c * unit_scale(c)
        fill_ext(ext, v_rim[:, wide], v_ref[:, wide], DV)
        value[j] = silu(conv_sum(ext, DV, conv_v[:, wide], place, taps))
        head = step * per_step + j
        cum[j] = jnp.broadcast_to(column(cum_ref[...], head), (count, DK))
        rate[j] = jnp.broadcast_to(column(rate_ref[...], head), (count, DK))

    row, col, within, below = grid_masks()

    def local(pair, carry):
        at = pl.ds(pl.multiple_of(pair * PAIR, PAIR), PAIR)
        for j in range(per_step):
            g = cum[j, at, :]
            b = rate[j, at, :]
            k = key[j, at, :]
            k_low = low(k)
            spread = jnp.where(within, jnp.exp(jnp.where(within, g - g.T, 0.0)), 0.0)
            keys = mm_nt(k_low, k_low)
            inverse = low(unit_inverse(jnp.where(below, b * keys * spread, 0.0), row, col))
            inverse_ref[j, at, :] = inverse
            score[j, at, :] = low(mm_nt(low(query[j, at, :]), k_low) * spread)
            grown = jnp.exp(g)
            v = value[j, at, :]
            u_part[j, at, :] = mm(inverse, low(jnp.concatenate([b, b], axis=1) * v))
            w_part[j, at, :] = low(mm(inverse, low(b * grown * k)))
            ends = jnp.concatenate(
                [
                    jnp.broadcast_to(g[GROUP - 1 : GROUP], (GROUP, DK)),
                    jnp.broadcast_to(g[PAIR - 1 : PAIR], (GROUP, DK)),
                ],
                axis=0,
            )
            tail[j, at, :] = low(jnp.exp(ends - g) * k)
            query[j, at, :] = grown * query[j, at, :]
        return carry

    lax.fori_loop(0, pairs, local, 0, unroll=2)

    for j in range(per_step):
        states[j] = jnp.concatenate(
            [jnp.where(row == col, 1.0, 0.0), jnp.zeros((DK, DV), jnp.float32)], axis=1
        )

    def advance(block, carry):
        at = pl.ds(pl.multiple_of(block * GROUP, GROUP), GROUP)
        start = base + block * GROUP
        keep = jnp.where((start != 0) & (start != first), 1.0, 0.0)
        for j in range(per_step):
            state = states[j] * keep
            state_low = low(state)
            moved = mm(w_part[j, at, :], state_low)
            change = jnp.concatenate([-moved[:, :DK], u_part[j, at, :] - moved[:, DK:]], axis=1)
            change_low = low(change)
            delta[j, at, :] = change_low
            last = jnp.exp(cum[j, pl.ds(block * GROUP + GROUP - 1, 1), :])
            last = jnp.concatenate([last] * 3, axis=1)
            states[j] = last * state + mm_tn(tail[j, at, :], change_low)
            out = mm(low(query[j, at, :]), state_low)
            reach_ref[at, j * DK : (j + 1) * DK] = low(out[:, :DK])
            mixed_ref[at, j * DV : (j + 1) * DV] = out[:, DK:]
        return carry

    lax.fori_loop(0, blocks, advance, 0)

    def finish(pair, carry):
        at = pl.ds(pl.multiple_of(pair * PAIR, PAIR), PAIR)
        for j in range(per_step):
            out = mm(score[j, at, :], delta[j, at, :])
            cols = slice(j * DK, (j + 1) * DK)
            wide = slice(j * DV, (j + 1) * DV)
            reach_ref[at, cols] = low(high(reach_ref[at, cols]) + out[:, :DK])
            mixed_ref[at, wide] = mixed_ref[at, wide] + out[:, DK:]
        return carry

    lax.fori_loop(0, pairs, finish, 0, unroll=2)
    for j in range(per_step):
        map_ref[j] = low(states[j, :, :DK])
        add_ref[j] = low(states[j, :, DK:])


def spec(shape, index):
    return pl.BlockSpec(shape, index)


def state_forward(q, k, v, rims, convs, decay, beta, decay_log, decay_bias, spot, per_step):
    count = q.shape[0]
    heads = decay.shape[1]
    taps = convs[0].shape[0]
    n = per_step
    along = lambda i: (0, i)
    fixed = lambda i: (0, 0)
    lead = lambda i: (i, 0, 0)
    f32, bf16 = jnp.float32, jnp.bfloat16
    return pl.pallas_call(
        functools.partial(state_kernel, taps, n),
        grid=(heads // n,),
        in_specs=[
            pl.BlockSpec(memory_space=pltpu.SMEM),
            spec((count, n * DK), along),
            spec((count, n * DK), along),
            spec((count, n * DV), along),
            spec((RIM, n * DK), along),
            spec((RIM, n * DK), along),
            spec((RIM, n * DV), along),
            spec((taps, n * DK), along),
            spec((taps, n * DK), along),
            spec((taps, n * DV), along),
            spec((count, heads), fixed),
            spec((count, heads), fixed),
            spec((1, heads), fixed),
            spec((1, heads), fixed),
        ],
        out_specs=[
            spec((count, n * DV), along),
            spec((count, n * DK), along),
            spec((n, DK, DK), lead),
            spec((n, DK, DV), lead),
            spec((n, count, PAIR), lead),
            spec((count, heads), fixed),
            spec((count, heads), fixed),
        ],
        out_shape=[
            jax.ShapeDtypeStruct((count, heads * DV), f32),
            jax.ShapeDtypeStruct((count, heads * DK), bf16),
            jax.ShapeDtypeStruct((heads, DK, DK), bf16),
            jax.ShapeDtypeStruct((heads, DK, DV), bf16),
            jax.ShapeDtypeStruct((heads, count, PAIR), bf16),
            jax.ShapeDtypeStruct((count, heads), f32),
            jax.ShapeDtypeStruct((count, heads), f32),
        ],
        scratch_shapes=[
            pltpu.VMEM((count + RIM, DV), f32),
            pltpu.VMEM((n, count, DK), f32),
            pltpu.VMEM((n, count, DK), f32),
            pltpu.VMEM((n, count, DV), f32),
            pltpu.VMEM((n, count, DK), f32),
            pltpu.VMEM((n, count, DK), f32),
            pltpu.VMEM((n, count, DV), f32),
            pltpu.VMEM((n, count, DK), bf16),
            pltpu.VMEM((n, count, PAIR), bf16),
            pltpu.VMEM((n, count, DK), bf16),
            pltpu.VMEM((n, count, DK + DV), bf16),
            pltpu.VMEM((n, DK, DK + DV), f32),
        ],
        compiler_params=pltpu.CompilerParams(
            dimension_semantics=("arbitrary",), vmem_limit_bytes=VMEM_BYTES
        ),
        cost_estimate=pl.CostEstimate(
            flops=heads * count * 2 * 128 * 2600, bytes_accessed=count * heads * 4000, transcendentals=0
        ),
    )(spot, q, k, v, *rims, *convs, decay, beta, decay_log, decay_bias)


def gate_kernel(per_step, mixed_ref, reach_ref, map_ref, add_ref, far_ref, gate_ref, gain_ref, gated_ref, kept_ref, start_ref):
    for j in range(per_step):
        cols = slice(j * DK, (j + 1) * DK)
        wide = slice(j * DV, (j + 1) * DV)
        start = low(high(add_ref[j]) + mm(map_ref[j], far_ref[j]))
        start_ref[j] = start
        mixed = mixed_ref[:, wide] + mm(reach_ref[:, cols], start)
        kept_ref[:, wide] = low(mixed)
        scale = lax.rsqrt(jnp.mean(mixed * mixed, axis=-1, keepdims=True) + EPS)
        gated_ref[:, wide] = low(mixed * scale * gain_ref[...] * silu(gate_ref[:, wide]))


def gate_forward(mixed, reach, near_map, near_add, far_add, gate, gain, per_step):
    count = mixed.shape[0]
    heads = near_map.shape[0]
    n = per_step
    along = lambda i: (0, i)
    lead = lambda i: (i, 0, 0)
    bf16 = jnp.bfloat16
    return pl.pallas_call(
        functools.partial(gate_kernel, n),
        grid=(heads // n,),
        in_specs=[
            spec((count, n * DV), along),
            spec((count, n * DK), along),
            spec((n, DK, DK), lead),
            spec((n, DK, DV), lead),
            spec((n, DK, DV), lead),
            spec((count, n * DV), along),
            spec((1, DV), lambda i: (0, 0)),
        ],
        out_specs=[
            spec((count, n * DV), along),
            spec((count, n * DV), along),
            spec((n, DK, DV), lead),
        ],
        out_shape=[
            jax.ShapeDtypeStruct((count, heads * DV), bf16),
            jax.ShapeDtypeStruct((count, heads * DV), bf16),
            jax.ShapeDtypeStruct((heads, DK, DV), bf16),
        ],
        compiler_params=pltpu.CompilerParams(
            dimension_semantics=("arbitrary",), vmem_limit_bytes=VMEM_BYTES
        ),
    )(mixed, reach, near_map, near_add, far_add, gate, gain)


def gate_back_kernel(per_step, d_gated_ref, kept_ref, reach_ref, gate_ref, gain_ref, d_mixed_ref, d_gate_ref, d_start_ref, d_gain_ref):
    @pl.when(pl.program_id(0) == 0)
    def _():
        d_gain_ref[...] = jnp.zeros_like(d_gain_ref)

    for j in range(per_step):
        cols = slice(j * DK, (j + 1) * DK)
        wide = slice(j * DV, (j + 1) * DV)
        mixed = high(kept_ref[:, wide])
        scale = lax.rsqrt(jnp.mean(mixed * mixed, axis=-1, keepdims=True) + EPS)
        normal = mixed * scale
        gate = gate_ref[:, wide]
        sig = jax.nn.sigmoid(gate)
        d_gated = d_gated_ref[:, wide]
        d_scaled = d_gated * (gate * sig)
        d_gain_ref[...] += jnp.sum(d_scaled * normal, axis=0, keepdims=True)
        d_gate_ref[:, wide] = low(
            d_gated * (normal * gain_ref[...]) * (sig * (1.0 + gate * (1.0 - sig)))
        )
        d_normal = d_scaled * gain_ref[...]
        d_mixed = low(scale * (d_normal - normal * jnp.mean(d_normal * normal, axis=-1, keepdims=True)))
        d_mixed_ref[:, wide] = d_mixed
        d_start_ref[j] = low(mm_tn(reach_ref[:, cols], d_mixed))


def gate_backward(d_gated, kept, reach, gate, gain, per_step):
    count = kept.shape[0]
    heads = kept.shape[1] // DV
    n = per_step
    along = lambda i: (0, i)
    lead = lambda i: (i, 0, 0)
    bf16 = jnp.bfloat16
    return pl.pallas_call(
        functools.partial(gate_back_kernel, n),
        grid=(heads // n,),
        in_specs=[
            spec((count, n * DV), along),
            spec((count, n * DV), along),
            spec((count, n * DK), along),
            spec((count, n * DV), along),
            spec((1, DV), lambda i: (0, 0)),
        ],
        out_specs=[
            spec((count, n * DV), along),
            spec((count, n * DV), along),
            spec((n, DK, DV), lead),
            spec((1, DV), lambda i: (0, 0)),
        ],
        out_shape=[
            jax.ShapeDtypeStruct((count, heads * DV), bf16),
            jax.ShapeDtypeStruct((count, heads * DV), bf16),
            jax.ShapeDtypeStruct((heads, DK, DV), bf16),
            jax.ShapeDtypeStruct((1, DV), jnp.float32),
        ],
        compiler_params=pltpu.CompilerParams(
            dimension_semantics=("arbitrary",), vmem_limit_bytes=VMEM_BYTES
        ),
    )(d_gated, kept, reach, gate, gain)


def state_back_kernel(
    taps,
    per_step,
    spot,
    q_ref,
    k_ref,
    v_ref,
    q_rim,
    k_rim,
    v_rim,
    conv_q,
    conv_k,
    conv_v,
    decay_ref,
    log_ref,
    bias_ref,
    cum_ref,
    rate_ref,
    inverse_ref,
    start_ref,
    d_mixed_ref,
    near_ref,
    map_ref,
    far_ref,
    dq_ref,
    dk_ref,
    dv_ref,
    dq_rim,
    dk_rim,
    dv_rim,
    dq_end,
    dk_end,
    dv_end,
    d_conv_q,
    d_conv_k,
    d_conv_v,
    d_decay_ref,
    d_beta_ref,
    d_log_ref,
    d_bias_ref,
    ext,
    d_ext,
    query,
    key,
    value,
    cum,
    rate,
    u_part,
    w_part,
    score,
    tail,
    grown_q,
    grown_k,
    pull,
    local_r,
    delta,
    starts,
    ends,
    states,
    d_rhs,
    d_cum,
    d_rate,
):
    step = pl.program_id(0)
    count = q_ref.shape[0]
    pairs = count // PAIR
    blocks = count // GROUP
    first, base = spot[0], spot[1]
    place = ranges(base, first, count)

    @pl.when(step == 0)
    def _():
        d_cum[...] = jnp.zeros_like(d_cum)
        d_rate[...] = jnp.zeros_like(d_rate)

    for j in range(per_step):
        cols = slice(j * DK, (j + 1) * DK)
        wide = slice(j * DV, (j + 1) * DV)
        fill_ext(ext, q_rim[:, cols], q_ref[:, cols], DK)
        c = silu(conv_sum(ext, DK, conv_q[:, cols], place, taps))
        query[j] = c * (unit_scale(c) * DK**-0.5)
        fill_ext(ext, k_rim[:, cols], k_ref[:, cols], DK)
        c = silu(conv_sum(ext, DK, conv_k[:, cols], place, taps))
        key[j] = c * unit_scale(c)
        fill_ext(ext, v_rim[:, wide], v_ref[:, wide], DV)
        value[j] = silu(conv_sum(ext, DV, conv_v[:, wide], place, taps))
        head = step * per_step + j
        cum[j] = jnp.broadcast_to(column(cum_ref[...], head), (count, DK))
        rate[j] = jnp.broadcast_to(column(rate_ref[...], head), (count, DK))

    row, col, within, below = grid_masks()

    def block_ends(g):
        return jnp.concatenate(
            [
                jnp.broadcast_to(g[GROUP - 1 : GROUP], (GROUP, DK)),
                jnp.broadcast_to(g[PAIR - 1 : PAIR], (GROUP, DK)),
            ],
            axis=0,
        )

    def local(pair, carry):
        at = pl.ds(pl.multiple_of(pair * PAIR, PAIR), PAIR)
        for j in range(per_step):
            g = cum[j, at, :]
            b = rate[j, at, :]
            k = key[j, at, :]
            q = query[j, at, :]
            spread = jnp.where(within, jnp.exp(jnp.where(within, g - g.T, 0.0)), 0.0)
            inverse = inverse_ref[j, at, :]
            scored = low(mm_nt(low(q), low(k)) * spread)
            grown = jnp.exp(g)
            v = value[j, at, :]
            kb = low(b * grown * k)
            grown_k[j, at, :] = kb
            u_part[j, at, :] = mm(inverse, low(jnp.concatenate([b, b], axis=1) * v))
            w_part[j, at, :] = low(mm(inverse, kb))
            t = low(jnp.exp(block_ends(g) - g) * k)
            tail[j, at, :] = t
            grown_q[j, at, :] = low(grown * q)
            pull[j, at, :] = low(mm_tn(inverse, t))
            d_out = d_mixed_ref[at, j * DV : (j + 1) * DV]
            local_r[j, at, :] = mm_tn(inverse, low(mm_tn(scored, d_out)))
        return carry

    lax.fori_loop(0, pairs, local, 0, unroll=2)

    for j in range(per_step):
        states[j] = high(start_ref[j])

    def advance(block, carry):
        at = pl.ds(pl.multiple_of(block * GROUP, GROUP), GROUP)
        begin = base + block * GROUP
        keep = jnp.where((begin != 0) & (begin != first), 1.0, 0.0)
        for j in range(per_step):
            state = states[j] * keep
            state_low = low(state)
            starts[j, block] = state_low
            change_low = low(u_part[j, at, :] - mm(w_part[j, at, :], state_low))
            delta[j, at, :] = change_low
            last = jnp.exp(cum[j, pl.ds(block * GROUP + GROUP - 1, 1), :])
            last = jnp.concatenate([last, last], axis=1)
            states[j] = last * state + mm_tn(tail[j, at, :], change_low)
        return carry

    lax.fori_loop(0, blocks, advance, 0)

    for j in range(per_step):
        states[j] = high(near_ref[j]) + mm_tn(map_ref[j], far_ref[j])

    def retreat(reverse, carry):
        block = blocks - 1 - reverse
        at = pl.ds(pl.multiple_of(block * GROUP, GROUP), GROUP)
        begin = base + block * GROUP
        keep = jnp.where((begin != 0) & (begin != first), 1.0, 0.0)
        for j in range(per_step):
            d_state = states[j]
            d_low = low(d_state)
            ends[j, block] = d_low
            change = low(local_r[j, at, :] + mm(pull[j, at, :], d_low))
            d_rhs[j, at, :] = change
            last = jnp.exp(cum[j, pl.ds(block * GROUP + GROUP - 1, 1), :])
            last = jnp.concatenate([last, last], axis=1)
            d_out = d_mixed_ref[at, j * DV : (j + 1) * DV]
            states[j] = keep * (
                last * d_state
                + mm_tn(grown_q[j, at, :], d_out)
                - mm_tn(grown_k[j, at, :], change)
            )
        return carry

    lax.fori_loop(0, blocks, retreat, 0)

    lane = lax.broadcasted_iota(jnp.int32, (PAIR, d_cum.shape[1]), 1)
    tall = lax.broadcasted_iota(jnp.int32, (PAIR, 1), 0)

    def assemble(pair, carry):
        at = pl.ds(pl.multiple_of(pair * PAIR, PAIR), PAIR)
        for j in range(per_step):
            g = cum[j, at, :]
            b = rate[j, at, :]
            k = key[j, at, :]
            q = query[j, at, :]
            v = value[j, at, :]
            k_low, q_low = low(k), low(q)
            spread = jnp.where(within, jnp.exp(jnp.where(within, g - g.T, 0.0)), 0.0)
            d_out = d_mixed_ref[at, j * DV : (j + 1) * DV]
            change = delta[j, at, :]
            rhs = d_rhs[j, at, :]
            d_lower = jnp.where(below, -mm_nt(rhs, change), 0.0)
            d_score = mm_nt(d_out, change) * spread
            d_gk, d_gq, d_tail = [], [], []
            bonus = []
            for half in range(2):
                block = 2 * pair + half
                part = slice(half * GROUP, (half + 1) * GROUP)
                state, d_end = starts[j, block], ends[j, block]
                d_gk.append(-mm_nt(rhs[part], state))
                d_gq.append(mm_nt(d_out[part], state))
                d_tail.append(mm_nt(change[part], d_end))
                bonus.append(jnp.sum(high(state) * high(d_end)))
            d_gk = jnp.concatenate(d_gk, axis=0)
            d_gq = jnp.concatenate(d_gq, axis=0)
            d_tail = jnp.concatenate(d_tail, axis=0)
            grown = jnp.exp(g)
            fall = jnp.exp(block_ends(g) - g)
            shape = mm_nt(k_low, k_low) * spread
            d_a = d_lower * shape
            cross = d_a * b + d_score * mm_nt(q_low, k_low)
            gk_k = d_gk * k
            rate_col = jnp.sum(d_a + grown * gk_k, axis=-1, keepdims=True) + jnp.sum(
                high(rhs) * v, axis=-1, keepdims=True
            )
            tail_sum = jnp.sum(d_tail * (fall * k), axis=-1, keepdims=True)
            cum_col = (
                jnp.sum(
                    cross - cross.T + b * grown * gk_k + d_gq * (grown * q), axis=-1, keepdims=True
                )
                - tail_sum
            )
            for half in range(2):
                part = slice(half * GROUP, (half + 1) * GROUP)
                at_end = half * GROUP + GROUP - 1
                extra = jnp.sum(tail_sum[part], axis=0, keepdims=True) + bonus[half] * grown[
                    at_end : at_end + 1, :1
                ]
                cum_col = cum_col + jnp.where(tall == at_end, extra, 0.0)
            head = step * per_step + j
            d_cum[at, :] = d_cum[at, :] + jnp.where(lane == head, cum_col, 0.0)
            d_rate[at, :] = d_rate[at, :] + jnp.where(lane == head, rate_col, 0.0)
            d_keys = d_lower * spread * b
            d_keys = low(d_keys + d_keys.T)
            d_score_low = low(d_score)
            d_query = grown * d_gq + mm(d_score_low, k_low)
            d_key = b * grown * d_gk + fall * d_tail + mm(d_keys, k_low) + mm_tn(d_score_low, q_low)
            query[j, at, :] = d_query
            key[j, at, :] = d_key
            value[j, at, :] = jnp.concatenate([b, b], axis=1) * high(rhs)
        return carry

    lax.fori_loop(0, pairs, assemble, 0)

    def conv_back(width, weight, d_total, out_ref, rim_ref, end_ref, d_weight_ref, cols):
        d_ext[:, :width] = jnp.zeros((count + 2 * RIM, width), jnp.float32)
        grads = []
        for tap in range(taps):
            offset = RIM - taps + 1 + tap
            part = d_total
            if tap < taps - 1:
                part = jnp.where(place >= taps - 1 - tap, part, 0.0)
            grads.append(
                jnp.sum(part * ext[offset : offset + count, :width], axis=0, keepdims=True)
            )
            d_ext[offset : offset + count, :width] += part * weight[tap : tap + 1, :]
        d_weight_ref[:, cols] = jnp.concatenate(grads, axis=0)
        rim_ref[:, cols] = d_ext[0:RIM, :width]
        out_ref[:, cols] = low(d_ext[RIM : RIM + count, :width])
        end_ref[:, cols] = d_ext[count : count + RIM, :width]

    for j in range(per_step):
        cols = slice(j * DK, (j + 1) * DK)
        wide = slice(j * DV, (j + 1) * DV)

        def unit_back(rim, body, weight, d_unit, factor):
            fill_ext(ext, rim, body, DK)
            total = conv_sum(ext, DK, weight, place, taps)
            sig = jax.nn.sigmoid(total)
            c = total * sig
            scale = unit_scale(c)
            unit = c * scale
            d_unit = d_unit * factor
            d_c = scale * (d_unit - unit * jnp.sum(d_unit * unit, axis=-1, keepdims=True))
            return d_c * (sig * (1.0 + total * (1.0 - sig)))

        d_total = unit_back(q_rim[:, cols], q_ref[:, cols], conv_q[:, cols], query[j], DK**-0.5)
        conv_back(DK, conv_q[:, cols], d_total, dq_ref, dq_rim, dq_end, d_conv_q, cols)
        d_total = unit_back(k_rim[:, cols], k_ref[:, cols], conv_k[:, cols], key[j], 1.0)
        conv_back(DK, conv_k[:, cols], d_total, dk_ref, dk_rim, dk_end, d_conv_k, cols)
        fill_ext(ext, v_rim[:, wide], v_ref[:, wide], DV)
        total = conv_sum(ext, DV, conv_v[:, wide], place, taps)
        sig = jax.nn.sigmoid(total)
        d_total = value[j] * (sig * (1.0 + total * (1.0 - sig)))
        conv_back(DV, conv_v[:, wide], d_total, dv_ref, dv_rim, dv_end, d_conv_v, wide)

    @pl.when(step == pl.num_programs(0) - 1)
    def _():
        shifted_in = decay_ref[...] + bias_ref[...]
        soft = jnp.maximum(shifted_in, 0.0) + jnp.log1p(jnp.exp(-jnp.abs(shifted_in)))
        speed = -jnp.exp(log_ref[...])
        after = jnp.where(within, 1.0, 0.0)
        d_log = jnp.zeros_like(d_log_ref)
        d_bias = jnp.zeros_like(d_bias_ref)
        for pair in range(pairs):
            rows = slice(pair * PAIR, (pair + 1) * PAIR)
            d_decay = lax.dot_general(
                after,
                d_cum[rows, :],
                (((0,), (0,)), ((), ())),
                precision=lax.Precision.HIGHEST,
                preferred_element_type=jnp.float32,
            )
            d_log = d_log + jnp.sum(d_decay * (speed * soft[rows]), axis=0, keepdims=True)
            d_in = d_decay * speed * jax.nn.sigmoid(shifted_in[rows])
            d_bias = d_bias + jnp.sum(d_in, axis=0, keepdims=True)
            d_decay_ref[rows, :] = d_in
        d_log_ref[...] = d_log
        d_bias_ref[...] = d_bias
        rates = rate_ref[...]
        d_beta_ref[...] = d_rate[...] * rates * (1.0 - rates)


def state_backward(
    q, k, v, rims, convs, decay, decay_log, decay_bias, cum, rate, inverse, start, d_mixed, near, near_map, far, spot, per_step
):
    count = q.shape[0]
    heads = decay.shape[1]
    taps = convs[0].shape[0]
    n = per_step
    along = lambda i: (0, i)
    fixed = lambda i: (0, 0)
    lead = lambda i: (i, 0, 0)
    f32, bf16 = jnp.float32, jnp.bfloat16
    shape = jax.ShapeDtypeStruct
    vm = pltpu.VMEM
    return pl.pallas_call(
        functools.partial(state_back_kernel, taps, n),
        grid=(heads // n,),
        in_specs=[
            pl.BlockSpec(memory_space=pltpu.SMEM),
            spec((count, n * DK), along),
            spec((count, n * DK), along),
            spec((count, n * DV), along),
            spec((RIM, n * DK), along),
            spec((RIM, n * DK), along),
            spec((RIM, n * DV), along),
            spec((taps, n * DK), along),
            spec((taps, n * DK), along),
            spec((taps, n * DV), along),
            spec((count, heads), fixed),
            spec((1, heads), fixed),
            spec((1, heads), fixed),
            spec((count, heads), fixed),
            spec((count, heads), fixed),
            spec((n, count, PAIR), lead),
            spec((n, DK, DV), lead),
            spec((count, n * DV), along),
            spec((n, DK, DV), lead),
            spec((n, DK, DK), lead),
            spec((n, DK, DV), lead),
        ],
        out_specs=[
            spec((count, n * DK), along),
            spec((count, n * DK), along),
            spec((count, n * DV), along),
            spec((RIM, n * DK), along),
            spec((RIM, n * DK), along),
            spec((RIM, n * DV), along),
            spec((RIM, n * DK), along),
            spec((RIM, n * DK), along),
            spec((RIM, n * DV), along),
            spec((taps, n * DK), along),
            spec((taps, n * DK), along),
            spec((taps, n * DV), along),
            spec((count, heads), fixed),
            spec((count, heads), fixed),
            spec((1, heads), fixed),
            spec((1, heads), fixed),
        ],
        out_shape=[
            shape((count, heads * DK), bf16),
            shape((count, heads * DK), bf16),
            shape((count, heads * DV), bf16),
            shape((RIM, heads * DK), f32),
            shape((RIM, heads * DK), f32),
            shape((RIM, heads * DV), f32),
            shape((RIM, heads * DK), f32),
            shape((RIM, heads * DK), f32),
            shape((RIM, heads * DV), f32),
            shape((taps, heads * DK), f32),
            shape((taps, heads * DK), f32),
            shape((taps, heads * DV), f32),
            shape((count, heads), f32),
            shape((count, heads), f32),
            shape((1, heads), f32),
            shape((1, heads), f32),
        ],
        scratch_shapes=[
            vm((count + RIM, DV), f32),
            vm((count + 2 * RIM, DV), f32),
            vm((n, count, DK), f32),
            vm((n, count, DK), f32),
            vm((n, count, DV), f32),
            vm((n, count, DK), f32),
            vm((n, count, DK), f32),
            vm((n, count, DV), f32),
            vm((n, count, DK), bf16),
            vm((n, 16, PAIR), bf16),
            vm((n, count, DK), bf16),
            vm((n, count, DK), bf16),
            vm((n, count, DK), bf16),
            vm((n, count, DK), bf16),
            vm((n, count, DV), f32),
            vm((n, count, DV), bf16),
            vm((n, count // GROUP, DK, DV), bf16),
            vm((n, count // GROUP, DK, DV), bf16),
            vm((n, DK, DV), f32),
            vm((n, count, DV), bf16),
            vm((count, heads), f32),
            vm((count, heads), f32),
        ],
        compiler_params=pltpu.CompilerParams(
            dimension_semantics=("arbitrary",), vmem_limit_bytes=VMEM_BYTES
        ),
        cost_estimate=pl.CostEstimate(
            flops=heads * count * 2 * 128 * 5000, bytes_accessed=count * heads * 6000, transcendentals=0
        ),
    )(spot, q, k, v, *rims, *convs, decay, decay_log, decay_bias, cum, rate, inverse, start, d_mixed, near, near_map, far)


def shifted(value, axis, steps):
    count = lax.axis_size(axis)
    leading, last = (max(0, -steps), min(count, count - steps))
    return lax.ppermute(value, axis, [(source, source + steps) for source in range(leading, last)])


def rms_scale(values, gain):
    return values * lax.rsqrt(jnp.mean(values * values, axis=-1, keepdims=True) + EPS) * gain


def swish_product(gate_ffn, up_ffn):
    return jax.nn.silu(gate_ffn) * up_ffn


def project(rows, weight):
    return jnp.dot(rows, weight, preferred_element_type=jnp.float32)


def rows_product(left, right):
    return jnp.dot(left, right, preferred_element_type=jnp.float32)


def rows_back(left, weight):
    return jnp.einsum("tc,dc->td", left, weight, preferred_element_type=jnp.float32)


def weight_grad(rows, grads):
    return jnp.einsum("td,tc->dc", rows, grads, preferred_element_type=jnp.float32)


STAGES = {"x": ("seq", 0, 1), "y": ("seq", 1, 2), "l": ("dp", 0, 4), "h": ("dp", 1, 8)}


def trade(value, stage):
    axis, bit, _ = STAGES[stage]
    count = lax.axis_size(axis)
    return lax.ppermute(value, axis, [(place, place ^ (1 << bit)) for place in range(count)])


def relative_order(rows, order):
    own = lax.axis_index("dp") * lax.axis_size("seq") + lax.axis_index("seq")
    width = rows.shape[1] // 16
    parts = []
    for place in range(16):
        mask = sum(STAGES[stage][2] for k, stage in enumerate(order) if place >> (3 - k) & 1)
        parts.append(lax.dynamic_slice_in_dim(rows, (own ^ mask) * width, width, 1))
    return jnp.concatenate(parts, axis=1)


def scattered_grad(rows, grads, order):
    width = rows.shape[1] // 16
    first = trade(low(weight_grad(rows[:, 8 * width :], grads)), order[0])
    second = trade(
        low(weight_grad(rows[:, 4 * width : 8 * width], grads) + high(first[4 * width :])), order[1]
    )
    rest = weight_grad(rows[:, : 4 * width], grads) + high(first[: 4 * width])
    third = trade(low(rest[2 * width :] + high(second[2 * width :])), order[2])
    rest = rest[: 2 * width] + high(second[: 2 * width])
    fourth = trade(low(rest[width:] + high(third[width:])), order[3])
    return rest[:width] + high(third[:width]) + high(fourth)


def sum_all(value):
    for stage in "xylh":
        value = value + trade(value, stage)
    return value


def heads_gather(rows):
    count = lax.axis_size("heads")
    own = lax.axis_index("heads")
    step = 1
    while step < count:
        other = lax.ppermute(rows, "heads", [(place, place ^ step) for place in range(count)])
        size = rows.shape[0]
        upper = lax.rem(own // step, 2)
        both = jnp.zeros((2 * size,) + rows.shape[1:], rows.dtype)
        both = lax.dynamic_update_slice_in_dim(both, rows, upper * size, 0)
        rows = lax.dynamic_update_slice_in_dim(both, other, (1 - upper) * size, 0)
        step *= 2
    return rows


def heads_sum(compute, count, kind):
    if lax.axis_size("heads") != 2:
        whole = compute(lambda rows: rows).astype(kind)
        return high(lax.psum_scatter(whole, "heads", scatter_dimension=0, tiled=True))
    own = lax.axis_index("heads")
    half = count // 2

    def part(which):
        return compute(lambda rows: lax.dynamic_slice_in_dim(rows, which * half, half, 0))

    got = lax.ppermute(part(1 - own).astype(kind), "heads", [(0, 1), (1, 0)])
    return part(own) + high(got)


ORDERS = ("xylh", "ylxh", "lxyh")


def body(
    hidden_in,
    out_cotangent,
    lengths,
    norm_gain,
    q_weight,
    k_weight,
    v_weight,
    gate_weight,
    decay_weight,
    beta_weight,
    conv_q,
    conv_k,
    conv_v,
    decay_log,
    decay_bias,
    out_gain,
    out_weight,
    ffn_gain,
    ffn_gate,
    ffn_up,
    ffn_down,
):
    resid = hidden_in[0].astype(jnp.float32)
    normed_own = rms_scale(resid, norm_gain).astype(jnp.bfloat16)
    normed, cotangent = (
        heads_gather(normed_own),
        heads_gather(out_cotangent[0]),
    )
    span = normed.shape[0]
    taps = conv_q.shape[0]
    q_proj = project(normed, q_weight)
    k_proj = project(normed, k_weight)
    v_proj = project(normed, v_weight)
    gate_proj = project(normed, gate_weight)
    heads = decay_weight.shape[1]
    per_step = min(2, heads)
    narrow = project(normed, jnp.concatenate([decay_weight, beta_weight], axis=1))
    decay_proj, beta_proj = narrow[:, :heads], narrow[:, heads:]
    seq_index = lax.axis_index("seq")
    spot = jnp.stack([lengths[0, 0], seq_index * span]).astype(jnp.int32)
    rims = shifted((q_proj[span - RIM :], k_proj[span - RIM :], v_proj[span - RIM :]), "seq", 1)
    convs = (conv_q, conv_k, conv_v)
    log_row, bias_row, gain_row = decay_log[None], decay_bias[None], out_gain[None]
    mixed_local, reach, span_map, span_add, inverse, cum, rate = state_forward(
        q_proj, k_proj, v_proj, rims, convs, decay_proj, beta_proj, log_row, bias_row, spot, per_step
    )
    near_map, near_add = shifted((span_map, span_add), "seq", 1)
    far_add = shifted(span_add, "seq", 2)
    next_map = shifted(span_map, "seq", -1)
    gated_low, mixed_low, start_state = gate_forward(
        mixed_local, reach, near_map, near_add, far_add, gate_proj, gain_row, per_step
    )
    mixer = heads_sum(
        lambda pick: rows_product(pick(gated_low), out_weight), span, jnp.float32
    )
    resid_mid = resid + mixer
    ffn_own = rms_scale(resid_mid, ffn_gain).astype(jnp.bfloat16)
    ffn_in = heads_gather(ffn_own)
    gate_ffn = project(ffn_in, ffn_gate)
    up_ffn = project(ffn_in, ffn_up)
    act, act_pull = jax.vjp(swish_product, gate_ffn, up_ffn)
    act_low = act.astype(jnp.bfloat16)
    ffn_out = heads_sum(lambda pick: rows_product(pick(act_low), ffn_down), span, jnp.bfloat16)
    output = (resid_mid + ffn_out).astype(jnp.bfloat16)
    d_act = jnp.einsum("td,fd->tf", cotangent, ffn_down, preferred_element_type=jnp.float32)
    d_gate_ffn, d_up_ffn = act_pull(d_act)
    d_gate_low = d_gate_ffn.astype(jnp.bfloat16)
    d_up_low = d_up_ffn.astype(jnp.bfloat16)
    ffn_rel = {order: relative_order(ffn_in, order) for order in ORDERS[:2]}
    cotangent_rel = relative_order(cotangent, ORDERS[2])
    grad_gate = scattered_grad(ffn_rel[ORDERS[0]], d_gate_low, ORDERS[0])
    grad_up = scattered_grad(ffn_rel[ORDERS[1]], d_up_low, ORDERS[1])
    grad_down = scattered_grad(cotangent_rel, act_low, ORDERS[2]).T
    d_ffn = heads_sum(
        lambda pick: rows_back(pick(d_gate_low), ffn_gate) + rows_back(pick(d_up_low), ffn_up),
        span,
        jnp.float32,
    )
    _, ffn_norm_pull = jax.vjp(rms_scale, resid_mid, ffn_gain)
    d_mid_norm, d_ffn_gain = ffn_norm_pull(d_ffn)
    d_mid = out_cotangent[0].astype(jnp.float32) + d_mid_norm
    d_mid_all = heads_gather(low(d_mid))
    grad_out = scattered_grad(relative_order(d_mid_all, ORDERS[2]), gated_low, ORDERS[2]).T
    d_gated = jnp.einsum("td,cd->tc", d_mid_all, out_weight, preferred_element_type=jnp.float32)
    d_mixed, d_gate_low_mix, d_start, d_out_gain = gate_backward(
        d_gated, mixed_low, reach, gate_proj, gain_row, per_step
    )
    next_start = shifted(d_start, "seq", -1)
    beyond_start = shifted(d_start, "seq", -2)
    back = state_backward(
        q_proj,
        k_proj,
        v_proj,
        rims,
        convs,
        decay_proj,
        log_row,
        bias_row,
        cum,
        rate,
        inverse,
        start_state,
        d_mixed,
        next_start,
        next_map,
        beyond_start,
        spot,
        per_step,
    )
    passed = shifted(tuple(back[3:6]), "seq", -1)
    d_q_low, d_k_low, d_v_low = (
        lax.dynamic_update_slice_in_dim(whole, low(end + more), span - RIM, 0)
        for whole, end, more in zip(back[0:3], back[6:9], passed)
    )
    conv_grads = back[9:12]
    d_decay_low, d_beta_low = low(back[12]), low(back[13])
    d_log, d_bias = back[14][0], back[15][0]
    normed_rel = {order: relative_order(normed, order) for order in ORDERS}
    grad_gate_mix = jnp.concatenate(
        [
            scattered_grad(normed_rel[ORDERS[0]], d_gate_low_mix[:, : d_gate_low_mix.shape[1] // 2], ORDERS[0]),
            scattered_grad(normed_rel[ORDERS[1]], d_gate_low_mix[:, d_gate_low_mix.shape[1] // 2 :], ORDERS[1]),
        ],
        axis=1,
    )
    mix_low = jnp.concatenate([d_q_low, d_k_low, d_v_low, d_decay_low, d_beta_low], axis=1)
    width_q = d_q_low.shape[1]
    width_v = d_v_low.shape[1]
    cuts = (0, 4 * width_q // 3 // 128 * 128, 8 * width_q // 3 // 128 * 128, mix_low.shape[1])
    grad_mix = jnp.concatenate(
        [
            scattered_grad(normed_rel[order], mix_low[:, cuts[k] : cuts[k + 1]], order)
            for k, order in enumerate(ORDERS)
        ],
        axis=1,
    )
    heads_here = d_decay_low.shape[1]
    ends = (width_q, 2 * width_q, 2 * width_q + width_v, 2 * width_q + width_v + heads_here)
    grad_q, grad_k, grad_v, grad_decay, grad_beta = jnp.split(grad_mix, ends, axis=1)
    pairs = (
        (d_q_low, q_weight),
        (d_k_low, k_weight),
        (d_v_low, v_weight),
        (d_gate_low_mix, gate_weight),
        (d_decay_low, decay_weight),
        (d_beta_low, beta_weight),
    )
    d_normed = heads_sum(
        lambda pick: sum(rows_back(pick(rows), weight) for rows, weight in pairs),
        span,
        jnp.bfloat16,
    )
    _, in_norm_pull = jax.vjp(rms_scale, resid, norm_gain)
    d_in_norm, d_norm_gain = in_norm_pull(d_normed)
    input_grad = d_mid + d_in_norm
    shared = (d_norm_gain, d_ffn_gain, d_out_gain[0])
    owned = (d_log, d_bias) + tuple(part.reshape(-1) for part in conv_grads)
    flat = sum_all(jnp.concatenate(shared + owned))
    everyone = heads_gather(flat[None])
    marks = np.cumsum([part.size for part in shared + owned])
    pieces = jnp.split(everyone, marks[:-1], axis=1)
    small = [piece.sum(0) for piece in pieces[:3]] + [pieces[3].reshape(-1), pieces[4].reshape(-1)]
    for piece in pieces[5:]:
        small.append(
            jnp.swapaxes(piece.reshape(piece.shape[0], taps, -1), 0, 1).reshape(taps, -1)
        )
    return (
        output[None],
        input_grad[None],
        small[0],
        grad_q,
        grad_k,
        grad_v,
        grad_gate_mix,
        grad_decay,
        grad_beta,
        small[5],
        small[6],
        small[7],
        small[3],
        small[4],
        small[2],
        grad_out,
        small[1],
        grad_gate,
        grad_up,
        grad_down,
    )


def solution(mesh):
    in_specs = (
        P("dp", ("seq", "heads"), None),
        P("dp", ("seq", "heads"), None),
        P("dp", None),
        P(),
        P(None, "heads"),
        P(None, "heads"),
        P(None, "heads"),
        P(None, "heads"),
        P(None, "heads"),
        P(None, "heads"),
        P(None, "heads"),
        P(None, "heads"),
        P(None, "heads"),
        P("heads"),
        P("heads"),
        P(),
        P("heads", None),
        P(),
        P(None, "heads"),
        P(None, "heads"),
        P("heads", None),
    )
    out_specs = (
        P("dp", ("seq", "heads"), None),
        P("dp", ("seq", "heads"), None),
        P(),
        P(("dp", "seq"), "heads"),
        P(("dp", "seq"), "heads"),
        P(("dp", "seq"), "heads"),
        P(("dp", "seq"), "heads"),
        P(("dp", "seq"), "heads"),
        P(("dp", "seq"), "heads"),
        P(),
        P(),
        P(),
        P(),
        P(),
        P(),
        P("heads", ("dp", "seq")),
        P(),
        P(("dp", "seq"), "heads"),
        P(("dp", "seq"), "heads"),
        P("heads", ("dp", "seq")),
    )
    return jax.shard_map(body, mesh=mesh, in_specs=in_specs, out_specs=out_specs, check_vma=False)
```

```python
import functools

import jax
import jax.numpy as jnp
import numpy as np
from jax import lax
from jax.experimental import pallas as pl
from jax.experimental.pallas import tpu as pltpu
from jax.sharding import PartitionSpec as P

HEADS = 16
DK = 128
DV = 256
GROUP = 64
EPS = 1e-06
PAIR = 2 * GROUP
RIM = 8
VMEM_BYTES = 56 * 1024 * 1024


def mm(left, right):
    return lax.dot_general(
        left, right, (((1,), (0,)), ((), ())), preferred_element_type=jnp.float32
    )


def mm_nt(left, right):
    return lax.dot_general(
        left, right, (((1,), (1,)), ((), ())), preferred_element_type=jnp.float32
    )


def mm_tn(left, right):
    return lax.dot_general(
        left, right, (((0,), (0,)), ((), ())), preferred_element_type=jnp.float32
    )


def low(value):
    return value.astype(jnp.bfloat16)


def high(value):
    return value.astype(jnp.float32)


def grid_masks():
    row = lax.broadcasted_iota(jnp.int32, (PAIR, PAIR), 0)
    col = lax.broadcasted_iota(jnp.int32, (PAIR, PAIR), 1)
    same = (row // GROUP) == (col // GROUP)
    return row, col, same & (row >= col), same & (row > col)


def masks_low(row, col):
    sizes, masks = [], []
    size = 1
    while size < GROUP:
        here = ((row // (2 * size)) == (col // (2 * size))) & ((row // size) > (col // size))
        masks.append(low(jnp.where(here, 1.0, 0.0)))
        sizes.append(size)
        size *= 2
    return masks


def sigmoid(value):
    return 0.5 * jnp.tanh(0.5 * value) + 0.5


def unit_scale(value):
    return lax.rsqrt(jnp.sum(value * value, axis=-1, keepdims=True) + EPS)


def column(table, head):
    lane = lax.broadcasted_iota(jnp.int32, table.shape, 1)
    return jnp.sum(jnp.where(lane == head, table, 0.0), axis=1, keepdims=True)


def reset_row(first, base, count):
    inside = (first > base) & (first < base + count)
    return pl.multiple_of(jnp.where(inside, first - base, 0), GROUP)


def reset_places(first, base, reset):
    token = base + reset + lax.broadcasted_iota(jnp.int32, (RIM, 1), 0)
    return token - jnp.where(token >= first, first, 0)


def conv_total(ext, total, weight, reset, places):
    count, taps = total.shape[0], weight.shape[0]
    lead = RIM - taps + 1
    whole = ext[lead : lead + count, :] * weight[0:1, :]
    for tap in range(1, taps):
        whole = whole + ext[lead + tap : lead + tap + count, :] * weight[tap : tap + 1, :]
    total[...] = whole
    near = ext[pl.ds(reset, 2 * RIM), :]
    fixed = near[RIM : 2 * RIM] * weight[taps - 1 : taps, :]
    for tap in range(taps - 1):
        rows = jnp.where(places >= taps - 1 - tap, near[lead + tap : lead + tap + RIM], 0.0)
        fixed = fixed + rows * weight[tap : tap + 1, :]
    total[pl.ds(reset, RIM), :] = fixed


def load_ext(ext, rim, body):
    ext[0:RIM, :] = rim
    ext[RIM : RIM + body.shape[0], :] = body


def load_features(taps, j, refs, ext, total, reset, places):
    q_ref, k_ref, v_ref, q_rim, k_rim, v_rim, conv_q, conv_k, conv_v = refs
    cols = slice(j * DK, (j + 1) * DK)
    sources = [(q_ref, q_rim, conv_q, cols), (k_ref, k_rim, conv_k, cols)]
    for half in range(DV // DK):
        begin = j * DV + half * DK
        sources.append((v_ref, v_rim, conv_v, slice(begin, begin + DK)))
    for piece, (body, rim, weight, cut) in enumerate(sources):
        load_ext(ext.at[j, piece], rim[:, cut], body[:, cut])
        conv_total(ext.at[j, piece], total.at[j, piece], weight[:, cut], reset, places)


def block_ends(g):
    return jnp.concatenate(
        [
            jnp.broadcast_to(g[GROUP - 1 : GROUP], (GROUP, DK)),
            jnp.broadcast_to(g[PAIR - 1 : PAIR], (GROUP, DK)),
        ],
        axis=0,
    )


def decay_tables(decay_ref, beta_ref, log_ref, bias_ref, cum_ref, rate_ref):
    count = decay_ref.shape[0]
    shifted_in = decay_ref[...] + bias_ref[...]
    soft = jnp.maximum(shifted_in, 0.0) + jnp.log1p(jnp.exp(-jnp.abs(shifted_in)))
    log_decay = -jnp.exp(log_ref[...]) * soft
    _, _, within, _ = grid_masks()
    ones = jnp.where(within, 1.0, 0.0)
    for pair in range(count // PAIR):
        rows = slice(pair * PAIR, (pair + 1) * PAIR)
        cum_ref[rows, :] = lax.dot_general(
            ones,
            log_decay[rows, :],
            (((1,), (0,)), ((), ())),
            precision=lax.Precision.HIGHEST,
            preferred_element_type=jnp.float32,
        )
    rate_ref[...] = jax.nn.sigmoid(beta_ref[...])


def state_kernel(
    taps,
    per_step,
    spot,
    q_ref,
    k_ref,
    v_ref,
    q_rim,
    k_rim,
    v_rim,
    conv_q,
    conv_k,
    conv_v,
    decay_ref,
    beta_ref,
    log_ref,
    bias_ref,
    mixed_ref,
    reach_ref,
    map_ref,
    add_ref,
    inverse_ref,
    pass_ref,
    turn_ref,
    gain_ref,
    cum_ref,
    rate_ref,
    ext,
    total,
    cum,
    lower,
    halfway,
    score,
    grown_q,
    grown_k,
    scaled_v,
    tail,
    states,
    starts,
):
    step = pl.program_id(0)
    count = q_ref.shape[0]
    pairs = count // PAIR
    blocks = count // GROUP
    first, base = spot[0], spot[1]
    reset = reset_row(first, base, count)
    places = reset_places(first, base, reset)

    @pl.when(step == 0)
    def _():
        decay_tables(decay_ref, beta_ref, log_ref, bias_ref, cum_ref, rate_ref)

    row, col, within, below = grid_masks()
    refs = (q_ref, k_ref, v_ref, q_rim, k_rim, v_rim, conv_q, conv_k, conv_v)
    for j in range(per_step):
        load_features(taps, j, refs, ext, total, reset, places)
        head = step * per_step + j
        cum[j] = jnp.broadcast_to(column(cum_ref[...], head), (count, DK))
        halfway[j] = jnp.broadcast_to(column(rate_ref[...], head), (count, DK))

    def local(pair, carry):
        at = pl.ds(pl.multiple_of(pair * PAIR, PAIR), PAIR)
        for j in range(per_step):
            g = cum[j, at, :]
            b = halfway[j, at, :]
            u = total[j, 0, at, :]
            c = u * sigmoid(u)
            q = c * (unit_scale(c) * DK**-0.5)
            u = total[j, 1, at, :]
            c = u * sigmoid(u)
            k = c * unit_scale(c)
            k_low = low(k)
            spread = jnp.where(within, jnp.exp(jnp.where(within, g - g.T, 0.0)), 0.0)
            keys = mm_nt(k_low, k_low)
            lower[j, at, :] = low(jnp.where(below, b * keys * spread, 0.0))
            score[j, at, :] = low(mm_nt(low(q), k_low) * spread)
            grown = jnp.exp(g)
            for half in range(DV // DK):
                u = total[j, 2 + half, at, :]
                scaled_v[j, at, half * DK : (half + 1) * DK] = low(b * (u * sigmoid(u)))
            grown_k[j, at, :] = low(b * grown * k)
            tail[j, at, :] = low(jnp.exp(block_ends(g) - g) * k)
            grown_q[j, at, :] = grown * q
        return carry

    lax.fori_loop(0, pairs, local, 0, unroll=2)

    masks = masks_low(row, col)
    spots = [
        (j, slice(pair * PAIR, (pair + 1) * PAIR))
        for pair in range(pairs)
        for j in range(per_step)
    ]
    eye = low(jnp.where(row == col, 1.0, 0.0))
    for j, at in spots:
        inverse_ref[j, at, :] = eye - lower[j, at, :] * masks[0]
    for mask in masks[1:]:
        for j, at in spots:
            halfway[j, at, :] = mm(lower[j, at, :] * mask, inverse_ref[j, at, :])
        for j, at in spots:
            inverse = inverse_ref[j, at, :]
            inverse_ref[j, at, :] = inverse - low(mm(inverse, low(halfway[j, at, :])))

    def combine(pair, carry):
        at = pl.ds(pl.multiple_of(pair * PAIR, PAIR), PAIR)
        for j in range(per_step):
            cols = slice(j * DK, (j + 1) * DK)
            wide = slice(j * DV, (j + 1) * DV)
            inverse = inverse_ref[j, at, :]
            scored = score[j, at, :]
            u_low = low(mm(inverse, scaled_v[j, at, :]))
            w_low = low(mm(inverse, grown_k[j, at, :]))
            mixed_ref[at, wide] = mm(scored, u_low)
            pass_ref[at, cols] = low(grown_q[j, at, :] - mm(scored, w_low))
            falls = tail[j, at, :]
            for half in range(2):
                part = slice(half * GROUP, (half + 1) * GROUP)
                turn_ref[j, 2 * pair + half] = low(mm_tn(falls[part], w_low[part]))
                gain_ref[j, 2 * pair + half] = low(mm_tn(falls[part], u_low[part]))
        return carry

    lax.fori_loop(0, pairs, combine, 0, unroll=2)

    for j in range(per_step):
        states[j] = jnp.concatenate(
            [jnp.where(row == col, 1.0, 0.0), jnp.zeros((DK, DV), jnp.float32)], axis=1
        )

    def advance(block, carry):
        begin = base + block * GROUP
        keep = jnp.where((begin != 0) & (begin != first), 1.0, 0.0)
        for j in range(per_step):
            state = states[j] * keep
            state_low = low(state)
            starts[j, block] = state_low
            last = jnp.exp(cum[j, pl.ds(block * GROUP + GROUP - 1, 1), :])
            last = jnp.concatenate([last] * 3, axis=1)
            moved = last * state - mm(turn_ref[j, block], state_low)
            states[j, :, :DK] = moved[:, :DK]
            states[j, :, DK:] = moved[:, DK:] + high(gain_ref[j, block])
        return carry

    lax.fori_loop(0, blocks, advance, 0, unroll=2)

    def close(block, carry):
        at = pl.ds(pl.multiple_of(block * GROUP, GROUP), GROUP)
        for j in range(per_step):
            cols = slice(j * DK, (j + 1) * DK)
            wide = slice(j * DV, (j + 1) * DV)
            out = mm(pass_ref[at, cols], starts[j, block])
            reach_ref[at, cols] = low(out[:, :DK])
            mixed_ref[at, wide] = mixed_ref[at, wide] + out[:, DK:]
        return carry

    lax.fori_loop(0, blocks, close, 0, unroll=4)
    for j in range(per_step):
        map_ref[j] = low(states[j, :, :DK])
        add_ref[j] = low(states[j, :, DK:])


def spec(shape, index):
    return pl.BlockSpec(shape, index)


def state_forward(q, k, v, rims, convs, decay, beta, decay_log, decay_bias, spot, per_step):
    count = q.shape[0]
    heads = decay.shape[1]
    taps = convs[0].shape[0]
    n = per_step
    blocks = count // GROUP
    along = lambda i: (0, i)
    fixed = lambda i: (0, 0)
    lead = lambda i: (i, 0, 0)
    lead4 = lambda i: (i, 0, 0, 0)
    f32, bf16 = jnp.float32, jnp.bfloat16
    shape = jax.ShapeDtypeStruct
    vm = pltpu.VMEM
    return pl.pallas_call(
        functools.partial(state_kernel, taps, n),
        grid=(heads // n,),
        in_specs=[
            pl.BlockSpec(memory_space=pltpu.SMEM),
            spec((count, n * DK), along),
            spec((count, n * DK), along),
            spec((count, n * DV), along),
            spec((RIM, n * DK), along),
            spec((RIM, n * DK), along),
            spec((RIM, n * DV), along),
            spec((taps, n * DK), along),
            spec((taps, n * DK), along),
            spec((taps, n * DV), along),
            spec((count, heads), fixed),
            spec((count, heads), fixed),
            spec((1, heads), fixed),
            spec((1, heads), fixed),
        ],
        out_specs=[
            spec((count, n * DV), along),
            spec((count, n * DK), along),
            spec((n, DK, DK), lead),
            spec((n, DK, DV), lead),
            spec((n, count, PAIR), lead),
            spec((count, n * DK), along),
            spec((n, blocks, DK, DK), lead4),
            spec((n, blocks, DK, DV), lead4),
            spec((count, heads), fixed),
            spec((count, heads), fixed),
        ],
        out_shape=[
            shape((count, heads * DV), f32),
            shape((count, heads * DK), bf16),
            shape((heads, DK, DK), bf16),
            shape((heads, DK, DV), bf16),
            shape((heads, count, PAIR), bf16),
            shape((count, heads * DK), bf16),
            shape((heads, blocks, DK, DK), bf16),
            shape((heads, blocks, DK, DV), bf16),
            shape((count, heads), f32),
            shape((count, heads), f32),
        ],
        scratch_shapes=[
            vm((n, 4, count + RIM, DK), f32),
            vm((n, 4, count, DK), f32),
            vm((n, count, DK), f32),
            vm((n, count, PAIR), bf16),
            vm((n, count, PAIR), f32),
            vm((n, count, PAIR), bf16),
            vm((n, count, DK), f32),
            vm((n, count, DK), bf16),
            vm((n, count, DV), bf16),
            vm((n, count, DK), bf16),
            vm((n, DK, DK + DV), f32),
            vm((n, blocks, DK, DK + DV), bf16),
        ],
        compiler_params=pltpu.CompilerParams(
            dimension_semantics=("arbitrary",), vmem_limit_bytes=VMEM_BYTES
        ),
        cost_estimate=pl.CostEstimate(
            flops=heads * count * 10_000_000, bytes_accessed=count * heads * 4000, transcendentals=0
        ),
    )(spot, q, k, v, *rims, *convs, decay, beta, decay_log, decay_bias)


def silu(value):
    return value * sigmoid(value)


def gate_kernel(per_step, mixed_ref, reach_ref, map_ref, add_ref, far_ref, gate_ref, gain_ref, gated_ref, kept_ref, start_ref):
    for j in range(per_step):
        cols = slice(j * DK, (j + 1) * DK)
        wide = slice(j * DV, (j + 1) * DV)
        start = low(high(add_ref[j]) + mm(map_ref[j], far_ref[j]))
        start_ref[j] = start
        mixed = mixed_ref[:, wide] + mm(reach_ref[:, cols], start)
        kept_ref[:, wide] = low(mixed)
        scale = lax.rsqrt(jnp.mean(mixed * mixed, axis=-1, keepdims=True) + EPS)
        gated_ref[:, wide] = low(mixed * scale * gain_ref[...] * silu(gate_ref[:, wide]))


def gate_forward(mixed, reach, near_map, near_add, far_add, gate, gain, per_step):
    count = mixed.shape[0]
    heads = near_map.shape[0]
    n = per_step
    along = lambda i: (0, i)
    lead = lambda i: (i, 0, 0)
    bf16 = jnp.bfloat16
    return pl.pallas_call(
        functools.partial(gate_kernel, n),
        grid=(heads // n,),
        in_specs=[
            spec((count, n * DV), along),
            spec((count, n * DK), along),
            spec((n, DK, DK), lead),
            spec((n, DK, DV), lead),
            spec((n, DK, DV), lead),
            spec((count, n * DV), along),
            spec((1, DV), lambda i: (0, 0)),
        ],
        out_specs=[
            spec((count, n * DV), along),
            spec((count, n * DV), along),
            spec((n, DK, DV), lead),
        ],
        out_shape=[
            jax.ShapeDtypeStruct((count, heads * DV), bf16),
            jax.ShapeDtypeStruct((count, heads * DV), bf16),
            jax.ShapeDtypeStruct((heads, DK, DV), bf16),
        ],
        compiler_params=pltpu.CompilerParams(
            dimension_semantics=("arbitrary",), vmem_limit_bytes=VMEM_BYTES
        ),
    )(mixed, reach, near_map, near_add, far_add, gate, gain)


def gate_back_kernel(per_step, d_gated_ref, kept_ref, reach_ref, gate_ref, gain_ref, d_mixed_ref, d_gate_ref, d_start_ref, d_gain_ref):
    @pl.when(pl.program_id(0) == 0)
    def _():
        d_gain_ref[...] = jnp.zeros_like(d_gain_ref)

    for j in range(per_step):
        cols = slice(j * DK, (j + 1) * DK)
        wide = slice(j * DV, (j + 1) * DV)
        mixed = high(kept_ref[:, wide])
        scale = lax.rsqrt(jnp.mean(mixed * mixed, axis=-1, keepdims=True) + EPS)
        normal = mixed * scale
        gate = gate_ref[:, wide]
        sig = sigmoid(gate)
        d_gated = d_gated_ref[:, wide]
        d_scaled = d_gated * (gate * sig)
        d_gain_ref[...] += jnp.sum(d_scaled * normal, axis=0, keepdims=True)
        d_gate_ref[:, wide] = low(
            d_gated * (normal * gain_ref[...]) * (sig * (1.0 + gate * (1.0 - sig)))
        )
        d_normal = d_scaled * gain_ref[...]
        d_mixed = low(scale * (d_normal - normal * jnp.mean(d_normal * normal, axis=-1, keepdims=True)))
        d_mixed_ref[:, wide] = d_mixed
        d_start_ref[j] = low(mm_tn(reach_ref[:, cols], d_mixed))


def gate_backward(d_gated, kept, reach, gate, gain, per_step):
    count = kept.shape[0]
    heads = kept.shape[1] // DV
    n = per_step
    along = lambda i: (0, i)
    lead = lambda i: (i, 0, 0)
    bf16 = jnp.bfloat16
    return pl.pallas_call(
        functools.partial(gate_back_kernel, n),
        grid=(heads // n,),
        in_specs=[
            spec((count, n * DV), along),
            spec((count, n * DV), along),
            spec((count, n * DK), along),
            spec((count, n * DV), along),
            spec((1, DV), lambda i: (0, 0)),
        ],
        out_specs=[
            spec((count, n * DV), along),
            spec((count, n * DV), along),
            spec((n, DK, DV), lead),
            spec((1, DV), lambda i: (0, 0)),
        ],
        out_shape=[
            jax.ShapeDtypeStruct((count, heads * DV), bf16),
            jax.ShapeDtypeStruct((count, heads * DV), bf16),
            jax.ShapeDtypeStruct((heads, DK, DV), bf16),
            jax.ShapeDtypeStruct((1, DV), jnp.float32),
        ],
        compiler_params=pltpu.CompilerParams(
            dimension_semantics=("arbitrary",), vmem_limit_bytes=VMEM_BYTES
        ),
    )(d_gated, kept, reach, gate, gain)


def state_back_kernel(
    taps,
    per_step,
    offset,
    extra,
    spot,
    q_ref,
    k_ref,
    v_ref,
    q_rim,
    k_rim,
    v_rim,
    conv_q,
    conv_k,
    conv_v,
    decay_ref,
    log_ref,
    bias_ref,
    cum_ref,
    rate_ref,
    inverse_ref,
    pass_ref,
    turn_ref,
    gain_ref,
    start_ref,
    d_mixed_ref,
    near_ref,
    map_ref,
    far_ref,
    *rest,
):
    (
        dq_ref,
        dk_ref,
        dv_ref,
        dq_rim,
        dk_rim,
        dv_rim,
        dq_end,
        dk_end,
        dv_end,
        d_conv_q,
        d_conv_k,
        d_conv_v,
        d_decay_ref,
        d_beta_ref,
        d_log_ref,
        d_bias_ref,
        ext,
        total,
        query,
        key,
        d_value,
        cum,
        rate,
        starts,
        ends,
        states,
        d_states,
        d_total,
        d_ext,
        d_cum,
        d_rate,
    ) = rest[extra:]
    step = pl.program_id(0)
    count = q_ref.shape[0]
    pairs = count // PAIR
    blocks = count // GROUP
    first, base = spot[0], spot[1]
    reset = reset_row(first, base, count)
    places = reset_places(first, base, reset)

    @pl.when(step == 0)
    def _():
        d_cum[...] = jnp.zeros_like(d_cum)
        d_rate[...] = jnp.zeros_like(d_rate)

    refs = (q_ref, k_ref, v_ref, q_rim, k_rim, v_rim, conv_q, conv_k, conv_v)
    for j in range(per_step):
        load_features(taps, j, refs, ext, total, reset, places)
        head = offset + step * per_step + j
        cum[j] = jnp.broadcast_to(column(cum_ref[...], head), (count, DK))
        rate[j] = jnp.broadcast_to(column(rate_ref[...], head), (count, DK))
        u = total[j, 0]
        c = u * sigmoid(u)
        query[j] = c * (unit_scale(c) * DK**-0.5)
        u = total[j, 1]
        c = u * sigmoid(u)
        key[j] = c * unit_scale(c)
        states[j] = high(start_ref[j])
        d_states[j] = high(near_ref[j]) + mm_tn(map_ref[j], far_ref[j])

    row, col, within, below = grid_masks()

    def keep_of(block):
        begin = base + block * GROUP
        return jnp.where((begin != 0) & (begin != first), 1.0, 0.0)

    def last_of(j, block):
        last = jnp.exp(cum[j, pl.ds(block * GROUP + GROUP - 1, 1), :])
        return jnp.concatenate([last, last], axis=1)

    def chain(block, carry):
        back = blocks - 1 - block
        at = pl.ds(pl.multiple_of(back * GROUP, GROUP), GROUP)
        for j in range(per_step):
            state = states[j] * keep_of(block)
            state_low = low(state)
            starts[j, block] = state_low
            states[j] = (
                last_of(j, block) * state
                - mm(turn_ref[j, block], state_low)
                + high(gain_ref[j, block])
            )
            d_state = d_states[j]
            d_low = low(d_state)
            ends[j, back] = d_low
            d_out = d_mixed_ref[at, j * DV : (j + 1) * DV]
            d_states[j] = keep_of(back) * (
                last_of(j, back) * d_state
                - mm_tn(turn_ref[j, back], d_low)
                + mm_tn(pass_ref[at, j * DK : (j + 1) * DK], d_out)
            )
        return carry

    lax.fori_loop(0, blocks, chain, 0, unroll=2)

    lane = lax.broadcasted_iota(jnp.int32, (PAIR, d_cum.shape[1]), 1)
    tall = lax.broadcasted_iota(jnp.int32, (PAIR, 1), 0)

    def assemble(pair, carry):
        at = pl.ds(pl.multiple_of(pair * PAIR, PAIR), PAIR)
        halves = [slice(half * GROUP, (half + 1) * GROUP) for half in range(2)]
        for j in range(per_step):
            g = cum[j, at, :]
            b = rate[j, at, :]
            k = key[j, at, :]
            q = query[j, at, :]
            v = []
            for half in range(DV // DK):
                u = total[j, 2 + half, at, :]
                v.append(u * sigmoid(u))
            v = jnp.concatenate(v, axis=1)
            bb = jnp.concatenate([b, b], axis=1)
            k_low, q_low = low(k), low(q)
            inverse = inverse_ref[j, at, :]
            spread = jnp.where(within, jnp.exp(jnp.where(within, g - g.T, 0.0)), 0.0)
            grown = jnp.exp(g)
            fall = jnp.exp(block_ends(g) - g)
            scores = mm_nt(q_low, k_low)
            d_out = d_mixed_ref[at, j * DV : (j + 1) * DV]
            grown_k = low(b * grown * k)
            falls = low(fall * k)
            begin = [starts[j, 2 * pair + half] for half in range(2)]
            end = [ends[j, 2 * pair + half] for half in range(2)]
            known = jnp.concatenate(
                [mm(grown_k[part], begin[half]) for half, part in enumerate(halves)], axis=0
            )
            change = low(mm(inverse, low(bb * v - known)))
            pulled = jnp.concatenate(
                [mm(falls[part], end[half]) for half, part in enumerate(halves)], axis=0
            )
            rhs = mm_tn(inverse, low(mm_tn(low(scores * spread), d_out) + pulled))
            rhs_low = low(rhs)
            d_lower = jnp.where(below, -mm_nt(rhs_low, change), 0.0)
            d_score = mm_nt(d_out, change) * spread
            d_gk = jnp.concatenate(
                [-mm_nt(rhs_low[part], begin[half]) for half, part in enumerate(halves)], axis=0
            )
            d_gq = jnp.concatenate(
                [mm_nt(d_out[part], begin[half]) for half, part in enumerate(halves)], axis=0
            )
            d_tail = jnp.concatenate(
                [mm_nt(change[part], end[half]) for half, part in enumerate(halves)], axis=0
            )
            bonus = [jnp.sum(high(begin[half]) * high(end[half])) for half in range(2)]
            d_a = d_lower * mm_nt(k_low, k_low) * spread
            cross = d_a * b + d_score * scores
            gk_k = d_gk * k
            rate_col = jnp.sum(d_a + grown * gk_k, axis=-1, keepdims=True) + jnp.sum(
                rhs * v, axis=-1, keepdims=True
            )
            tail_sum = jnp.sum(d_tail * (fall * k), axis=-1, keepdims=True)
            cum_col = (
                jnp.sum(
                    cross - cross.T + b * grown * gk_k + d_gq * (grown * q), axis=-1, keepdims=True
                )
                - tail_sum
            )
            for half, part in enumerate(halves):
                at_end = half * GROUP + GROUP - 1
                more = jnp.sum(tail_sum[part], axis=0, keepdims=True) + bonus[half] * grown[
                    at_end : at_end + 1, :1
                ]
                cum_col = cum_col + jnp.where(tall == at_end, more, 0.0)
            head = offset + step * per_step + j
            d_cum[at, :] = d_cum[at, :] + jnp.where(lane == head, cum_col, 0.0)
            d_rate[at, :] = d_rate[at, :] + jnp.where(lane == head, rate_col, 0.0)
            d_keys = d_lower * spread * b
            d_keys = low(d_keys + d_keys.T)
            d_score_low = low(d_score)
            d_query = grown * d_gq + mm(d_score_low, k_low)
            d_key = b * grown * d_gk + fall * d_tail + mm(d_keys, k_low) + mm_tn(d_score_low, q_low)
            query[j, at, :] = d_query
            key[j, at, :] = d_key
            d_value[j, at, :] = bb * rhs
        return carry

    lax.fori_loop(0, pairs, assemble, 0, unroll=2)

    d_total[0:RIM, :] = jnp.zeros((RIM, DK), jnp.float32)
    d_total[RIM + count : 2 * RIM + count, :] = jnp.zeros((RIM, DK), jnp.float32)

    def conv_back(rows, weight, out_ref, rim_ref, end_ref, d_weight_ref, cols):
        size = count + RIM
        spread_rows = None
        grads = []
        for tap in range(taps):
            moved = d_total[taps - 1 - tap : taps - 1 - tap + size, :]
            term = moved * weight[tap : tap + 1, :]
            spread_rows = term if spread_rows is None else spread_rows + term
            grads.append(jnp.sum(moved * rows[...], axis=0, keepdims=True))
        d_ext[...] = spread_rows
        near = d_total[pl.ds(reset + RIM, RIM), :]
        around = rows[pl.ds(reset, 2 * RIM), :]
        wrong_rows = jnp.zeros((2 * RIM, DK), jnp.float32)
        for tap in range(taps - 1):
            lead = RIM - taps + 1 + tap
            wrong = jnp.where(places >= taps - 1 - tap, 0.0, near)
            grads[tap] = grads[tap] - jnp.sum(
                wrong * around[lead : lead + RIM], axis=0, keepdims=True
            )
            wrong_rows = wrong_rows + jnp.concatenate(
                [
                    jnp.zeros((lead, DK), jnp.float32),
                    wrong * weight[tap : tap + 1, :],
                    jnp.zeros((RIM - lead, DK), jnp.float32),
                ],
                axis=0,
            )
        d_ext[pl.ds(reset, 2 * RIM), :] = d_ext[pl.ds(reset, 2 * RIM), :] - wrong_rows
        d_weight_ref[:, cols] = jnp.concatenate(grads, axis=0)
        rim_ref[:, cols] = d_ext[0:RIM, :]
        out_ref[:, cols] = low(d_ext[RIM : RIM + count, :])
        end_ref[:, cols] = d_ext[count : count + RIM, :]

    for j in range(per_step):
        cols = slice(j * DK, (j + 1) * DK)

        def unit_back(piece, d_unit, factor):
            u = total[j, piece]
            sig = sigmoid(u)
            c = u * sig
            scale = unit_scale(c)
            unit = c * scale
            d_unit = d_unit * factor
            d_c = scale * (d_unit - unit * jnp.sum(d_unit * unit, axis=-1, keepdims=True))
            d_total[RIM : RIM + count, :] = d_c * (sig * (1.0 + u * (1.0 - sig)))

        unit_back(0, query[j], DK**-0.5)
        conv_back(ext.at[j, 0], conv_q[:, cols], dq_ref, dq_rim, dq_end, d_conv_q, cols)
        unit_back(1, key[j], 1.0)
        conv_back(ext.at[j, 1], conv_k[:, cols], dk_ref, dk_rim, dk_end, d_conv_k, cols)
        for half in range(DV // DK):
            begin = j * DV + half * DK
            cut = slice(begin, begin + DK)
            u = total[j, 2 + half]
            sig = sigmoid(u)
            d_total[RIM : RIM + count, :] = d_value[j, :, half * DK : (half + 1) * DK] * (
                sig * (1.0 + u * (1.0 - sig))
            )
            conv_back(ext.at[j, 2 + half], conv_v[:, cut], dv_ref, dv_rim, dv_end, d_conv_v, cut)

    @pl.when(step == pl.num_programs(0) - 1)
    def _():
        shifted_in = decay_ref[...] + bias_ref[...]
        soft = jnp.maximum(shifted_in, 0.0) + jnp.log1p(jnp.exp(-jnp.abs(shifted_in)))
        speed = -jnp.exp(log_ref[...])
        after = jnp.where(within, 1.0, 0.0)
        d_log = jnp.zeros_like(d_log_ref)
        d_bias = jnp.zeros_like(d_bias_ref)
        for pair in range(pairs):
            rows = slice(pair * PAIR, (pair + 1) * PAIR)
            d_decay = lax.dot_general(
                after,
                d_cum[rows, :],
                (((0,), (0,)), ((), ())),
                precision=lax.Precision.HIGHEST,
                preferred_element_type=jnp.float32,
            )
            d_log = d_log + jnp.sum(d_decay * (speed * soft[rows]), axis=0, keepdims=True)
            d_in = d_decay * speed * jax.nn.sigmoid(shifted_in[rows])
            d_bias = d_bias + jnp.sum(d_in, axis=0, keepdims=True)
            d_decay_ref[rows, :] = d_in
        d_log_ref[...] = d_log
        d_bias_ref[...] = d_bias
        rates = rate_ref[...]
        d_beta_ref[...] = d_rate[...] * rates * (1.0 - rates)


def state_backward(
    q, k, v, rims, convs, decay, decay_log, decay_bias, cum, rate, saved, start, d_mixed, near, near_map, far, spot, per_step, offset, held, after
):
    count = q.shape[0]
    heads = decay.shape[1]
    taps = convs[0].shape[0]
    n = per_step
    blocks = count // GROUP
    skip = offset // n
    along = lambda i: (0, i + skip)
    fixed = lambda i: (0, 0)
    lead = lambda i: (i + skip, 0, 0)
    lead4 = lambda i: (i + skip, 0, 0, 0)
    out_along = lambda i: (0, i)
    f32, bf16 = jnp.float32, jnp.bfloat16
    shape = jax.ShapeDtypeStruct
    vm = pltpu.VMEM
    thin = [(RIM, DK), (RIM, DK), (RIM, DV)]
    out_blocks = [(count, DK), (count, DK), (count, DV)] + thin + thin
    out_blocks += [(taps, DK), (taps, DK), (taps, DV)]
    tables = [(count, heads), (count, heads), (1, heads), (1, heads)]
    return pl.pallas_call(
        functools.partial(state_back_kernel, taps, n, offset, len(after)),
        grid=(held // n,),
        in_specs=[
            pl.BlockSpec(memory_space=pltpu.SMEM),
            spec((count, n * DK), along),
            spec((count, n * DK), along),
            spec((count, n * DV), along),
            spec((RIM, n * DK), along),
            spec((RIM, n * DK), along),
            spec((RIM, n * DV), along),
            spec((taps, n * DK), along),
            spec((taps, n * DK), along),
            spec((taps, n * DV), along),
            spec((count, heads), fixed),
            spec((1, heads), fixed),
            spec((1, heads), fixed),
            spec((count, heads), fixed),
            spec((count, heads), fixed),
            spec((n, count, PAIR), lead),
            spec((count, n * DK), along),
            spec((n, blocks, DK, DK), lead4),
            spec((n, blocks, DK, DV), lead4),
            spec((n, DK, DV), lead),
            spec((count, n * DV), along),
            spec((n, DK, DV), lead),
            spec((n, DK, DK), lead),
            spec((n, DK, DV), lead),
        ]
        + [pl.BlockSpec(memory_space=pl.ANY) for _ in after],
        out_specs=[spec((rows, n * width), out_along) for rows, width in out_blocks]
        + [spec(block, fixed) for block in tables],
        out_shape=[
            shape((rows, held * width), bf16 if i < 3 else f32)
            for i, (rows, width) in enumerate(out_blocks)
        ]
        + [shape(block, f32) for block in tables],
        scratch_shapes=[
            vm((n, 4, count + RIM, DK), f32),
            vm((n, 4, count, DK), f32),
            vm((n, count, DK), f32),
            vm((n, count, DK), f32),
            vm((n, count, DV), f32),
            vm((n, count, DK), f32),
            vm((n, count, DK), f32),
            vm((n, blocks, DK, DV), bf16),
            vm((n, blocks, DK, DV), bf16),
            vm((n, DK, DV), f32),
            vm((n, DK, DV), f32),
            vm((count + 2 * RIM, DK), f32),
            vm((count + RIM, DK), f32),
            vm((count, heads), f32),
            vm((count, heads), f32),
        ],
        compiler_params=pltpu.CompilerParams(
            dimension_semantics=("arbitrary",), vmem_limit_bytes=VMEM_BYTES
        ),
        cost_estimate=pl.CostEstimate(
            flops=held * count * 14_000_000, bytes_accessed=count * held * 6000, transcendentals=0
        ),
    )(
        spot,
        q,
        k,
        v,
        *rims,
        *convs,
        decay,
        decay_log,
        decay_bias,
        cum,
        rate,
        *saved,
        start,
        d_mixed,
        near,
        near_map,
        far,
        *after,
    )


def shifted(value, axis, steps):
    count = lax.axis_size(axis)
    leading, last = (max(0, -steps), min(count, count - steps))
    return lax.ppermute(value, axis, [(source, source + steps) for source in range(leading, last)])


def rms_scale(values, gain):
    return values * lax.rsqrt(jnp.mean(values * values, axis=-1, keepdims=True) + EPS) * gain


def swish_product(gate_ffn, up_ffn):
    return jax.nn.silu(gate_ffn) * up_ffn


def project(rows, weight):
    return jnp.dot(rows, weight, preferred_element_type=jnp.float32)


def rows_product(left, right):
    return jnp.dot(left, right, preferred_element_type=jnp.float32)


def rows_back(left, weight):
    return jnp.einsum("tc,dc->td", left, weight, preferred_element_type=jnp.float32)


def weight_grad(rows, grads):
    return jnp.einsum("td,tc->dc", rows, grads, preferred_element_type=jnp.float32)


STAGES = {"x": ("seq", 0, 1), "y": ("seq", 1, 2), "l": ("dp", 0, 4), "h": ("dp", 1, 8)}


def trade(value, stage):
    axis, bit, _ = STAGES[stage]
    count = lax.axis_size(axis)
    return lax.ppermute(value, axis, [(place, place ^ (1 << bit)) for place in range(count)])


def arrange_kernel(picks, left_ref, right_ref, *rest):
    left_out, right_out = rest[-2:]
    width = left_ref.shape[1] // 16
    for place in range(16):
        source = pl.ds(pl.multiple_of(picks[place] * width, width), width)
        target = slice(place * width, (place + 1) * width)
        left_out[:, target] = left_ref[:, source]
        right_out[:, target] = right_ref[:, source]


def relative_order(rows, more, order, after):
    own = lax.axis_index("dp") * lax.axis_size("seq") + lax.axis_index("seq")
    masks = [
        sum(STAGES[stage][2] for k, stage in enumerate(order) if place >> (3 - k) & 1)
        for place in range(16)
    ]
    picks = own ^ jnp.array(masks, jnp.int32)
    count, width = rows.shape
    size = 96
    piece = pl.BlockSpec((size, width), lambda i: (i, 0))
    return pl.pallas_call(
        arrange_kernel,
        grid=(count // size,),
        in_specs=[pl.BlockSpec(memory_space=pltpu.SMEM), piece, piece]
        + [pl.BlockSpec(memory_space=pl.ANY) for _ in after],
        out_specs=[piece, piece],
        out_shape=[jax.ShapeDtypeStruct((count, width), rows.dtype)] * 2,
        compiler_params=pltpu.CompilerParams(
            dimension_semantics=("arbitrary",), vmem_limit_bytes=VMEM_BYTES
        ),
        cost_estimate=pl.CostEstimate(
            flops=0, bytes_accessed=12 * count * width, transcendentals=0
        ),
    )(picks, rows, more, *after)


def own_side(stage):
    axis, bit, _ = STAGES[stage]
    return lax.rem(lax.axis_index(axis) // (1 << bit), 2)


def paired_rows(own_rows, got_rows, order, *after):
    both = relative_order(own_rows, got_rows, order[1:] + order[:1], after)
    return tuple(heads_gather(rows) for rows in both)


def trade_halves(grads, order):
    half = grads.shape[1] // 2
    side = own_side(order[0])
    mine = lax.dynamic_slice_in_dim(grads, side * half, half, 1)
    theirs = lax.dynamic_slice_in_dim(grads, (1 - side) * half, half, 1)
    return mine, trade(theirs, order[0])


def pair_grad(rows, halves, begin, end):
    width = rows[0].shape[1] // 16
    cut = slice(begin * width, end * width)
    return sum(weight_grad(part[:, cut], grads) for part, grads in zip(rows, halves))


def grad_open(rows, halves, order):
    sent = low(pair_grad(rows, halves, 8, 16))
    return rows, halves, sent, trade(sent, order[1])


def grad_next(opened, order):
    rows, halves, _, first = opened
    width = rows[0].shape[1] // 16
    sent = low(pair_grad(rows, halves, 4, 8) + high(first[4 * width :]))
    rest = pair_grad(rows, halves, 0, 4) + high(first[: 4 * width])
    return rest, sent, trade(sent, order[2])


def grad_close(moved, order):
    rest, _, second = moved
    width = rest.shape[0] // 4
    half = rest.shape[1]
    side = own_side(order[0])
    third = trade(low(rest[2 * width :] + high(second[2 * width :])), order[3])
    final = rest[: 2 * width] + high(second[: 2 * width]) + high(third)
    other = high(trade(low(final[width:]), order[0]))
    left = jnp.where(side == 0, final[:width], other)
    right = jnp.where(side == 0, other, final[:width])
    return jnp.concatenate([left, right], axis=1)


def finish_kernel(plan, head_steps, *refs):
    groups = len(plan)
    grads, small_ref = refs[:groups], refs[groups]
    outs, small_out = refs[groups + 1 : 2 * groups + 1], refs[2 * groups + 1]
    scratch = refs[2 * groups + 2 :]
    buffers = [scratch[7 * g : 7 * g + 7] for g in range(groups)]
    small_sum, small_got, send_sem, recv_sem, small_send, small_recv = scratch[7 * groups :]
    width = grads[0].shape[0] // 16

    def side(stage):
        axis, bit, _ = STAGES[stage]
        return lax.rem(lax.axis_index(axis) // (1 << bit), 2)

    def partner(stage):
        axis, bit, _ = STAGES[stage]
        return {axis: lax.axis_index(axis) + (1 - 2 * side(stage)) * (1 << bit)}

    def head_partner(step):
        me = lax.axis_index("heads")
        return {"heads": me + (1 - 2 * lax.rem(me // step, 2)) * step}

    barrier = pltpu.get_barrier_semaphore()
    targets = [partner(stage) for stage in "xylh"] + [head_partner(step) for step in head_steps]
    for target in targets:
        pl.semaphore_signal(
            barrier, inc=1, device_id=target, device_id_type=pl.DeviceIdType.MESH
        )
    pl.semaphore_wait(barrier, len(targets))

    started = []

    def send(source, target, sems, device):
        copy = pltpu.make_async_remote_copy(
            src_ref=source,
            dst_ref=target,
            send_sem=sems[0],
            recv_sem=sems[1],
            device_id=device,
            device_id_type=pl.DeviceIdType.MESH,
        )
        copy.start()
        started.append(copy)
        return copy

    most = max(len(cuts) for _, cuts in plan)
    chunks, number = [], 0
    rounds = [[] for _ in range(most)]
    for g, (order, cuts) in enumerate(plan):
        for k, cut in enumerate(cuts):
            chunks.append((g, order, slice(*cut)))
            rounds[k].append(number)
            number += 1
    copies = {}

    def launch(stage, index, source, target, name):
        sems = (send_sem.at[4 * index + stage], recv_sem.at[4 * index + stage])
        copies[stage, index] = send(source, target, sems, partner(name))

    def open_chunk(index):
        g, order, cut = chunks[index]
        launch(0, index, grads[g].at[8 * width :, cut], buffers[g][0].at[:, cut], order[1])

    def second_chunk(index):
        g, order, cut = chunks[index]
        copies[0, index].wait_recv()
        got, sent, got_next = buffers[g][0], buffers[g][4], buffers[g][1]
        rows = slice(4 * width, 8 * width)
        sent[:, cut] = low(high(grads[g][rows, cut]) + high(got[rows, cut]))
        launch(1, index, sent.at[:, cut], got_next.at[:, cut], order[2])

    def third_chunk(index):
        g, order, cut = chunks[index]
        copies[1, index].wait_recv()
        rows = slice(2 * width, 4 * width)
        first, second, sent = buffers[g][0], buffers[g][1], buffers[g][5]
        sent[:, cut] = low(
            high(grads[g][rows, cut]) + high(first[rows, cut]) + high(second[rows, cut])
        )
        launch(2, index, sent.at[:, cut], buffers[g][2].at[:, cut], order[3])

    def fourth_chunk(index):
        g, order, cut = chunks[index]
        copies[2, index].wait_recv()
        first, second, third, sent = (buffers[g][k] for k in (0, 1, 2, 6))
        half = grads[g].shape[1]
        rows = slice(0, 2 * width)
        final = high(grads[g][rows, cut]) + high(first[rows, cut])
        final = final + high(second[rows, cut]) + high(third[:, cut])
        sent[:, cut] = low(final[width:])
        launch(3, index, sent.at[:, cut], buffers[g][3].at[:, cut], order[0])
        place = pl.multiple_of(side(order[0]) * half + cut.start, 128)
        outs[g][:, pl.ds(place, cut.stop - cut.start)] = final[:width]

    def last_chunk(index):
        g, order, cut = chunks[index]
        copies[3, index].wait_recv()
        half = grads[g].shape[1]
        place = pl.multiple_of((1 - side(order[0])) * half + cut.start, 128)
        outs[g][:, pl.ds(place, cut.stop - cut.start)] = high(buffers[g][3][:, cut])

    small_copies = []
    names = "xylh"

    def small_step(step):
        if step >= 1 and step <= 4:
            small_copies[step - 1].wait_recv()
            small_sum[step] = small_sum[step - 1] + small_got[step - 1]
        if step == 4:
            small_out[pl.ds(lax.axis_index("heads"), 1)] = small_sum[4:5]
        if step < 4:
            if step == 0:
                small_sum[0] = small_ref[...]
            sems = (small_send.at[step], small_recv.at[step])
            small_copies.append(
                send(small_sum.at[step], small_got.at[step], sems, partner(names[step]))
            )
        elif step - 4 <= len(head_steps):
            k = step - 4
            if k >= 1:
                small_copies[step - 1].wait_recv()
            if k < len(head_steps):
                size = head_steps[k]
                begin = lax.axis_index("heads") // size * size
                block = small_out.at[pl.ds(begin, size)]
                sems = (small_send.at[step], small_recv.at[step])
                small_copies.append(send(block, block, sems, head_partner(size)))

    total_small = 5 + len(head_steps)
    for index in rounds[0]:
        open_chunk(index)
    small_step(0)
    if most > 1:
        for index in rounds[1]:
            open_chunk(index)
    for t in range(max(most + 3, total_small - 1)):
        if t < most:
            for index in rounds[t]:
                second_chunk(index)
        if t + 2 < most:
            for index in rounds[t + 2]:
                open_chunk(index)
        for lag, work in ((1, third_chunk), (2, fourth_chunk), (3, last_chunk)):
            if 0 <= t - lag < most:
                for index in rounds[t - lag]:
                    work(index)
        if t + 1 < total_small:
            small_step(t + 1)
    for copy in started:
        copy.wait_send()


def finish(grads, orders, small):
    count = lax.axis_size("heads")
    head_steps = []
    while 1 << len(head_steps) < count:
        head_steps.append(1 << len(head_steps))
    plan, scratch = [], []
    for array, order in zip(grads, orders):
        full, half = array.shape
        step = min(256, half)
        plan.append((order, [(at, at + step) for at in range(0, half, step)]))
        for rows in (8, 4, 2, 1, 4, 2, 1):
            scratch.append(pltpu.VMEM((full // 16 * rows, half), jnp.bfloat16))
    pieces = sum(len(cuts) for _, cuts in plan)
    inside = pl.BlockSpec(memory_space=pltpu.VMEM)
    rows = small.shape[0]
    f32 = jnp.float32
    return pl.pallas_call(
        functools.partial(finish_kernel, tuple(plan), tuple(head_steps)),
        in_specs=[inside] * (len(grads) + 1),
        out_specs=[inside] * (len(grads) + 1),
        out_shape=[
            jax.ShapeDtypeStruct((array.shape[0] // 16, 2 * array.shape[1]), f32)
            for array in grads
        ]
        + [jax.ShapeDtypeStruct((count, rows, 128), f32)],
        scratch_shapes=scratch
        + [
            pltpu.VMEM((5, rows, 128), f32),
            pltpu.VMEM((4, rows, 128), f32),
            pltpu.SemaphoreType.DMA((4 * pieces,)),
            pltpu.SemaphoreType.DMA((4 * pieces,)),
            pltpu.SemaphoreType.DMA((8,)),
            pltpu.SemaphoreType.DMA((8,)),
        ],
        compiler_params=pltpu.CompilerParams(
            collective_id=0, has_side_effects=True, vmem_limit_bytes=VMEM_BYTES
        ),
        cost_estimate=pl.CostEstimate(
            flops=100_000_000_000, bytes_accessed=20_000_000, transcendentals=0
        ),
    )(*grads, small)


def heads_gather(rows):
    count = lax.axis_size("heads")
    own = lax.axis_index("heads")
    step = 1
    while step < count:
        other = lax.ppermute(rows, "heads", [(place, place ^ step) for place in range(count)])
        upper = lax.rem(own // step, 2) == 1
        rows = jnp.concatenate(
            [jnp.where(upper, other, rows), jnp.where(upper, rows, other)], axis=0
        )
        step *= 2
    return rows


def heads_sum(compute, count, kind):
    if lax.axis_size("heads") != 2:
        whole = compute(lambda rows: rows).astype(kind)
        return high(lax.psum_scatter(whole, "heads", scatter_dimension=0, tiled=True))
    own = lax.axis_index("heads")
    half = count // 2

    def part(which):
        return compute(lambda rows: lax.dynamic_slice_in_dim(rows, which * half, half, 0))

    got = lax.ppermute(part(1 - own).astype(kind), "heads", [(0, 1), (1, 0)])
    return part(own) + high(got)


ORDERS = ("xylh", "ylxh", "lxyh")


def body(
    hidden_in,
    out_cotangent,
    lengths,
    norm_gain,
    q_weight,
    k_weight,
    v_weight,
    gate_weight,
    decay_weight,
    beta_weight,
    conv_q,
    conv_k,
    conv_v,
    decay_log,
    decay_bias,
    out_gain,
    out_weight,
    ffn_gain,
    ffn_gate,
    ffn_up,
    ffn_down,
):
    resid = hidden_in[0].astype(jnp.float32)
    normed_own = rms_scale(resid, norm_gain).astype(jnp.bfloat16)
    normed, cotangent = (
        heads_gather(normed_own),
        heads_gather(out_cotangent[0]),
    )
    span = normed.shape[0]
    normed_got = {order: trade(normed_own, order[0]) for order in ORDERS}
    cotangent_got = trade(out_cotangent[0], ORDERS[2][0])
    taps = conv_q.shape[0]
    q_proj = project(normed, q_weight)
    k_proj = project(normed, k_weight)
    v_proj = project(normed, v_weight)
    gate_proj = project(normed, gate_weight)
    heads = decay_weight.shape[1]
    per_step = min(2, heads)
    narrow = project(normed, jnp.concatenate([decay_weight, beta_weight], axis=1))
    decay_proj, beta_proj = narrow[:, :heads], narrow[:, heads:]
    seq_index = lax.axis_index("seq")
    spot = jnp.stack([lengths[0, 0], seq_index * span]).astype(jnp.int32)
    rims = shifted((q_proj[span - RIM :], k_proj[span - RIM :], v_proj[span - RIM :]), "seq", 1)
    convs = (conv_q, conv_k, conv_v)
    log_row, bias_row, gain_row = decay_log[None], decay_bias[None], out_gain[None]
    mixed_local, reach, span_map, span_add, *saved, cum, rate = state_forward(
        q_proj, k_proj, v_proj, rims, convs, decay_proj, beta_proj, log_row, bias_row, spot, per_step
    )
    near_map, near_add = shifted((span_map, span_add), "seq", 1)
    far_add = shifted(span_add, "seq", 2)
    next_map = shifted(span_map, "seq", -1)
    gated_low, mixed_low, start_state = gate_forward(
        mixed_local, reach, near_map, near_add, far_add, gate_proj, gain_row, per_step
    )
    mixer = heads_sum(
        lambda pick: rows_product(pick(gated_low), out_weight), span, jnp.float32
    )
    resid_mid = resid + mixer
    ffn_own = rms_scale(resid_mid, ffn_gain).astype(jnp.bfloat16)
    ffn_in = heads_gather(ffn_own)
    ffn_got = {order: trade(ffn_own, order[0]) for order in ORDERS[:2]}
    out_halves = trade_halves(gated_low, ORDERS[0])
    gate_ffn = project(ffn_in, ffn_gate)
    up_ffn = project(ffn_in, ffn_up)
    act, act_pull = jax.vjp(swish_product, gate_ffn, up_ffn)
    act_low = act.astype(jnp.bfloat16)
    down_halves = trade_halves(act_low, ORDERS[2])
    ffn_out = heads_sum(lambda pick: rows_product(pick(act_low), ffn_down), span, jnp.bfloat16)
    output = (resid_mid + ffn_out).astype(jnp.bfloat16)
    d_act = jnp.einsum("td,fd->tf", cotangent, ffn_down, preferred_element_type=jnp.float32)
    d_gate_ffn, d_up_ffn = act_pull(d_act)
    d_gate_low = d_gate_ffn.astype(jnp.bfloat16)
    d_up_low = d_up_ffn.astype(jnp.bfloat16)
    cotangent_rel = paired_rows(out_cotangent[0], cotangent_got, ORDERS[2], act_low)
    gate_halves = trade_halves(d_gate_low, ORDERS[0])
    up_halves = trade_halves(d_up_low, ORDERS[1])
    ffn_rel = {
        order: paired_rows(ffn_own, ffn_got[order], order, d_gate_low) for order in ORDERS[:2]
    }
    down_open = grad_open(cotangent_rel, down_halves, ORDERS[2])
    gate_open = grad_open(ffn_rel[ORDERS[0]], gate_halves, ORDERS[0])
    up_open = grad_open(ffn_rel[ORDERS[1]], up_halves, ORDERS[1])
    d_ffn = heads_sum(
        lambda pick: rows_back(pick(d_gate_low), ffn_gate) + rows_back(pick(d_up_low), ffn_up),
        span,
        jnp.float32,
    )
    _, ffn_norm_pull = jax.vjp(rms_scale, resid_mid, ffn_gain)
    d_mid_norm, d_ffn_gain = ffn_norm_pull(d_ffn)
    d_mid = out_cotangent[0].astype(jnp.float32) + d_mid_norm
    d_mid_low = low(d_mid)
    d_mid_all = heads_gather(d_mid_low)
    d_mid_got = trade(d_mid_low, ORDERS[0][0])
    d_gated = jnp.einsum("td,cd->tc", d_mid_all, out_weight, preferred_element_type=jnp.float32)
    d_mixed, d_gate_low_mix, d_start, d_out_gain = gate_backward(
        d_gated, mixed_low, reach, gate_proj, gain_row, per_step
    )
    next_start = shifted(d_start, "seq", -1)
    beyond_start = shifted(d_start, "seq", -2)
    mix_halves = trade_halves(d_gate_low_mix, ORDERS[2])
    parts = 2 if heads > 1 else 1
    held = heads // parts
    per_step = min(per_step, held)
    backs, grads_low, mix_halves_part = [], [], []
    for part in range(parts):
        if part == 0:
            after = (down_open[2], gate_open[2], up_open[2])
        else:
            down_next = grad_next(down_open, ORDERS[2])
            gate_next = grad_next(gate_open, ORDERS[0])
            up_next = grad_next(up_open, ORDERS[1])
            gate_mix_rel = paired_rows(normed_own, normed_got[ORDERS[2]], ORDERS[2], up_next[1])
            gate_mix_grad = low(pair_grad(gate_mix_rel, mix_halves, 0, 16))
            d_mid_rel = paired_rows(d_mid_low, d_mid_got, ORDERS[0], up_next[1])
            out_grad = low(pair_grad(d_mid_rel, out_halves, 0, 16))
            after = (down_next[1], gate_next[1], up_next[1], gate_mix_grad, out_grad)
        back = state_backward(
            q_proj,
            k_proj,
            v_proj,
            rims,
            convs,
            decay_proj,
            log_row,
            bias_row,
            cum,
            rate,
            saved,
            start_state,
            d_mixed,
            next_start,
            next_map,
            beyond_start,
            spot,
            per_step,
            part * held,
            held,
            after,
        )
        rim = shifted(jnp.concatenate(back[3:6], axis=1), "seq", -1)
        passed = jnp.split(rim, (held * DK, 2 * held * DK), axis=1)
        lows = [
            lax.dynamic_update_slice_in_dim(whole, low(end + more), span - RIM, 0)
            for whole, end, more in zip(back[0:3], back[6:9], passed)
        ]
        backs.append(back)
        grads_low.append(lows)
    d_q_low, d_k_low, d_v_low = (jnp.concatenate(part, axis=1) for part in zip(*grads_low))
    conv_grads = [jnp.concatenate(part, axis=1) for part in zip(*(back[9:12] for back in backs))]
    d_decay_low, d_beta_low, d_log, d_bias = (
        sum(part) for part in zip(*(back[12:16] for back in backs))
    )
    d_decay_low, d_beta_low = low(d_decay_low), low(d_beta_low)
    d_log, d_bias = d_log[0], d_bias[0]
    grad_down = grad_close(down_next, ORDERS[2]).T
    grad_gate = grad_close(gate_next, ORDERS[0])
    grad_up = grad_close(up_next, ORDERS[1])
    tails, tail_orders = [gate_mix_grad, out_grad], [ORDERS[2], ORDERS[0]]
    for part, lows in enumerate(grads_low):
        flat_low = jnp.concatenate(lows, axis=1)
        pieces = 2 if part == parts - 1 and parts > 1 else 1
        size = flat_low.shape[1] // pieces
        for piece in range(pieces):
            order = ORDERS[(1, 0, 2)[part + piece]]
            if order == ORDERS[2]:
                rows = gate_mix_rel
            else:
                rows = paired_rows(normed_own, normed_got[order], order, backs[0][0])
            halves = trade_halves(flat_low[:, piece * size : (piece + 1) * size], order)
            tails.append(low(pair_grad(rows, halves, 0, 16)))
            tail_orders.append(order)
    narrow_grad = weight_grad(jnp.concatenate([d_decay_low, d_beta_low], axis=1), normed)
    pairs = (
        (d_q_low, q_weight),
        (d_k_low, k_weight),
        (d_v_low, v_weight),
        (d_gate_low_mix, gate_weight),
        (d_decay_low, decay_weight),
        (d_beta_low, beta_weight),
    )
    d_normed = heads_sum(
        lambda pick: sum(rows_back(pick(rows), weight) for rows, weight in pairs),
        span,
        jnp.bfloat16,
    )
    _, in_norm_pull = jax.vjp(rms_scale, resid, norm_gain)
    d_in_norm, d_norm_gain = in_norm_pull(d_normed)
    input_grad = d_mid + d_in_norm
    owned = (d_log, d_bias) + tuple(part.reshape(-1) for part in conv_grads)
    shared = (d_norm_gain, d_ffn_gain, d_out_gain[0], narrow_grad.reshape(-1))
    marks = [int(mark) for mark in np.cumsum([part.size for part in shared + owned])]
    rows = -(-marks[-1] // 1024) * 8
    blank = jnp.zeros((rows * 128 - marks[-1],), jnp.float32)
    flat = jnp.concatenate(shared + owned + (blank,)).reshape(rows, 128)
    grad_gate_mix, grad_out, *mixes, everyone = finish(tails, tail_orders, flat)
    grad_out = grad_out.T
    everyone = everyone.reshape(everyone.shape[0], -1)
    own_head = lax.axis_index("heads")
    narrow_own = lax.dynamic_slice(
        everyone, (own_head, marks[2]), (1, narrow_grad.size)
    ).reshape(narrow_grad.shape)
    shard = lax.axis_index("dp") * lax.axis_size("seq") + lax.axis_index("seq")
    size = narrow_grad.shape[1] // 16
    narrow_sum = lax.dynamic_slice_in_dim(narrow_own, shard * size, size, 1).T
    grad_decay, grad_beta = narrow_sum[:, :heads], narrow_sum[:, heads:]
    pieces = jnp.split(everyone, marks, axis=1)[:-1]
    small = [piece.sum(0) for piece in pieces[:3]]
    small += [pieces[4].reshape(-1), pieces[5].reshape(-1)]
    for piece in pieces[6:]:
        small.append(
            jnp.swapaxes(piece.reshape(piece.shape[0], taps, -1), 0, 1).reshape(taps, -1)
        )
    wide = held * DK
    by_part = [mixes[0]] if parts == 1 else [mixes[0], jnp.concatenate(mixes[1:], axis=1)]
    grad_q, grad_k, grad_v = (
        jnp.concatenate(part, axis=1)
        for part in zip(*(jnp.split(mix, (wide, 2 * wide), axis=1) for mix in by_part))
    )
    return (
        output[None],
        input_grad[None],
        small[0],
        grad_q,
        grad_k,
        grad_v,
        grad_gate_mix,
        grad_decay,
        grad_beta,
        small[5],
        small[6],
        small[7],
        small[3],
        small[4],
        small[2],
        grad_out,
        small[1],
        grad_gate,
        grad_up,
        grad_down,
    )


def solution(mesh):
    in_specs = (
        P("dp", ("seq", "heads"), None),
        P("dp", ("seq", "heads"), None),
        P("dp", None),
        P(),
        P(None, "heads"),
        P(None, "heads"),
        P(None, "heads"),
        P(None, "heads"),
        P(None, "heads"),
        P(None, "heads"),
        P(None, "heads"),
        P(None, "heads"),
        P(None, "heads"),
        P("heads"),
        P("heads"),
        P(),
        P("heads", None),
        P(),
        P(None, "heads"),
        P(None, "heads"),
        P("heads", None),
    )
    out_specs = (
        P("dp", ("seq", "heads"), None),
        P("dp", ("seq", "heads"), None),
        P(),
        P(("dp", "seq"), "heads"),
        P(("dp", "seq"), "heads"),
        P(("dp", "seq"), "heads"),
        P(("dp", "seq"), "heads"),
        P(("dp", "seq"), "heads"),
        P(("dp", "seq"), "heads"),
        P(),
        P(),
        P(),
        P(),
        P(),
        P(),
        P("heads", ("dp", "seq")),
        P(),
        P(("dp", "seq"), "heads"),
        P(("dp", "seq"), "heads"),
        P("heads", ("dp", "seq")),
    )
    return jax.shard_map(body, mesh=mesh, in_specs=in_specs, out_specs=out_specs, check_vma=False)
```

```python
import functools

import jax
import jax.numpy as jnp
from jax import lax
from jax.experimental import pallas as pl
from jax.experimental.pallas import tpu as pltpu
from jax.sharding import PartitionSpec as P

HEADS = 16
DK = 128
DV = 256
GROUP = 64
EPS = 1e-06
PAIR = 2 * GROUP
RIM = 8
VMEM_BYTES = 56 * 1024 * 1024
LITTLE = pl.CostEstimate(flops=0, bytes_accessed=0, transcendentals=0)


def mm(left, right):
    return lax.dot_general(
        left, right, (((1,), (0,)), ((), ())), preferred_element_type=jnp.float32
    )


def mm_nt(left, right):
    return lax.dot_general(
        left, right, (((1,), (1,)), ((), ())), preferred_element_type=jnp.float32
    )


def mm_tn(left, right):
    return lax.dot_general(
        left, right, (((0,), (0,)), ((), ())), preferred_element_type=jnp.float32
    )


def low(value):
    return value.astype(jnp.bfloat16)


def high(value):
    return value.astype(jnp.float32)


def grid_masks():
    row = lax.broadcasted_iota(jnp.int32, (PAIR, PAIR), 0)
    col = lax.broadcasted_iota(jnp.int32, (PAIR, PAIR), 1)
    same = (row // GROUP) == (col // GROUP)
    return row, col, same & (row >= col), same & (row > col)


def masks_low(row, col):
    sizes, masks = [], []
    size = 1
    while size < GROUP:
        here = ((row // (2 * size)) == (col // (2 * size))) & ((row // size) > (col // size))
        masks.append(low(jnp.where(here, 1.0, 0.0)))
        sizes.append(size)
        size *= 2
    return masks


def sigmoid(value):
    return 0.5 * jnp.tanh(0.5 * value) + 0.5


def unit_scale(value):
    return lax.rsqrt(jnp.sum(value * value, axis=-1, keepdims=True) + EPS)


def column(table, head):
    lane = lax.broadcasted_iota(jnp.int32, table.shape, 1)
    return jnp.sum(jnp.where(lane == head, table, 0.0), axis=1, keepdims=True)


def reset_row(first, base, count):
    inside = (first > base) & (first < base + count)
    return pl.multiple_of(jnp.where(inside, first - base, 0), GROUP)


def reset_places(first, base, reset):
    token = base + reset + lax.broadcasted_iota(jnp.int32, (RIM, 1), 0)
    return token - jnp.where(token >= first, first, 0)


def conv_total(ext, total, weight, reset, places):
    count, taps = total.shape[0], weight.shape[0]
    lead = RIM - taps + 1
    whole = ext[lead : lead + count, :] * weight[0:1, :]
    for tap in range(1, taps):
        whole = whole + ext[lead + tap : lead + tap + count, :] * weight[tap : tap + 1, :]
    total[...] = whole
    near = ext[pl.ds(reset, 2 * RIM), :]
    fixed = near[RIM : 2 * RIM] * weight[taps - 1 : taps, :]
    for tap in range(taps - 1):
        rows = jnp.where(places >= taps - 1 - tap, near[lead + tap : lead + tap + RIM], 0.0)
        fixed = fixed + rows * weight[tap : tap + 1, :]
    total[pl.ds(reset, RIM), :] = fixed


def load_ext(ext, rim, body):
    ext[0:RIM, :] = rim
    ext[RIM : RIM + body.shape[0], :] = body


def load_features(taps, j, refs, ext, total, reset, places):
    q_ref, k_ref, v_ref, q_rim, k_rim, v_rim, conv_q, conv_k, conv_v = refs
    cols = slice(j * DK, (j + 1) * DK)
    sources = [(q_ref, q_rim, conv_q, cols), (k_ref, k_rim, conv_k, cols)]
    for half in range(DV // DK):
        begin = j * DV + half * DK
        sources.append((v_ref, v_rim, conv_v, slice(begin, begin + DK)))
    for piece, (body, rim, weight, cut) in enumerate(sources):
        load_ext(ext.at[j, piece], rim[:, cut], body[:, cut])
        conv_total(ext.at[j, piece], total.at[j, piece], weight[:, cut], reset, places)


def block_ends(g):
    return jnp.concatenate(
        [
            jnp.broadcast_to(g[GROUP - 1 : GROUP], (GROUP, DK)),
            jnp.broadcast_to(g[PAIR - 1 : PAIR], (GROUP, DK)),
        ],
        axis=0,
    )


def decay_tables(decay_ref, beta_ref, log_ref, bias_ref, cum_ref, rate_ref):
    count = decay_ref.shape[0]
    shifted_in = decay_ref[...] + bias_ref[...]
    soft = jnp.maximum(shifted_in, 0.0) + jnp.log1p(jnp.exp(-jnp.abs(shifted_in)))
    log_decay = -jnp.exp(log_ref[...]) * soft
    _, _, within, _ = grid_masks()
    ones = jnp.where(within, 1.0, 0.0)
    for pair in range(count // PAIR):
        rows = slice(pair * PAIR, (pair + 1) * PAIR)
        cum_ref[rows, :] = lax.dot_general(
            ones,
            log_decay[rows, :],
            (((1,), (0,)), ((), ())),
            precision=lax.Precision.HIGHEST,
            preferred_element_type=jnp.float32,
        )
    rate_ref[...] = jax.nn.sigmoid(beta_ref[...])


def state_kernel(
    taps,
    per_step,
    spot,
    q_ref,
    k_ref,
    v_ref,
    q_rim,
    k_rim,
    v_rim,
    conv_q,
    conv_k,
    conv_v,
    decay_ref,
    beta_ref,
    log_ref,
    bias_ref,
    mixed_ref,
    reach_ref,
    map_ref,
    add_ref,
    inverse_ref,
    pass_ref,
    turn_ref,
    gain_ref,
    cum_ref,
    rate_ref,
    ext,
    total,
    cum,
    lower,
    halfway,
    score,
    grown_q,
    grown_k,
    scaled_v,
    tail,
    states,
    starts,
):
    step = pl.program_id(0)
    count = q_ref.shape[0]
    pairs = count // PAIR
    blocks = count // GROUP
    first, base = spot[0], spot[1]
    reset = reset_row(first, base, count)
    places = reset_places(first, base, reset)

    @pl.when(step == 0)
    def _():
        decay_tables(decay_ref, beta_ref, log_ref, bias_ref, cum_ref, rate_ref)

    row, col, within, below = grid_masks()
    refs = (q_ref, k_ref, v_ref, q_rim, k_rim, v_rim, conv_q, conv_k, conv_v)
    for j in range(per_step):
        load_features(taps, j, refs, ext, total, reset, places)
        head = step * per_step + j
        cum[j] = jnp.broadcast_to(column(cum_ref[...], head), (count, DK))
        halfway[j] = jnp.broadcast_to(column(rate_ref[...], head), (count, DK))

    def local(pair, carry):
        at = pl.ds(pl.multiple_of(pair * PAIR, PAIR), PAIR)
        for j in range(per_step):
            g = cum[j, at, :]
            b = halfway[j, at, :]
            u = total[j, 0, at, :]
            c = u * sigmoid(u)
            q = c * (unit_scale(c) * DK**-0.5)
            u = total[j, 1, at, :]
            c = u * sigmoid(u)
            k = c * unit_scale(c)
            k_low = low(k)
            spread = jnp.where(within, jnp.exp(jnp.where(within, g - g.T, 0.0)), 0.0)
            keys = mm_nt(k_low, k_low)
            lower[j, at, :] = low(jnp.where(below, b * keys * spread, 0.0))
            score[j, at, :] = low(mm_nt(low(q), k_low) * spread)
            grown = jnp.exp(g)
            for half in range(DV // DK):
                u = total[j, 2 + half, at, :]
                scaled_v[j, at, half * DK : (half + 1) * DK] = low(b * (u * sigmoid(u)))
            grown_k[j, at, :] = low(b * grown * k)
            tail[j, at, :] = low(jnp.exp(block_ends(g) - g) * k)
            grown_q[j, at, :] = grown * q
        return carry

    lax.fori_loop(0, pairs, local, 0, unroll=2)

    masks = masks_low(row, col)
    spots = [
        (j, slice(pair * PAIR, (pair + 1) * PAIR))
        for pair in range(pairs)
        for j in range(per_step)
    ]
    eye = low(jnp.where(row == col, 1.0, 0.0))
    for j, at in spots:
        inverse_ref[j, at, :] = eye - lower[j, at, :] * masks[0]
    for mask in masks[1:]:
        for j, at in spots:
            halfway[j, at, :] = mm(lower[j, at, :] * mask, inverse_ref[j, at, :])
        for j, at in spots:
            inverse = inverse_ref[j, at, :]
            inverse_ref[j, at, :] = inverse - low(mm(inverse, low(halfway[j, at, :])))

    def combine(pair, carry):
        at = pl.ds(pl.multiple_of(pair * PAIR, PAIR), PAIR)
        for j in range(per_step):
            cols = slice(j * DK, (j + 1) * DK)
            wide = slice(j * DV, (j + 1) * DV)
            inverse = inverse_ref[j, at, :]
            scored = score[j, at, :]
            u_low = low(mm(inverse, scaled_v[j, at, :]))
            w_low = low(mm(inverse, grown_k[j, at, :]))
            mixed_ref[at, wide] = mm(scored, u_low)
            pass_ref[at, cols] = low(grown_q[j, at, :] - mm(scored, w_low))
            falls = tail[j, at, :]
            for half in range(2):
                part = slice(half * GROUP, (half + 1) * GROUP)
                turn_ref[j, 2 * pair + half] = low(mm_tn(falls[part], w_low[part]))
                gain_ref[j, 2 * pair + half] = low(mm_tn(falls[part], u_low[part]))
        return carry

    lax.fori_loop(0, pairs, combine, 0, unroll=2)

    for j in range(per_step):
        states[j] = jnp.concatenate(
            [jnp.where(row == col, 1.0, 0.0), jnp.zeros((DK, DV), jnp.float32)], axis=1
        )

    def advance(block, carry):
        begin = base + block * GROUP
        keep = jnp.where((begin != 0) & (begin != first), 1.0, 0.0)
        for j in range(per_step):
            state = states[j] * keep
            state_low = low(state)
            starts[j, block] = state_low
            last = jnp.exp(cum[j, pl.ds(block * GROUP + GROUP - 1, 1), :])
            last = jnp.concatenate([last] * 3, axis=1)
            moved = last * state - mm(turn_ref[j, block], state_low)
            states[j, :, :DK] = moved[:, :DK]
            states[j, :, DK:] = moved[:, DK:] + high(gain_ref[j, block])
        return carry

    lax.fori_loop(0, blocks, advance, 0, unroll=2)

    def close(block, carry):
        at = pl.ds(pl.multiple_of(block * GROUP, GROUP), GROUP)
        for j in range(per_step):
            cols = slice(j * DK, (j + 1) * DK)
            wide = slice(j * DV, (j + 1) * DV)
            out = mm(pass_ref[at, cols], starts[j, block])
            reach_ref[at, cols] = low(out[:, :DK])
            mixed_ref[at, wide] = mixed_ref[at, wide] + out[:, DK:]
        return carry

    lax.fori_loop(0, blocks, close, 0, unroll=4)
    for j in range(per_step):
        map_ref[j] = low(states[j, :, :DK])
        add_ref[j] = low(states[j, :, DK:])


def spec(shape, index):
    return pl.BlockSpec(shape, index)


def state_forward(q, k, v, rims, convs, decay, beta, decay_log, decay_bias, spot, per_step):
    count = q.shape[0]
    heads = decay.shape[1]
    taps = convs[0].shape[0]
    n = per_step
    blocks = count // GROUP
    along = lambda i: (0, i)
    fixed = lambda i: (0, 0)
    lead = lambda i: (i, 0, 0)
    lead4 = lambda i: (i, 0, 0, 0)
    f32, bf16 = jnp.float32, jnp.bfloat16
    shape = jax.ShapeDtypeStruct
    vm = pltpu.VMEM
    return pl.pallas_call(
        functools.partial(state_kernel, taps, n),
        grid=(heads // n,),
        in_specs=[
            pl.BlockSpec(memory_space=pltpu.SMEM),
            spec((count, n * DK), along),
            spec((count, n * DK), along),
            spec((count, n * DV), along),
            spec((RIM, n * DK), along),
            spec((RIM, n * DK), along),
            spec((RIM, n * DV), along),
            spec((taps, n * DK), along),
            spec((taps, n * DK), along),
            spec((taps, n * DV), along),
            spec((count, heads), fixed),
            spec((count, heads), fixed),
            spec((1, heads), fixed),
            spec((1, heads), fixed),
        ],
        out_specs=[
            spec((count, n * DV), along),
            spec((count, n * DK), along),
            spec((n, DK, DK), lead),
            spec((n, DK, DV), lead),
            spec((n, count, PAIR), lead),
            spec((count, n * DK), along),
            spec((n, blocks, DK, DK), lead4),
            spec((n, blocks, DK, DV), lead4),
            spec((count, heads), fixed),
            spec((count, heads), fixed),
        ],
        out_shape=[
            shape((count, heads * DV), f32),
            shape((count, heads * DK), bf16),
            shape((heads, DK, DK), bf16),
            shape((heads, DK, DV), bf16),
            shape((heads, count, PAIR), bf16),
            shape((count, heads * DK), bf16),
            shape((heads, blocks, DK, DK), bf16),
            shape((heads, blocks, DK, DV), bf16),
            shape((count, heads), f32),
            shape((count, heads), f32),
        ],
        scratch_shapes=[
            vm((n, 4, count + RIM, DK), f32),
            vm((n, 4, count, DK), f32),
            vm((n, count, DK), f32),
            vm((n, count, PAIR), bf16),
            vm((n, count, PAIR), f32),
            vm((n, count, PAIR), bf16),
            vm((n, count, DK), f32),
            vm((n, count, DK), bf16),
            vm((n, count, DV), bf16),
            vm((n, count, DK), bf16),
            vm((n, DK, DK + DV), f32),
            vm((n, blocks, DK, DK + DV), bf16),
        ],
        compiler_params=pltpu.CompilerParams(
            dimension_semantics=("arbitrary",), vmem_limit_bytes=VMEM_BYTES
        ),
        cost_estimate=LITTLE,
    )(spot, q, k, v, *rims, *convs, decay, beta, decay_log, decay_bias)


def silu(value):
    return value * sigmoid(value)


def gate_kernel(per_step, mixed_ref, reach_ref, map_ref, add_ref, far_ref, gate_ref, gain_ref, gated_ref, kept_ref, start_ref):
    for j in range(per_step):
        cols = slice(j * DK, (j + 1) * DK)
        wide = slice(j * DV, (j + 1) * DV)
        start = low(high(add_ref[j]) + mm(map_ref[j], far_ref[j]))
        start_ref[j] = start
        mixed = mixed_ref[:, wide] + mm(reach_ref[:, cols], start)
        kept_ref[:, wide] = low(mixed)
        scale = lax.rsqrt(jnp.mean(mixed * mixed, axis=-1, keepdims=True) + EPS)
        gated_ref[:, wide] = low(mixed * scale * gain_ref[...] * silu(gate_ref[:, wide]))


def gate_forward(mixed, reach, near_map, near_add, far_add, gate, gain, per_step):
    count = mixed.shape[0]
    heads = near_map.shape[0]
    n = per_step
    along = lambda i: (0, i)
    lead = lambda i: (i, 0, 0)
    bf16 = jnp.bfloat16
    return pl.pallas_call(
        functools.partial(gate_kernel, n),
        grid=(heads // n,),
        in_specs=[
            spec((count, n * DV), along),
            spec((count, n * DK), along),
            spec((n, DK, DK), lead),
            spec((n, DK, DV), lead),
            spec((n, DK, DV), lead),
            spec((count, n * DV), along),
            spec((1, DV), lambda i: (0, 0)),
        ],
        out_specs=[
            spec((count, n * DV), along),
            spec((count, n * DV), along),
            spec((n, DK, DV), lead),
        ],
        out_shape=[
            jax.ShapeDtypeStruct((count, heads * DV), bf16),
            jax.ShapeDtypeStruct((count, heads * DV), bf16),
            jax.ShapeDtypeStruct((heads, DK, DV), bf16),
        ],
        compiler_params=pltpu.CompilerParams(
            dimension_semantics=("arbitrary",), vmem_limit_bytes=VMEM_BYTES
        ),
        cost_estimate=LITTLE,
    )(mixed, reach, near_map, near_add, far_add, gate, gain)


def gate_back_kernel(per_step, d_gated_ref, kept_ref, reach_ref, gate_ref, gain_ref, d_mixed_ref, d_gate_ref, d_start_ref, d_gain_ref):
    @pl.when(pl.program_id(0) == 0)
    def _():
        d_gain_ref[...] = jnp.zeros_like(d_gain_ref)

    for j in range(per_step):
        cols = slice(j * DK, (j + 1) * DK)
        wide = slice(j * DV, (j + 1) * DV)
        mixed = high(kept_ref[:, wide])
        scale = lax.rsqrt(jnp.mean(mixed * mixed, axis=-1, keepdims=True) + EPS)
        normal = mixed * scale
        gate = gate_ref[:, wide]
        sig = sigmoid(gate)
        d_gated = d_gated_ref[:, wide]
        d_scaled = d_gated * (gate * sig)
        d_gain_ref[...] += jnp.sum(d_scaled * normal, axis=0, keepdims=True)
        d_gate_ref[:, wide] = low(
            d_gated * (normal * gain_ref[...]) * (sig * (1.0 + gate * (1.0 - sig)))
        )
        d_normal = d_scaled * gain_ref[...]
        d_mixed = low(scale * (d_normal - normal * jnp.mean(d_normal * normal, axis=-1, keepdims=True)))
        d_mixed_ref[:, wide] = d_mixed
        d_start_ref[j] = low(mm_tn(reach_ref[:, cols], d_mixed))


def gate_backward(d_gated, kept, reach, gate, gain, per_step):
    count = kept.shape[0]
    heads = kept.shape[1] // DV
    n = per_step
    along = lambda i: (0, i)
    lead = lambda i: (i, 0, 0)
    bf16 = jnp.bfloat16
    return pl.pallas_call(
        functools.partial(gate_back_kernel, n),
        grid=(heads // n,),
        in_specs=[
            spec((count, n * DV), along),
            spec((count, n * DV), along),
            spec((count, n * DK), along),
            spec((count, n * DV), along),
            spec((1, DV), lambda i: (0, 0)),
        ],
        out_specs=[
            spec((count, n * DV), along),
            spec((count, n * DV), along),
            spec((n, DK, DV), lead),
            spec((1, DV), lambda i: (0, 0)),
        ],
        out_shape=[
            jax.ShapeDtypeStruct((count, heads * DV), bf16),
            jax.ShapeDtypeStruct((count, heads * DV), bf16),
            jax.ShapeDtypeStruct((heads, DK, DV), bf16),
            jax.ShapeDtypeStruct((1, DV), jnp.float32),
        ],
        compiler_params=pltpu.CompilerParams(
            dimension_semantics=("arbitrary",), vmem_limit_bytes=VMEM_BYTES
        ),
        cost_estimate=LITTLE,
    )(d_gated, kept, reach, gate, gain)


def state_back_kernel(
    taps,
    per_step,
    offset,
    extra,
    spot,
    q_ref,
    k_ref,
    v_ref,
    q_rim,
    k_rim,
    v_rim,
    conv_q,
    conv_k,
    conv_v,
    decay_ref,
    log_ref,
    bias_ref,
    cum_ref,
    rate_ref,
    inverse_ref,
    pass_ref,
    turn_ref,
    gain_ref,
    start_ref,
    d_mixed_ref,
    near_ref,
    map_ref,
    far_ref,
    *rest,
):
    (
        dq_ref,
        dk_ref,
        dv_ref,
        dq_rim,
        dk_rim,
        dv_rim,
        dq_end,
        dk_end,
        dv_end,
        d_conv_q,
        d_conv_k,
        d_conv_v,
        d_decay_ref,
        d_beta_ref,
        d_log_ref,
        d_bias_ref,
        ext,
        total,
        query,
        key,
        d_value,
        cum,
        rate,
        starts,
        ends,
        states,
        d_states,
        d_total,
        d_ext,
        d_cum,
        d_rate,
    ) = rest[extra:]
    step = pl.program_id(0)
    count = q_ref.shape[0]
    pairs = count // PAIR
    blocks = count // GROUP
    first, base = spot[0], spot[1]
    reset = reset_row(first, base, count)
    places = reset_places(first, base, reset)

    @pl.when(step == 0)
    def _():
        d_cum[...] = jnp.zeros_like(d_cum)
        d_rate[...] = jnp.zeros_like(d_rate)

    refs = (q_ref, k_ref, v_ref, q_rim, k_rim, v_rim, conv_q, conv_k, conv_v)
    for j in range(per_step):
        load_features(taps, j, refs, ext, total, reset, places)
        head = offset + step * per_step + j
        cum[j] = jnp.broadcast_to(column(cum_ref[...], head), (count, DK))
        rate[j] = jnp.broadcast_to(column(rate_ref[...], head), (count, DK))
        u = total[j, 0]
        c = u * sigmoid(u)
        query[j] = c * (unit_scale(c) * DK**-0.5)
        u = total[j, 1]
        c = u * sigmoid(u)
        key[j] = c * unit_scale(c)
        states[j] = high(start_ref[j])
        d_states[j] = high(near_ref[j]) + mm_tn(map_ref[j], far_ref[j])

    row, col, within, below = grid_masks()

    def keep_of(block):
        begin = base + block * GROUP
        return jnp.where((begin != 0) & (begin != first), 1.0, 0.0)

    def last_of(j, block):
        last = jnp.exp(cum[j, pl.ds(block * GROUP + GROUP - 1, 1), :])
        return jnp.concatenate([last, last], axis=1)

    def chain(block, carry):
        back = blocks - 1 - block
        at = pl.ds(pl.multiple_of(back * GROUP, GROUP), GROUP)
        for j in range(per_step):
            state = states[j] * keep_of(block)
            state_low = low(state)
            starts[j, block] = state_low
            states[j] = (
                last_of(j, block) * state
                - mm(turn_ref[j, block], state_low)
                + high(gain_ref[j, block])
            )
            d_state = d_states[j]
            d_low = low(d_state)
            ends[j, back] = d_low
            d_out = d_mixed_ref[at, j * DV : (j + 1) * DV]
            d_states[j] = keep_of(back) * (
                last_of(j, back) * d_state
                - mm_tn(turn_ref[j, back], d_low)
                + mm_tn(pass_ref[at, j * DK : (j + 1) * DK], d_out)
            )
        return carry

    lax.fori_loop(0, blocks, chain, 0, unroll=2)

    lane = lax.broadcasted_iota(jnp.int32, (PAIR, d_cum.shape[1]), 1)
    tall = lax.broadcasted_iota(jnp.int32, (PAIR, 1), 0)

    def assemble(pair, carry):
        at = pl.ds(pl.multiple_of(pair * PAIR, PAIR), PAIR)
        halves = [slice(half * GROUP, (half + 1) * GROUP) for half in range(2)]
        for j in range(per_step):
            g = cum[j, at, :]
            b = rate[j, at, :]
            k = key[j, at, :]
            q = query[j, at, :]
            v = []
            for half in range(DV // DK):
                u = total[j, 2 + half, at, :]
                v.append(u * sigmoid(u))
            v = jnp.concatenate(v, axis=1)
            bb = jnp.concatenate([b, b], axis=1)
            k_low, q_low = low(k), low(q)
            inverse = inverse_ref[j, at, :]
            spread = jnp.where(within, jnp.exp(jnp.where(within, g - g.T, 0.0)), 0.0)
            grown = jnp.exp(g)
            fall = jnp.exp(block_ends(g) - g)
            scores = mm_nt(q_low, k_low)
            d_out = d_mixed_ref[at, j * DV : (j + 1) * DV]
            grown_k = low(b * grown * k)
            falls = low(fall * k)
            begin = [starts[j, 2 * pair + half] for half in range(2)]
            end = [ends[j, 2 * pair + half] for half in range(2)]
            known = jnp.concatenate(
                [mm(grown_k[part], begin[half]) for half, part in enumerate(halves)], axis=0
            )
            change = low(mm(inverse, low(bb * v - known)))
            pulled = jnp.concatenate(
                [mm(falls[part], end[half]) for half, part in enumerate(halves)], axis=0
            )
            rhs = mm_tn(inverse, low(mm_tn(low(scores * spread), d_out) + pulled))
            rhs_low = low(rhs)
            d_lower = jnp.where(below, -mm_nt(rhs_low, change), 0.0)
            d_score = mm_nt(d_out, change) * spread
            d_gk = jnp.concatenate(
                [-mm_nt(rhs_low[part], begin[half]) for half, part in enumerate(halves)], axis=0
            )
            d_gq = jnp.concatenate(
                [mm_nt(d_out[part], begin[half]) for half, part in enumerate(halves)], axis=0
            )
            d_tail = jnp.concatenate(
                [mm_nt(change[part], end[half]) for half, part in enumerate(halves)], axis=0
            )
            bonus = [jnp.sum(high(begin[half]) * high(end[half])) for half in range(2)]
            d_a = d_lower * mm_nt(k_low, k_low) * spread
            cross = d_a * b + d_score * scores
            gk_k = d_gk * k
            rate_col = jnp.sum(d_a + grown * gk_k, axis=-1, keepdims=True) + jnp.sum(
                rhs * v, axis=-1, keepdims=True
            )
            tail_sum = jnp.sum(d_tail * (fall * k), axis=-1, keepdims=True)
            cum_col = (
                jnp.sum(
                    cross - cross.T + b * grown * gk_k + d_gq * (grown * q), axis=-1, keepdims=True
                )
                - tail_sum
            )
            for half, part in enumerate(halves):
                at_end = half * GROUP + GROUP - 1
                more = jnp.sum(tail_sum[part], axis=0, keepdims=True) + bonus[half] * grown[
                    at_end : at_end + 1, :1
                ]
                cum_col = cum_col + jnp.where(tall == at_end, more, 0.0)
            head = offset + step * per_step + j
            d_cum[at, :] = d_cum[at, :] + jnp.where(lane == head, cum_col, 0.0)
            d_rate[at, :] = d_rate[at, :] + jnp.where(lane == head, rate_col, 0.0)
            d_keys = d_lower * spread * b
            d_keys = low(d_keys + d_keys.T)
            d_score_low = low(d_score)
            d_query = grown * d_gq + mm(d_score_low, k_low)
            d_key = b * grown * d_gk + fall * d_tail + mm(d_keys, k_low) + mm_tn(d_score_low, q_low)
            query[j, at, :] = d_query
            key[j, at, :] = d_key
            d_value[j, at, :] = bb * rhs
        return carry

    lax.fori_loop(0, pairs, assemble, 0, unroll=2)

    d_total[0:RIM, :] = jnp.zeros((RIM, DK), jnp.float32)
    d_total[RIM + count : 2 * RIM + count, :] = jnp.zeros((RIM, DK), jnp.float32)

    def conv_back(rows, weight, out_ref, rim_ref, end_ref, d_weight_ref, cols):
        size = count + RIM
        spread_rows = None
        grads = []
        for tap in range(taps):
            moved = d_total[taps - 1 - tap : taps - 1 - tap + size, :]
            term = moved * weight[tap : tap + 1, :]
            spread_rows = term if spread_rows is None else spread_rows + term
            grads.append(jnp.sum(moved * rows[...], axis=0, keepdims=True))
        d_ext[...] = spread_rows
        near = d_total[pl.ds(reset + RIM, RIM), :]
        around = rows[pl.ds(reset, 2 * RIM), :]
        wrong_rows = jnp.zeros((2 * RIM, DK), jnp.float32)
        for tap in range(taps - 1):
            lead = RIM - taps + 1 + tap
            wrong = jnp.where(places >= taps - 1 - tap, 0.0, near)
            grads[tap] = grads[tap] - jnp.sum(
                wrong * around[lead : lead + RIM], axis=0, keepdims=True
            )
            wrong_rows = wrong_rows + jnp.concatenate(
                [
                    jnp.zeros((lead, DK), jnp.float32),
                    wrong * weight[tap : tap + 1, :],
                    jnp.zeros((RIM - lead, DK), jnp.float32),
                ],
                axis=0,
            )
        d_ext[pl.ds(reset, 2 * RIM), :] = d_ext[pl.ds(reset, 2 * RIM), :] - wrong_rows
        d_weight_ref[:, cols] = jnp.concatenate(grads, axis=0)
        rim_ref[:, cols] = d_ext[0:RIM, :]
        out_ref[:, cols] = low(d_ext[RIM : RIM + count, :])
        end_ref[:, cols] = d_ext[count : count + RIM, :]

    for j in range(per_step):
        cols = slice(j * DK, (j + 1) * DK)

        def unit_back(piece, d_unit, factor):
            u = total[j, piece]
            sig = sigmoid(u)
            c = u * sig
            scale = unit_scale(c)
            unit = c * scale
            d_unit = d_unit * factor
            d_c = scale * (d_unit - unit * jnp.sum(d_unit * unit, axis=-1, keepdims=True))
            d_total[RIM : RIM + count, :] = d_c * (sig * (1.0 + u * (1.0 - sig)))

        unit_back(0, query[j], DK**-0.5)
        conv_back(ext.at[j, 0], conv_q[:, cols], dq_ref, dq_rim, dq_end, d_conv_q, cols)
        unit_back(1, key[j], 1.0)
        conv_back(ext.at[j, 1], conv_k[:, cols], dk_ref, dk_rim, dk_end, d_conv_k, cols)
        for half in range(DV // DK):
            begin = j * DV + half * DK
            cut = slice(begin, begin + DK)
            u = total[j, 2 + half]
            sig = sigmoid(u)
            d_total[RIM : RIM + count, :] = d_value[j, :, half * DK : (half + 1) * DK] * (
                sig * (1.0 + u * (1.0 - sig))
            )
            conv_back(ext.at[j, 2 + half], conv_v[:, cut], dv_ref, dv_rim, dv_end, d_conv_v, cut)

    @pl.when(step == pl.num_programs(0) - 1)
    def _():
        shifted_in = decay_ref[...] + bias_ref[...]
        soft = jnp.maximum(shifted_in, 0.0) + jnp.log1p(jnp.exp(-jnp.abs(shifted_in)))
        speed = -jnp.exp(log_ref[...])
        after = jnp.where(within, 1.0, 0.0)
        d_log = jnp.zeros_like(d_log_ref)
        d_bias = jnp.zeros_like(d_bias_ref)
        for pair in range(pairs):
            rows = slice(pair * PAIR, (pair + 1) * PAIR)
            d_decay = lax.dot_general(
                after,
                d_cum[rows, :],
                (((0,), (0,)), ((), ())),
                precision=lax.Precision.HIGHEST,
                preferred_element_type=jnp.float32,
            )
            d_log = d_log + jnp.sum(d_decay * (speed * soft[rows]), axis=0, keepdims=True)
            d_in = d_decay * speed * jax.nn.sigmoid(shifted_in[rows])
            d_bias = d_bias + jnp.sum(d_in, axis=0, keepdims=True)
            d_decay_ref[rows, :] = d_in
        d_log_ref[...] = d_log
        d_bias_ref[...] = d_bias
        rates = rate_ref[...]
        d_beta_ref[...] = d_rate[...] * rates * (1.0 - rates)


def state_backward(
    q, k, v, rims, convs, decay, decay_log, decay_bias, cum, rate, saved, start, d_mixed, near, near_map, far, spot, per_step, offset, held, after
):
    count = q.shape[0]
    heads = decay.shape[1]
    taps = convs[0].shape[0]
    n = per_step
    blocks = count // GROUP
    skip = offset // n
    along = lambda i: (0, i + skip)
    fixed = lambda i: (0, 0)
    lead = lambda i: (i + skip, 0, 0)
    lead4 = lambda i: (i + skip, 0, 0, 0)
    out_along = lambda i: (0, i)
    f32, bf16 = jnp.float32, jnp.bfloat16
    shape = jax.ShapeDtypeStruct
    vm = pltpu.VMEM
    thin = [(RIM, DK), (RIM, DK), (RIM, DV)]
    out_blocks = [(count, DK), (count, DK), (count, DV)] + thin + thin
    out_blocks += [(taps, DK), (taps, DK), (taps, DV)]
    tables = [(count, heads), (count, heads), (1, heads), (1, heads)]
    return pl.pallas_call(
        functools.partial(state_back_kernel, taps, n, offset, len(after)),
        grid=(held // n,),
        in_specs=[
            pl.BlockSpec(memory_space=pltpu.SMEM),
            spec((count, n * DK), along),
            spec((count, n * DK), along),
            spec((count, n * DV), along),
            spec((RIM, n * DK), along),
            spec((RIM, n * DK), along),
            spec((RIM, n * DV), along),
            spec((taps, n * DK), along),
            spec((taps, n * DK), along),
            spec((taps, n * DV), along),
            spec((count, heads), fixed),
            spec((1, heads), fixed),
            spec((1, heads), fixed),
            spec((count, heads), fixed),
            spec((count, heads), fixed),
            spec((n, count, PAIR), lead),
            spec((count, n * DK), along),
            spec((n, blocks, DK, DK), lead4),
            spec((n, blocks, DK, DV), lead4),
            spec((n, DK, DV), lead),
            spec((count, n * DV), along),
            spec((n, DK, DV), lead),
            spec((n, DK, DK), lead),
            spec((n, DK, DV), lead),
        ]
        + [pl.BlockSpec(memory_space=pl.ANY) for _ in after],
        out_specs=[spec((rows, n * width), out_along) for rows, width in out_blocks]
        + [spec(block, fixed) for block in tables],
        out_shape=[
            shape((rows, held * width), bf16 if i < 3 else f32)
            for i, (rows, width) in enumerate(out_blocks)
        ]
        + [shape(block, f32) for block in tables],
        scratch_shapes=[
            vm((n, 4, count + RIM, DK), f32),
            vm((n, 4, count, DK), f32),
            vm((n, count, DK), f32),
            vm((n, count, DK), f32),
            vm((n, count, DV), f32),
            vm((n, count, DK), f32),
            vm((n, count, DK), f32),
            vm((n, blocks, DK, DV), bf16),
            vm((n, blocks, DK, DV), bf16),
            vm((n, DK, DV), f32),
            vm((n, DK, DV), f32),
            vm((count + 2 * RIM, DK), f32),
            vm((count + RIM, DK), f32),
            vm((count, heads), f32),
            vm((count, heads), f32),
        ],
        compiler_params=pltpu.CompilerParams(
            dimension_semantics=("arbitrary",), vmem_limit_bytes=VMEM_BYTES
        ),
        cost_estimate=LITTLE,
    )(
        spot,
        q,
        k,
        v,
        *rims,
        *convs,
        decay,
        decay_log,
        decay_bias,
        cum,
        rate,
        *saved,
        start,
        d_mixed,
        near,
        near_map,
        far,
        *after,
    )


def shifted(value, axis, steps):
    count = lax.axis_size(axis)
    leading, last = (max(0, -steps), min(count, count - steps))
    return lax.ppermute(value, axis, [(source, source + steps) for source in range(leading, last)])


def rms_scale(values, gain):
    return values * lax.rsqrt(jnp.mean(values * values, axis=-1, keepdims=True) + EPS) * gain


def swish_product(gate_ffn, up_ffn):
    return jax.nn.silu(gate_ffn) * up_ffn


def project(rows, weight):
    return jnp.dot(rows, weight, preferred_element_type=jnp.float32)


def rows_product(left, right):
    return jnp.dot(left, right, preferred_element_type=jnp.float32)


def rows_back(left, weight):
    return jnp.einsum("tc,dc->td", left, weight, preferred_element_type=jnp.float32)


def weight_grad(rows, grads):
    return jnp.einsum("td,tc->dc", rows, grads, preferred_element_type=jnp.float32)


STAGES = {"x": ("seq", 0, 1), "y": ("seq", 1, 2), "l": ("dp", 0, 4), "h": ("dp", 1, 8)}


def trade(value, stage):
    axis, bit, _ = STAGES[stage]
    count = lax.axis_size(axis)
    return lax.ppermute(value, axis, [(place, place ^ (1 << bit)) for place in range(count)])


def arrange_kernel(per_head, picks, full_ref, mine_ref, other_ref, *rest):
    out_ref = rest[-1]
    width = full_ref.shape[1] // 16
    mine = (pl.program_id(0) // per_head) == picks[16]
    for place in range(16):
        source = pl.ds(pl.multiple_of(picks[place] * width, width), width)
        target = slice(place * width, (place + 1) * width)
        out_ref[0, :, target] = full_ref[:, source]
        out_ref[1, :, target] = jnp.where(mine, mine_ref[:, source], other_ref[:, source])


def paired_rows(full, got, order, *after):
    order = order[1:] + order[:1]
    own = lax.axis_index("dp") * lax.axis_size("seq") + lax.axis_index("seq")
    masks = [
        sum(STAGES[stage][2] for k, stage in enumerate(order) if place >> (3 - k) & 1)
        for place in range(16)
    ]
    picks = jnp.concatenate(
        [own ^ jnp.array(masks, jnp.int32), lax.axis_index("heads").astype(jnp.int32)[None]]
    )
    if lax.axis_size("heads") == 2:
        other = lax.ppermute(got, "heads", [(0, 1), (1, 0)])
    else:
        got = other = heads_gather(got)
    count, width = full.shape
    size = 96
    blocks = got.shape[0] // size
    piece = pl.BlockSpec((size, width), lambda i: (i, 0))
    part = pl.BlockSpec((size, width), lambda i: (lax.rem(i, blocks), 0))
    both = pl.pallas_call(
        functools.partial(arrange_kernel, blocks),
        grid=(count // size,),
        in_specs=[pl.BlockSpec(memory_space=pltpu.SMEM), piece, part, part]
        + [pl.BlockSpec(memory_space=pl.ANY) for _ in after],
        out_specs=pl.BlockSpec((2, size, width), lambda i: (0, i, 0)),
        out_shape=jax.ShapeDtypeStruct((2, count, width), full.dtype),
        compiler_params=pltpu.CompilerParams(
            dimension_semantics=("arbitrary",), vmem_limit_bytes=VMEM_BYTES
        ),
        cost_estimate=LITTLE,
    )(picks, full, got, other, *after)
    return both.reshape(-1, width)


def own_side(stage):
    axis, bit, _ = STAGES[stage]
    return lax.rem(lax.axis_index(axis) // (1 << bit), 2)


def pick_half(grads, order, which):
    half = grads.shape[1] // 2
    side = own_side(order[0])
    return lax.dynamic_slice_in_dim(grads, (side if which else 1 - side) * half, half, 1)


def join_halves(grads, got, order):
    return jnp.concatenate([pick_half(grads, order, 1), got], axis=0)


def trade_halves(grads, order):
    return join_halves(grads, trade(pick_half(grads, order, 0), order[0]), order)


def pair_grad(rows, grads, begin, end):
    width = rows.shape[1] // 16
    return weight_grad(rows[:, begin * width : end * width], grads)


def grad_open(rows, grads, order):
    sent = low(pair_grad(rows, grads, 8, 16))
    return rows, grads, sent, trade(sent, order[1])


def grad_next(opened, order):
    rows, grads, _, first = opened
    middle = first.shape[0] // 2
    sent = low(pair_grad(rows, grads, 4, 8) + high(first[middle:]))
    rest = pair_grad(rows, grads, 0, 4) + high(first[:middle])
    return rest, sent, trade(sent, order[2])


def grad_last(moved):
    rest, _, second = moved
    return low(rest + high(second))


def finish_kernel(plan, head_steps, *refs):
    groups = len(plan)
    grads, small_ref = refs[:groups], refs[groups]
    outs, small_out = refs[groups + 1 : 2 * groups + 1], refs[2 * groups + 1]
    scratch = refs[2 * groups + 2 :]
    buffers = []
    for stages, _ in plan:
        buffers.append(scratch[: len(stages)])
        scratch = scratch[len(stages) :]
    small_sum, small_got, send_sem, recv_sem, small_send, small_recv = scratch

    def side(stage):
        axis, bit, _ = STAGES[stage]
        return lax.rem(lax.axis_index(axis) // (1 << bit), 2)

    def partner(stage):
        axis, bit, _ = STAGES[stage]
        return {axis: lax.axis_index(axis) + (1 - 2 * side(stage)) * (1 << bit)}

    def head_partner(step):
        me = lax.axis_index("heads")
        return {"heads": me + (1 - 2 * lax.rem(me // step, 2)) * step}

    barrier = pltpu.get_barrier_semaphore()
    targets = [partner(stage) for stage in "xylh"] + [head_partner(step) for step in head_steps]
    for target in targets:
        pl.semaphore_signal(
            barrier, inc=1, device_id=target, device_id_type=pl.DeviceIdType.MESH
        )
    pl.semaphore_wait(barrier, len(targets))

    started = []

    def send(source, target, sems, device):
        copy = pltpu.make_async_remote_copy(
            src_ref=source,
            dst_ref=target,
            send_sem=sems[0],
            recv_sem=sems[1],
            device_id=device,
            device_id_type=pl.DeviceIdType.MESH,
        )
        copy.start()
        started.append(copy)
        return copy

    most = max(len(cuts) for _, cuts in plan)
    longest = max(len(stages) for stages, _ in plan)
    chunks, number = [], 0
    rounds = [[] for _ in range(most)]
    for g, (stages, cuts) in enumerate(plan):
        for k, cut in enumerate(cuts):
            chunks.append((g, stages, slice(*cut)))
            rounds[k].append(number)
            number += 1
    copies = {}

    def advance(index, step):
        g, stages, cut = chunks[index]
        if step > len(stages):
            return
        if step > 0:
            copies[index, step - 1].wait_recv()
        full = grads[g].shape[0]
        here = buffers[g]
        if step == len(stages):
            there = 1 - side(stages[-1])
            outs[g][pl.ds(there, 1), :, cut] = here[-1][:, cut][None]
            return
        rows = slice(full >> (step + 1), full >> step)
        if step == 0:
            source = grads[g].at[rows, cut]
            if len(stages) == 1:
                outs[g][pl.ds(side(stages[0]), 1), :, cut] = grads[g][: rows.start, cut][None]
        else:
            last = step == len(stages) - 1
            begin = 0 if last else rows.start
            value = high(grads[g][begin : rows.stop, cut])
            for got in here[:step]:
                value = value + high(got[begin : rows.stop, cut])
            if last:
                outs[g][pl.ds(side(stages[-1]), 1), :, cut] = low(value[: rows.start])[None]
                value = value[rows.start :]
            here[0][rows, cut] = low(value)
            source = here[0].at[rows, cut]
        place = 4 * index + step
        copies[index, step] = send(
            source,
            here[step].at[:, cut],
            (send_sem.at[place], recv_sem.at[place]),
            partner(stages[step]),
        )

    small_copies = []
    names = "xylh"

    def small_step(step):
        if step >= 1 and step <= 4:
            small_copies[step - 1].wait_recv()
            small_sum[step] = small_sum[step - 1] + small_got[step - 1]
        if step == 4:
            small_out[pl.ds(lax.axis_index("heads"), 1)] = small_sum[4:5]
        if step < 4:
            if step == 0:
                small_sum[0] = small_ref[...]
            sems = (small_send.at[step], small_recv.at[step])
            small_copies.append(
                send(small_sum.at[step], small_got.at[step], sems, partner(names[step]))
            )
        elif step - 4 <= len(head_steps):
            k = step - 4
            if k >= 1:
                small_copies[step - 1].wait_recv()
            if k < len(head_steps):
                size = head_steps[k]
                begin = lax.axis_index("heads") // size * size
                block = small_out.at[pl.ds(begin, size)]
                sems = (small_send.at[step], small_recv.at[step])
                small_copies.append(send(block, block, sems, head_partner(size)))

    total_small = 5 + len(head_steps)
    small_step(0)
    for ahead in range(min(2, most)):
        for index in rounds[ahead]:
            advance(index, 0)
    for t in range(max(most + longest, total_small - 1)):
        for lag in range(longest):
            if lag == 1 and t + 2 < most:
                for index in rounds[t + 2]:
                    advance(index, 0)
            if 0 <= t - lag < most:
                for index in rounds[t - lag]:
                    advance(index, lag + 1)
        if t + 1 < total_small:
            small_step(t + 1)
    for copy in started:
        copy.wait_send()


def finish(grads, orders, small):
    count = lax.axis_size("heads")
    head_steps = []
    while 1 << len(head_steps) < count:
        head_steps.append(1 << len(head_steps))
    plan, scratch, outs = [], [], []
    for array, order in zip(grads, orders):
        full, half = array.shape
        step = min(256 if len(order) == 4 else 512, half) if half % 128 == 0 else half
        cuts = [(at, min(at + step, half)) for at in range(0, half, step)]
        plan.append((order[1:] + order[:1], cuts))
        for level in range(len(order)):
            scratch.append(pltpu.VMEM((full >> (level + 1), half), jnp.bfloat16))
        outs.append(jax.ShapeDtypeStruct((2, full >> len(order), half), jnp.bfloat16))
    pieces = sum(len(cuts) for _, cuts in plan)
    inside = pl.BlockSpec(memory_space=pltpu.VMEM)
    f32 = jnp.float32
    return pl.pallas_call(
        functools.partial(finish_kernel, tuple(plan), tuple(head_steps)),
        in_specs=[inside] * (len(grads) + 1),
        out_specs=[inside] * (len(grads) + 1),
        out_shape=outs + [jax.ShapeDtypeStruct((count,) + small.shape, f32)],
        scratch_shapes=scratch
        + [
            pltpu.VMEM((5,) + small.shape, f32),
            pltpu.VMEM((4,) + small.shape, f32),
            pltpu.SemaphoreType.DMA((4 * pieces,)),
            pltpu.SemaphoreType.DMA((4 * pieces,)),
            pltpu.SemaphoreType.DMA((8,)),
            pltpu.SemaphoreType.DMA((8,)),
        ],
        compiler_params=pltpu.CompilerParams(
            collective_id=0, has_side_effects=True, vmem_limit_bytes=60 * 1024 * 1024
        ),
        cost_estimate=LITTLE,
    )(*grads, small)


def fence(one, *after):
    return pl.pallas_call(
        lambda one_ref, *rest: rest[-1].__setitem__(..., one_ref[...]),
        in_specs=[pl.BlockSpec(memory_space=pltpu.VMEM)]
        + [pl.BlockSpec(memory_space=pl.ANY) for _ in after],
        out_specs=pl.BlockSpec(memory_space=pltpu.VMEM),
        out_shape=jax.ShapeDtypeStruct(one.shape, one.dtype),
        compiler_params=pltpu.CompilerParams(vmem_limit_bytes=VMEM_BYTES),
        cost_estimate=LITTLE,
    )(one, *after)


def order_kernel(*refs):
    pass


def ordered(values, *after):
    anywhere = pl.BlockSpec(memory_space=pl.ANY)
    return pl.pallas_call(
        order_kernel,
        in_specs=[anywhere] * (len(values) + len(after)),
        out_specs=[anywhere] * len(values),
        out_shape=[jax.ShapeDtypeStruct(part.shape, part.dtype) for part in values],
        input_output_aliases={k: k for k in range(len(values))},
        cost_estimate=LITTLE,
    )(*values, *after)


def heads_gather(rows, axis=0):
    count = lax.axis_size("heads")
    own = lax.axis_index("heads")
    step = 1
    while step < count:
        other = lax.ppermute(rows, "heads", [(place, place ^ step) for place in range(count)])
        upper = lax.rem(own // step, 2) == 1
        rows = jnp.concatenate(
            [jnp.where(upper, other, rows), jnp.where(upper, rows, other)], axis=axis
        )
        step *= 2
    return rows


def heads_sum(compute, count, kind):
    if lax.axis_size("heads") != 2:
        whole = compute(lambda rows: rows).astype(kind)
        return high(lax.psum_scatter(whole, "heads", scatter_dimension=0, tiled=True))
    own = lax.axis_index("heads")
    half = count // 2

    def part(which):
        return compute(lambda rows: lax.dynamic_slice_in_dim(rows, which * half, half, 0))

    got = lax.ppermute(part(1 - own).astype(kind), "heads", [(0, 1), (1, 0)])
    return part(own) + high(got)


ORDERS = ("xylh", "yxlh", "lxyh")
FFN_ORDERS = ("xlyh", "yxlh", "lyhx")


def body(
    hidden_in,
    out_cotangent,
    lengths,
    norm_gain,
    q_weight,
    k_weight,
    v_weight,
    gate_weight,
    decay_weight,
    beta_weight,
    conv_q,
    conv_k,
    conv_v,
    decay_log,
    decay_bias,
    out_gain,
    out_weight,
    ffn_gain,
    ffn_gate,
    ffn_up,
    ffn_down,
):
    resid = hidden_in[0].astype(jnp.float32)
    normed_own = rms_scale(resid, norm_gain).astype(jnp.bfloat16)
    normed, cotangent = (
        heads_gather(normed_own),
        heads_gather(out_cotangent[0]),
    )
    span = normed.shape[0]
    normed_got = {order: trade(normed_own, order[0]) for order in ORDERS[:2]}
    cotangent_got = trade(out_cotangent[0], FFN_ORDERS[2][0])
    taps = conv_q.shape[0]
    q_proj = project(normed, q_weight)
    k_proj = project(normed, k_weight)
    v_proj = project(normed, v_weight)
    gate_proj = project(normed, gate_weight)
    heads = decay_weight.shape[1]
    per_step = min(2, heads)
    narrow = project(normed, jnp.concatenate([decay_weight, beta_weight], axis=1))
    decay_proj, beta_proj = narrow[:, :heads], narrow[:, heads:]
    seq_index = lax.axis_index("seq")
    spot = jnp.stack([lengths[0, 0], seq_index * span]).astype(jnp.int32)
    rims = shifted((q_proj[span - RIM :], k_proj[span - RIM :], v_proj[span - RIM :]), "seq", 1)
    convs = (conv_q, conv_k, conv_v)
    log_row, bias_row, gain_row = decay_log[None], decay_bias[None], out_gain[None]
    mixed_local, reach, span_map, span_add, *saved, cum, rate = state_forward(
        q_proj, k_proj, v_proj, rims, convs, decay_proj, beta_proj, log_row, bias_row, spot, per_step
    )
    span_map, span_add = ordered((span_map, span_add), cotangent_got, *normed_got.values())
    near_map, near_add = shifted((span_map, span_add), "seq", 1)
    far_add = shifted(span_add, "seq", 2)
    next_map = shifted(span_map, "seq", -1)
    (mixed_local,) = ordered((mixed_local,), next_map)
    gated_low, mixed_low, start_state = gate_forward(
        mixed_local, reach, near_map, near_add, far_add, gate_proj, gain_row, per_step
    )
    mixer = heads_sum(
        lambda pick: rows_product(pick(gated_low), out_weight), span, jnp.bfloat16
    )
    resid_mid = resid + mixer
    ffn_own = rms_scale(resid_mid, ffn_gain).astype(jnp.bfloat16)
    ffn_in = heads_gather(ffn_own)
    ffn_got = {order: trade(ffn_own, order[0]) for order in FFN_ORDERS[:2]}
    gate_ffn = project(ffn_in, ffn_gate)
    up_ffn = project(ffn_in, ffn_up)
    act, act_pull = jax.vjp(swish_product, gate_ffn, up_ffn)
    act_low = act.astype(jnp.bfloat16)
    d_act = jnp.einsum("td,fd->tf", cotangent, ffn_down, preferred_element_type=jnp.float32)
    d_gate_ffn, d_up_ffn = act_pull(d_act)
    d_gate_low = d_gate_ffn.astype(jnp.bfloat16)
    d_up_low = d_up_ffn.astype(jnp.bfloat16)
    ffn_low = (d_gate_low, d_up_low, act_low)
    theirs = [pick_half(part, order, 0) for part, order in zip(ffn_low, FFN_ORDERS)]
    ffn_traded = [trade(part, order[0]) for part, order in zip(theirs, FFN_ORDERS)]
    ffn_low = ordered(ffn_low, *ffn_got.values(), *theirs)
    d_gate_low, d_up_low, act_low = ffn_low
    gate_halves, up_halves, down_halves = (
        join_halves(part, got, order)
        for part, got, order in zip(ffn_low, ffn_traded, FFN_ORDERS)
    )
    ffn_out = heads_sum(lambda pick: rows_product(pick(act_low), ffn_down), span, jnp.bfloat16)
    output = (resid_mid + ffn_out).astype(jnp.bfloat16)
    cotangent_rel = paired_rows(cotangent, cotangent_got, FFN_ORDERS[2], act_low)
    ffn_rel = [
        paired_rows(ffn_in, ffn_got[order], order, d_gate_low) for order in FFN_ORDERS[:2]
    ]
    gate_open = grad_open(ffn_rel[0], gate_halves, FFN_ORDERS[0])
    up_open = grad_open(ffn_rel[1], up_halves, FFN_ORDERS[1])
    down_open = grad_open(cotangent_rel, down_halves, FFN_ORDERS[2])
    d_ffn = heads_sum(
        lambda pick: rows_back(pick(d_gate_low), ffn_gate) + rows_back(pick(d_up_low), ffn_up),
        span,
        jnp.bfloat16,
    )
    _, ffn_norm_pull = jax.vjp(rms_scale, resid_mid, ffn_gain)
    d_mid_norm, d_ffn_gain = ffn_norm_pull(d_ffn)
    d_mid = out_cotangent[0].astype(jnp.float32) + d_mid_norm
    d_mid_low = low(d_mid)
    d_mid_all = heads_gather(d_mid_low)
    d_mid_got = trade(d_mid_low, ORDERS[2][0])
    d_gated = jnp.einsum("td,cd->tc", d_mid_all, out_weight, preferred_element_type=jnp.float32)
    d_mixed, d_gate_low_mix, d_start, d_out_gain = gate_backward(
        d_gated, mixed_low, reach, gate_proj, gain_row, per_step
    )
    next_start = shifted(d_start, "seq", -1)
    beyond_start = shifted(d_start, "seq", -2)
    mix_halves = trade_halves(d_gate_low_mix, ORDERS[0])
    (gated_low,) = ordered((gated_low,), d_gate_low_mix)
    out_halves = trade_halves(gated_low, ORDERS[2])
    normed_rel = [
        paired_rows(normed, normed_got[order], order, up_open[2]) for order in ORDERS[:2]
    ]
    d_mid_rel = paired_rows(d_mid_all, d_mid_got, ORDERS[2], up_open[2])
    moved = [
        grad_next(opened, order)
        for opened, order in zip((gate_open, up_open, down_open), FFN_ORDERS)
    ]
    back = state_backward(
        q_proj,
        k_proj,
        v_proj,
        rims,
        convs,
        decay_proj,
        log_row,
        bias_row,
        cum,
        rate,
        saved,
        start_state,
        d_mixed,
        next_start,
        next_map,
        beyond_start,
        spot,
        per_step,
        0,
        heads,
        [part[1] for part in moved] + [d_mid_rel, *normed_rel],
    )
    rim = jnp.concatenate(back[3:6], axis=1)
    (rim,) = ordered((rim,), *(part[2] for part in moved))
    rim = shifted(rim, "seq", -1)
    passed = jnp.split(rim, (heads * DK, 2 * heads * DK), axis=1)
    d_q_low, d_k_low, d_v_low = (
        lax.dynamic_update_slice_in_dim(whole, low(end + more), span - RIM, 0)
        for whole, end, more in zip(back[0:3], back[6:9], passed)
    )
    d_decay_low, d_beta_low = low(back[12]), low(back[13])
    flat_lows = (jnp.concatenate([d_q_low, d_k_low], axis=1), d_v_low)
    late = [pick_half(part, order, 0) for part, order in zip(flat_lows, ORDERS)]
    late_got = [trade(part, order[0]) for part, order in zip(late, ORDERS)]
    d_gate_low_mix, d_mid_rel, *normed_rel = ordered(
        (d_gate_low_mix, d_mid_rel, *normed_rel), *late
    )
    tails = [
        grad_last(moved[0]),
        grad_last(moved[1]),
        grad_last(moved[2]),
        low(pair_grad(normed_rel[0], mix_halves, 0, 16)),
        low(pair_grad(d_mid_rel, out_halves, 0, 16)),
    ]
    tail_orders = [order[:1] + order[3:] for order in FFN_ORDERS] + [ORDERS[0], ORDERS[2]]
    for flat_low, got, rows, order in zip(flat_lows, late_got, normed_rel, ORDERS):
        tails.append(low(pair_grad(rows, join_halves(flat_low, got, order), 0, 16)))
        tail_orders.append(order)
    narrow_grad = weight_grad(jnp.concatenate([d_decay_low, d_beta_low], axis=1), normed)
    pairs = (
        (d_q_low, q_weight),
        (d_k_low, k_weight),
        (d_v_low, v_weight),
        (d_gate_low_mix, gate_weight),
        (d_decay_low, decay_weight),
        (d_beta_low, beta_weight),
    )
    d_normed = heads_sum(
        lambda pick: sum(rows_back(pick(rows), weight) for rows, weight in pairs),
        span,
        jnp.bfloat16,
    )
    _, in_norm_pull = jax.vjp(rms_scale, resid, norm_gain)
    d_in_norm, d_norm_gain = in_norm_pull(d_normed)
    input_grad = d_mid + d_in_norm
    wide = normed.shape[1]
    conv_all = jnp.concatenate(back[9:12], axis=1)

    def full_rows(part):
        return jnp.pad(part, ((0, 0), (0, wide - part.shape[1])))

    conv_rows = [full_rows(conv_all[:, at : at + wide]) for at in range(0, conv_all.shape[1], wide)]
    last_row = full_rows(jnp.concatenate([d_out_gain, back[14], back[15]], axis=1))
    stacked = [narrow_grad] + conv_rows + [d_norm_gain[None], d_ffn_gain[None], last_row]
    flat = jnp.concatenate(stacked, axis=0)
    flat = jnp.pad(flat, ((0, -flat.shape[0] % 8), (0, 0)))
    *sums, everyone = finish(tails, tail_orders, flat)
    grad_gate, grad_up, grad_down, grad_gate_mix, grad_out, grad_qk, grad_v = (
        high(jnp.concatenate([part[0], part[1]], axis=1)) for part in sums
    )
    grad_down, grad_out = grad_down.T, grad_out.T
    grad_q, grad_k = jnp.split(grad_qk, 2, axis=1)
    shard = lax.axis_index("dp") * lax.axis_size("seq") + lax.axis_index("seq")
    size = wide // 16
    narrow_sum = lax.dynamic_slice(
        everyone, (lax.axis_index("heads"), 0, shard * size), (1, 2 * heads, size)
    )[0].T
    grad_decay, grad_beta = narrow_sum[:, :heads], narrow_sum[:, heads:]
    at = 2 * heads
    conv_sum = jnp.concatenate(
        [everyone[:, at + taps * k : at + taps * (k + 1)] for k in range(len(conv_rows))], axis=2
    )
    at += taps * len(conv_rows)
    width_k = heads * DK

    def by_head(part):
        return jnp.swapaxes(part, 0, 1).reshape(part.shape[1], -1)

    width_v = out_gain.shape[0]
    small = [
        everyone[:, at].sum(0),
        everyone[:, at + 1].sum(0),
        everyone[:, at + 2, :width_v].sum(0),
        everyone[:, at + 2, width_v : width_v + heads].reshape(-1),
        everyone[:, at + 2, width_v + heads : width_v + 2 * heads].reshape(-1),
        by_head(conv_sum[:, :, :width_k]),
        by_head(conv_sum[:, :, width_k : 2 * width_k]),
        by_head(conv_sum[:, :, 2 * width_k : 2 * width_k + heads * DV]),
    ]
    return (
        output[None],
        input_grad[None],
        small[0],
        grad_q,
        grad_k,
        grad_v,
        grad_gate_mix,
        grad_decay,
        grad_beta,
        small[5],
        small[6],
        small[7],
        small[3],
        small[4],
        small[2],
        grad_out,
        small[1],
        grad_gate,
        grad_up,
        grad_down,
    )


def solution(mesh):
    in_specs = (
        P("dp", ("seq", "heads"), None),
        P("dp", ("seq", "heads"), None),
        P("dp", None),
        P(),
        P(None, "heads"),
        P(None, "heads"),
        P(None, "heads"),
        P(None, "heads"),
        P(None, "heads"),
        P(None, "heads"),
        P(None, "heads"),
        P(None, "heads"),
        P(None, "heads"),
        P("heads"),
        P("heads"),
        P(),
        P("heads", None),
        P(),
        P(None, "heads"),
        P(None, "heads"),
        P("heads", None),
    )
    out_specs = (
        P("dp", ("seq", "heads"), None),
        P("dp", ("seq", "heads"), None),
        P(),
        P(("dp", "seq"), "heads"),
        P(("dp", "seq"), "heads"),
        P(("dp", "seq"), "heads"),
        P(("dp", "seq"), "heads"),
        P(("dp", "seq"), "heads"),
        P(("dp", "seq"), "heads"),
        P(),
        P(),
        P(),
        P(),
        P(),
        P(),
        P("heads", ("dp", "seq")),
        P(),
        P(("dp", "seq"), "heads"),
        P(("dp", "seq"), "heads"),
        P("heads", ("dp", "seq")),
    )
    return jax.shard_map(body, mesh=mesh, in_specs=in_specs, out_specs=out_specs, check_vma=False)
```

```python
import functools

import jax
import jax.numpy as jnp
from jax import lax
from jax.experimental import pallas as pl
from jax.experimental.pallas import tpu as pltpu
from jax.sharding import PartitionSpec as P

HEADS = 16
DK = 128
DV = 256
GROUP = 64
EPS = 1e-06
PAIR = 2 * GROUP
RIM = 8
VMEM_BYTES = 56 * 1024 * 1024
LITTLE = pl.CostEstimate(flops=0, bytes_accessed=0, transcendentals=0)


def mm(left, right):
    return lax.dot_general(
        left, right, (((1,), (0,)), ((), ())), preferred_element_type=jnp.float32
    )


def mm_nt(left, right):
    return lax.dot_general(
        left, right, (((1,), (1,)), ((), ())), preferred_element_type=jnp.float32
    )


def mm_tn(left, right):
    return lax.dot_general(
        left, right, (((0,), (0,)), ((), ())), preferred_element_type=jnp.float32
    )


def low(value):
    return value.astype(jnp.bfloat16)


def high(value):
    return value.astype(jnp.float32)


def grid_masks():
    row = lax.broadcasted_iota(jnp.int32, (PAIR, PAIR), 0)
    col = lax.broadcasted_iota(jnp.int32, (PAIR, PAIR), 1)
    same = (row // GROUP) == (col // GROUP)
    return row, col, same & (row >= col), same & (row > col)


def masks_low(row, col):
    sizes, masks = [], []
    size = 1
    while size < GROUP:
        here = ((row // (2 * size)) == (col // (2 * size))) & ((row // size) > (col // size))
        masks.append(low(jnp.where(here, 1.0, 0.0)))
        sizes.append(size)
        size *= 2
    return masks


def sigmoid(value):
    return 0.5 * jnp.tanh(0.5 * value) + 0.5


def unit_scale(value):
    return lax.rsqrt(jnp.sum(value * value, axis=-1, keepdims=True) + EPS)


def column(table, head):
    lane = lax.broadcasted_iota(jnp.int32, table.shape, 1)
    return jnp.sum(jnp.where(lane == head, table, 0.0), axis=1, keepdims=True)


def reset_row(first, base, count):
    inside = (first > base) & (first < base + count)
    return pl.multiple_of(jnp.where(inside, first - base, 0), GROUP)


def reset_places(first, base, reset):
    token = base + reset + lax.broadcasted_iota(jnp.int32, (RIM, 1), 0)
    return token - jnp.where(token >= first, first, 0)


def conv_total(ext, total, weight, reset, places):
    count, taps = total.shape[0], weight.shape[0]
    lead = RIM - taps + 1
    whole = ext[lead : lead + count, :] * weight[0:1, :]
    for tap in range(1, taps):
        whole = whole + ext[lead + tap : lead + tap + count, :] * weight[tap : tap + 1, :]
    total[...] = whole
    near = ext[pl.ds(reset, 2 * RIM), :]
    fixed = near[RIM : 2 * RIM] * weight[taps - 1 : taps, :]
    for tap in range(taps - 1):
        rows = jnp.where(places >= taps - 1 - tap, near[lead + tap : lead + tap + RIM], 0.0)
        fixed = fixed + rows * weight[tap : tap + 1, :]
    total[pl.ds(reset, RIM), :] = fixed


def load_ext(ext, rim, body):
    ext[0:RIM, :] = rim
    ext[RIM : RIM + body.shape[0], :] = body


def load_features(taps, j, refs, ext, total, reset, places):
    q_ref, k_ref, v_ref, q_rim, k_rim, v_rim, conv_q, conv_k, conv_v = refs
    cols = slice(j * DK, (j + 1) * DK)
    sources = [(q_ref, q_rim, conv_q, cols), (k_ref, k_rim, conv_k, cols)]
    for half in range(DV // DK):
        begin = j * DV + half * DK
        sources.append((v_ref, v_rim, conv_v, slice(begin, begin + DK)))
    for piece, (body, rim, weight, cut) in enumerate(sources):
        load_ext(ext.at[j, piece], rim[:, cut], body[:, cut])
        conv_total(ext.at[j, piece], total.at[j, piece], weight[:, cut], reset, places)


def block_ends(g):
    return jnp.concatenate(
        [
            jnp.broadcast_to(g[GROUP - 1 : GROUP], (GROUP, DK)),
            jnp.broadcast_to(g[PAIR - 1 : PAIR], (GROUP, DK)),
        ],
        axis=0,
    )


def decay_tables(decay_ref, beta_ref, log_ref, bias_ref, cum_ref, rate_ref):
    count = decay_ref.shape[0]
    shifted_in = decay_ref[...] + bias_ref[...]
    soft = jnp.maximum(shifted_in, 0.0) + jnp.log1p(jnp.exp(-jnp.abs(shifted_in)))
    log_decay = -jnp.exp(log_ref[...]) * soft
    _, _, within, _ = grid_masks()
    ones = jnp.where(within, 1.0, 0.0)
    for pair in range(count // PAIR):
        rows = slice(pair * PAIR, (pair + 1) * PAIR)
        cum_ref[rows, :] = lax.dot_general(
            ones,
            log_decay[rows, :],
            (((1,), (0,)), ((), ())),
            precision=lax.Precision.HIGHEST,
            preferred_element_type=jnp.float32,
        )
    rate_ref[...] = jax.nn.sigmoid(beta_ref[...])


def state_kernel(
    taps,
    per_step,
    spot,
    q_ref,
    k_ref,
    v_ref,
    q_rim,
    k_rim,
    v_rim,
    conv_q,
    conv_k,
    conv_v,
    decay_ref,
    beta_ref,
    log_ref,
    bias_ref,
    mixed_ref,
    reach_ref,
    map_ref,
    add_ref,
    inverse_ref,
    pass_ref,
    turn_ref,
    gain_ref,
    cum_ref,
    rate_ref,
    ext,
    total,
    cum,
    lower,
    halfway,
    score,
    grown_q,
    grown_k,
    scaled_v,
    tail,
    states,
    starts,
):
    step = pl.program_id(0)
    count = q_ref.shape[0]
    pairs = count // PAIR
    blocks = count // GROUP
    first, base = spot[0], spot[1]
    reset = reset_row(first, base, count)
    places = reset_places(first, base, reset)

    @pl.when(step == 0)
    def _():
        decay_tables(decay_ref, beta_ref, log_ref, bias_ref, cum_ref, rate_ref)

    row, col, within, below = grid_masks()
    refs = (q_ref, k_ref, v_ref, q_rim, k_rim, v_rim, conv_q, conv_k, conv_v)
    for j in range(per_step):
        load_features(taps, j, refs, ext, total, reset, places)
        head = step * per_step + j
        cum[j] = jnp.broadcast_to(column(cum_ref[...], head), (count, DK))
        halfway[j] = jnp.broadcast_to(column(rate_ref[...], head), (count, DK))

    def local(pair, carry):
        at = pl.ds(pl.multiple_of(pair * PAIR, PAIR), PAIR)
        for j in range(per_step):
            g = cum[j, at, :]
            b = halfway[j, at, :]
            u = total[j, 0, at, :]
            c = u * sigmoid(u)
            q = c * (unit_scale(c) * DK**-0.5)
            u = total[j, 1, at, :]
            c = u * sigmoid(u)
            k = c * unit_scale(c)
            k_low = low(k)
            spread = jnp.where(within, jnp.exp(jnp.where(within, g - g.T, 0.0)), 0.0)
            keys = mm_nt(k_low, k_low)
            lower[j, at, :] = low(jnp.where(below, b * keys * spread, 0.0))
            score[j, at, :] = low(mm_nt(low(q), k_low) * spread)
            grown = jnp.exp(g)
            for half in range(DV // DK):
                u = total[j, 2 + half, at, :]
                scaled_v[j, at, half * DK : (half + 1) * DK] = low(b * (u * sigmoid(u)))
            grown_k[j, at, :] = low(b * grown * k)
            tail[j, at, :] = low(jnp.exp(block_ends(g) - g) * k)
            grown_q[j, at, :] = grown * q
        return carry

    lax.fori_loop(0, pairs, local, 0, unroll=2)

    masks = masks_low(row, col)
    spots = [
        (j, slice(pair * PAIR, (pair + 1) * PAIR))
        for pair in range(pairs)
        for j in range(per_step)
    ]
    eye = low(jnp.where(row == col, 1.0, 0.0))
    for j, at in spots:
        inverse_ref[j, at, :] = eye - lower[j, at, :] * masks[0]
    for mask in masks[1:]:
        for j, at in spots:
            halfway[j, at, :] = mm(lower[j, at, :] * mask, inverse_ref[j, at, :])
        for j, at in spots:
            inverse = inverse_ref[j, at, :]
            inverse_ref[j, at, :] = inverse - low(mm(inverse, low(halfway[j, at, :])))

    def combine(pair, carry):
        at = pl.ds(pl.multiple_of(pair * PAIR, PAIR), PAIR)
        for j in range(per_step):
            cols = slice(j * DK, (j + 1) * DK)
            wide = slice(j * DV, (j + 1) * DV)
            inverse = inverse_ref[j, at, :]
            scored = score[j, at, :]
            u_low = low(mm(inverse, scaled_v[j, at, :]))
            w_low = low(mm(inverse, grown_k[j, at, :]))
            mixed_ref[at, wide] = mm(scored, u_low)
            pass_ref[at, cols] = low(grown_q[j, at, :] - mm(scored, w_low))
            falls = tail[j, at, :]
            for half in range(2):
                part = slice(half * GROUP, (half + 1) * GROUP)
                turn_ref[j, 2 * pair + half] = low(mm_tn(falls[part], w_low[part]))
                gain_ref[j, 2 * pair + half] = low(mm_tn(falls[part], u_low[part]))
        return carry

    lax.fori_loop(0, pairs, combine, 0, unroll=2)

    for j in range(per_step):
        states[j] = jnp.concatenate(
            [jnp.where(row == col, 1.0, 0.0), jnp.zeros((DK, DV), jnp.float32)], axis=1
        )

    def advance(block, carry):
        begin = base + block * GROUP
        keep = jnp.where((begin != 0) & (begin != first), 1.0, 0.0)
        for j in range(per_step):
            state = states[j] * keep
            state_low = low(state)
            starts[j, block] = state_low
            last = jnp.exp(cum[j, pl.ds(block * GROUP + GROUP - 1, 1), :])
            last = jnp.concatenate([last] * 3, axis=1)
            moved = last * state - mm(turn_ref[j, block], state_low)
            states[j, :, :DK] = moved[:, :DK]
            states[j, :, DK:] = moved[:, DK:] + high(gain_ref[j, block])
        return carry

    lax.fori_loop(0, blocks, advance, 0, unroll=2)

    def close(block, carry):
        at = pl.ds(pl.multiple_of(block * GROUP, GROUP), GROUP)
        for j in range(per_step):
            cols = slice(j * DK, (j + 1) * DK)
            wide = slice(j * DV, (j + 1) * DV)
            out = mm(pass_ref[at, cols], starts[j, block])
            reach_ref[at, cols] = low(out[:, :DK])
            mixed_ref[at, wide] = mixed_ref[at, wide] + out[:, DK:]
        return carry

    lax.fori_loop(0, blocks, close, 0, unroll=4)
    for j in range(per_step):
        map_ref[j] = low(states[j, :, :DK])
        add_ref[j] = low(states[j, :, DK:])


def spec(shape, index):
    return pl.BlockSpec(shape, index)


def state_forward(q, k, v, rims, convs, decay, beta, decay_log, decay_bias, spot, per_step):
    count = q.shape[0]
    heads = decay.shape[1]
    taps = convs[0].shape[0]
    n = per_step
    blocks = count // GROUP
    along = lambda i: (0, i)
    fixed = lambda i: (0, 0)
    lead = lambda i: (i, 0, 0)
    lead4 = lambda i: (i, 0, 0, 0)
    f32, bf16 = jnp.float32, jnp.bfloat16
    shape = jax.ShapeDtypeStruct
    vm = pltpu.VMEM
    return pl.pallas_call(
        functools.partial(state_kernel, taps, n),
        grid=(heads // n,),
        in_specs=[
            pl.BlockSpec(memory_space=pltpu.SMEM),
            spec((count, n * DK), along),
            spec((count, n * DK), along),
            spec((count, n * DV), along),
            spec((RIM, n * DK), along),
            spec((RIM, n * DK), along),
            spec((RIM, n * DV), along),
            spec((taps, n * DK), along),
            spec((taps, n * DK), along),
            spec((taps, n * DV), along),
            spec((count, heads), fixed),
            spec((count, heads), fixed),
            spec((1, heads), fixed),
            spec((1, heads), fixed),
        ],
        out_specs=[
            spec((count, n * DV), along),
            spec((count, n * DK), along),
            spec((n, DK, DK), lead),
            spec((n, DK, DV), lead),
            spec((n, count, PAIR), lead),
            spec((count, n * DK), along),
            spec((n, blocks, DK, DK), lead4),
            spec((n, blocks, DK, DV), lead4),
            spec((count, heads), fixed),
            spec((count, heads), fixed),
        ],
        out_shape=[
            shape((count, heads * DV), f32),
            shape((count, heads * DK), bf16),
            shape((heads, DK, DK), bf16),
            shape((heads, DK, DV), bf16),
            shape((heads, count, PAIR), bf16),
            shape((count, heads * DK), bf16),
            shape((heads, blocks, DK, DK), bf16),
            shape((heads, blocks, DK, DV), bf16),
            shape((count, heads), f32),
            shape((count, heads), f32),
        ],
        scratch_shapes=[
            vm((n, 4, count + RIM, DK), f32),
            vm((n, 4, count, DK), f32),
            vm((n, count, DK), f32),
            vm((n, count, PAIR), bf16),
            vm((n, count, PAIR), f32),
            vm((n, count, PAIR), bf16),
            vm((n, count, DK), f32),
            vm((n, count, DK), bf16),
            vm((n, count, DV), bf16),
            vm((n, count, DK), bf16),
            vm((n, DK, DK + DV), f32),
            vm((n, blocks, DK, DK + DV), bf16),
        ],
        compiler_params=pltpu.CompilerParams(
            dimension_semantics=("arbitrary",), vmem_limit_bytes=VMEM_BYTES
        ),
        cost_estimate=LITTLE,
    )(spot, q, k, v, *rims, *convs, decay, beta, decay_log, decay_bias)


def silu(value):
    return value * sigmoid(value)


def gate_kernel(per_step, mixed_ref, reach_ref, map_ref, add_ref, far_ref, gate_ref, gain_ref, gated_ref, kept_ref, start_ref):
    for j in range(per_step):
        cols = slice(j * DK, (j + 1) * DK)
        wide = slice(j * DV, (j + 1) * DV)
        start = low(high(add_ref[j]) + mm(map_ref[j], far_ref[j]))
        start_ref[j] = start
        mixed = mixed_ref[:, wide] + mm(reach_ref[:, cols], start)
        kept_ref[:, wide] = low(mixed)
        scale = lax.rsqrt(jnp.mean(mixed * mixed, axis=-1, keepdims=True) + EPS)
        gated_ref[:, wide] = low(mixed * scale * gain_ref[...] * silu(gate_ref[:, wide]))


def gate_forward(mixed, reach, near_map, near_add, far_add, gate, gain, per_step):
    count = mixed.shape[0]
    heads = near_map.shape[0]
    n = per_step
    along = lambda i: (0, i)
    lead = lambda i: (i, 0, 0)
    bf16 = jnp.bfloat16
    return pl.pallas_call(
        functools.partial(gate_kernel, n),
        grid=(heads // n,),
        in_specs=[
            spec((count, n * DV), along),
            spec((count, n * DK), along),
            spec((n, DK, DK), lead),
            spec((n, DK, DV), lead),
            spec((n, DK, DV), lead),
            spec((count, n * DV), along),
            spec((1, DV), lambda i: (0, 0)),
        ],
        out_specs=[
            spec((count, n * DV), along),
            spec((count, n * DV), along),
            spec((n, DK, DV), lead),
        ],
        out_shape=[
            jax.ShapeDtypeStruct((count, heads * DV), bf16),
            jax.ShapeDtypeStruct((count, heads * DV), bf16),
            jax.ShapeDtypeStruct((heads, DK, DV), bf16),
        ],
        compiler_params=pltpu.CompilerParams(
            dimension_semantics=("arbitrary",), vmem_limit_bytes=VMEM_BYTES
        ),
        cost_estimate=LITTLE,
    )(mixed, reach, near_map, near_add, far_add, gate, gain)


def gate_back_kernel(per_step, d_gated_ref, kept_ref, reach_ref, gate_ref, gain_ref, d_mixed_ref, d_gate_ref, d_start_ref, d_gain_ref):
    @pl.when(pl.program_id(0) == 0)
    def _():
        d_gain_ref[...] = jnp.zeros_like(d_gain_ref)

    for j in range(per_step):
        cols = slice(j * DK, (j + 1) * DK)
        wide = slice(j * DV, (j + 1) * DV)
        mixed = high(kept_ref[:, wide])
        scale = lax.rsqrt(jnp.mean(mixed * mixed, axis=-1, keepdims=True) + EPS)
        normal = mixed * scale
        gate = gate_ref[:, wide]
        sig = sigmoid(gate)
        d_gated = d_gated_ref[:, wide]
        d_scaled = d_gated * (gate * sig)
        d_gain_ref[...] += jnp.sum(d_scaled * normal, axis=0, keepdims=True)
        d_gate_ref[:, wide] = low(
            d_gated * (normal * gain_ref[...]) * (sig * (1.0 + gate * (1.0 - sig)))
        )
        d_normal = d_scaled * gain_ref[...]
        d_mixed = low(scale * (d_normal - normal * jnp.mean(d_normal * normal, axis=-1, keepdims=True)))
        d_mixed_ref[:, wide] = d_mixed
        d_start_ref[j] = low(mm_tn(reach_ref[:, cols], d_mixed))


def gate_backward(d_gated, kept, reach, gate, gain, per_step):
    count = kept.shape[0]
    heads = kept.shape[1] // DV
    n = per_step
    along = lambda i: (0, i)
    lead = lambda i: (i, 0, 0)
    bf16 = jnp.bfloat16
    return pl.pallas_call(
        functools.partial(gate_back_kernel, n),
        grid=(heads // n,),
        in_specs=[
            spec((count, n * DV), along),
            spec((count, n * DV), along),
            spec((count, n * DK), along),
            spec((count, n * DV), along),
            spec((1, DV), lambda i: (0, 0)),
        ],
        out_specs=[
            spec((count, n * DV), along),
            spec((count, n * DV), along),
            spec((n, DK, DV), lead),
            spec((1, DV), lambda i: (0, 0)),
        ],
        out_shape=[
            jax.ShapeDtypeStruct((count, heads * DV), bf16),
            jax.ShapeDtypeStruct((count, heads * DV), bf16),
            jax.ShapeDtypeStruct((heads, DK, DV), bf16),
            jax.ShapeDtypeStruct((1, DV), jnp.float32),
        ],
        compiler_params=pltpu.CompilerParams(
            dimension_semantics=("arbitrary",), vmem_limit_bytes=VMEM_BYTES
        ),
        cost_estimate=LITTLE,
    )(d_gated, kept, reach, gate, gain)


def state_back_kernel(
    taps,
    per_step,
    offset,
    extra,
    spot,
    q_ref,
    k_ref,
    v_ref,
    q_rim,
    k_rim,
    v_rim,
    conv_q,
    conv_k,
    conv_v,
    decay_ref,
    log_ref,
    bias_ref,
    cum_ref,
    rate_ref,
    inverse_ref,
    pass_ref,
    turn_ref,
    gain_ref,
    start_ref,
    d_mixed_ref,
    near_ref,
    map_ref,
    far_ref,
    *rest,
):
    (
        dq_ref,
        dk_ref,
        dv_ref,
        dq_rim,
        dk_rim,
        dv_rim,
        dq_end,
        dk_end,
        dv_end,
        d_conv_q,
        d_conv_k,
        d_conv_v,
        d_decay_ref,
        d_beta_ref,
        d_log_ref,
        d_bias_ref,
        ext,
        total,
        query,
        key,
        d_value,
        cum,
        rate,
        starts,
        ends,
        states,
        d_states,
        d_total,
        d_ext,
        d_cum,
        d_rate,
    ) = rest[extra:]
    step = pl.program_id(0)
    count = q_ref.shape[0]
    pairs = count // PAIR
    blocks = count // GROUP
    first, base = spot[0], spot[1]
    reset = reset_row(first, base, count)
    places = reset_places(first, base, reset)

    @pl.when(step == 0)
    def _():
        d_cum[...] = jnp.zeros_like(d_cum)
        d_rate[...] = jnp.zeros_like(d_rate)

    refs = (q_ref, k_ref, v_ref, q_rim, k_rim, v_rim, conv_q, conv_k, conv_v)
    for j in range(per_step):
        load_features(taps, j, refs, ext, total, reset, places)
        head = offset + step * per_step + j
        cum[j] = jnp.broadcast_to(column(cum_ref[...], head), (count, DK))
        rate[j] = jnp.broadcast_to(column(rate_ref[...], head), (count, DK))
        u = total[j, 0]
        c = u * sigmoid(u)
        query[j] = c * (unit_scale(c) * DK**-0.5)
        u = total[j, 1]
        c = u * sigmoid(u)
        key[j] = c * unit_scale(c)
        states[j] = high(start_ref[j])
        d_states[j] = high(near_ref[j]) + mm_tn(map_ref[j], far_ref[j])

    row, col, within, below = grid_masks()

    def keep_of(block):
        begin = base + block * GROUP
        return jnp.where((begin != 0) & (begin != first), 1.0, 0.0)

    def last_of(j, block):
        last = jnp.exp(cum[j, pl.ds(block * GROUP + GROUP - 1, 1), :])
        return jnp.concatenate([last, last], axis=1)

    def chain(block, carry):
        back = blocks - 1 - block
        at = pl.ds(pl.multiple_of(back * GROUP, GROUP), GROUP)
        for j in range(per_step):
            state = states[j] * keep_of(block)
            state_low = low(state)
            starts[j, block] = state_low
            states[j] = (
                last_of(j, block) * state
                - mm(turn_ref[j, block], state_low)
                + high(gain_ref[j, block])
            )
            d_state = d_states[j]
            d_low = low(d_state)
            ends[j, back] = d_low
            d_out = d_mixed_ref[at, j * DV : (j + 1) * DV]
            d_states[j] = keep_of(back) * (
                last_of(j, back) * d_state
                - mm_tn(turn_ref[j, back], d_low)
                + mm_tn(pass_ref[at, j * DK : (j + 1) * DK], d_out)
            )
        return carry

    lax.fori_loop(0, blocks, chain, 0, unroll=2)

    lane = lax.broadcasted_iota(jnp.int32, (PAIR, d_cum.shape[1]), 1)
    tall = lax.broadcasted_iota(jnp.int32, (PAIR, 1), 0)

    def assemble(pair, carry):
        at = pl.ds(pl.multiple_of(pair * PAIR, PAIR), PAIR)
        halves = [slice(half * GROUP, (half + 1) * GROUP) for half in range(2)]
        for j in range(per_step):
            g = cum[j, at, :]
            b = rate[j, at, :]
            k = key[j, at, :]
            q = query[j, at, :]
            v = []
            for half in range(DV // DK):
                u = total[j, 2 + half, at, :]
                v.append(u * sigmoid(u))
            v = jnp.concatenate(v, axis=1)
            bb = jnp.concatenate([b, b], axis=1)
            k_low, q_low = low(k), low(q)
            inverse = inverse_ref[j, at, :]
            spread = jnp.where(within, jnp.exp(jnp.where(within, g - g.T, 0.0)), 0.0)
            grown = jnp.exp(g)
            fall = jnp.exp(block_ends(g) - g)
            scores = mm_nt(q_low, k_low)
            d_out = d_mixed_ref[at, j * DV : (j + 1) * DV]
            grown_k = low(b * grown * k)
            falls = low(fall * k)
            begin = [starts[j, 2 * pair + half] for half in range(2)]
            end = [ends[j, 2 * pair + half] for half in range(2)]
            known = jnp.concatenate(
                [mm(grown_k[part], begin[half]) for half, part in enumerate(halves)], axis=0
            )
            change = low(mm(inverse, low(bb * v - known)))
            pulled = jnp.concatenate(
                [mm(falls[part], end[half]) for half, part in enumerate(halves)], axis=0
            )
            rhs = mm_tn(inverse, low(mm_tn(low(scores * spread), d_out) + pulled))
            rhs_low = low(rhs)
            d_lower = jnp.where(below, -mm_nt(rhs_low, change), 0.0)
            d_score = mm_nt(d_out, change) * spread
            d_gk = jnp.concatenate(
                [-mm_nt(rhs_low[part], begin[half]) for half, part in enumerate(halves)], axis=0
            )
            d_gq = jnp.concatenate(
                [mm_nt(d_out[part], begin[half]) for half, part in enumerate(halves)], axis=0
            )
            d_tail = jnp.concatenate(
                [mm_nt(change[part], end[half]) for half, part in enumerate(halves)], axis=0
            )
            bonus = [jnp.sum(high(begin[half]) * high(end[half])) for half in range(2)]
            d_a = d_lower * mm_nt(k_low, k_low) * spread
            cross = d_a * b + d_score * scores
            gk_k = d_gk * k
            rate_col = jnp.sum(d_a + grown * gk_k, axis=-1, keepdims=True) + jnp.sum(
                rhs * v, axis=-1, keepdims=True
            )
            tail_sum = jnp.sum(d_tail * (fall * k), axis=-1, keepdims=True)
            cum_col = (
                jnp.sum(
                    cross - cross.T + b * grown * gk_k + d_gq * (grown * q), axis=-1, keepdims=True
                )
                - tail_sum
            )
            for half, part in enumerate(halves):
                at_end = half * GROUP + GROUP - 1
                more = jnp.sum(tail_sum[part], axis=0, keepdims=True) + bonus[half] * grown[
                    at_end : at_end + 1, :1
                ]
                cum_col = cum_col + jnp.where(tall == at_end, more, 0.0)
            head = offset + step * per_step + j
            d_cum[at, :] = d_cum[at, :] + jnp.where(lane == head, cum_col, 0.0)
            d_rate[at, :] = d_rate[at, :] + jnp.where(lane == head, rate_col, 0.0)
            d_keys = d_lower * spread * b
            d_keys = low(d_keys + d_keys.T)
            d_score_low = low(d_score)
            d_query = grown * d_gq + mm(d_score_low, k_low)
            d_key = b * grown * d_gk + fall * d_tail + mm(d_keys, k_low) + mm_tn(d_score_low, q_low)
            query[j, at, :] = d_query
            key[j, at, :] = d_key
            d_value[j, at, :] = bb * rhs
        return carry

    lax.fori_loop(0, pairs, assemble, 0, unroll=2)

    d_total[0:RIM, :] = jnp.zeros((RIM, DK), jnp.float32)
    d_total[RIM + count : 2 * RIM + count, :] = jnp.zeros((RIM, DK), jnp.float32)

    def conv_back(rows, weight, out_ref, rim_ref, end_ref, d_weight_ref, cols):
        size = count + RIM
        spread_rows = None
        grads = []
        for tap in range(taps):
            moved = d_total[taps - 1 - tap : taps - 1 - tap + size, :]
            term = moved * weight[tap : tap + 1, :]
            spread_rows = term if spread_rows is None else spread_rows + term
            grads.append(jnp.sum(moved * rows[...], axis=0, keepdims=True))
        d_ext[...] = spread_rows
        near = d_total[pl.ds(reset + RIM, RIM), :]
        around = rows[pl.ds(reset, 2 * RIM), :]
        wrong_rows = jnp.zeros((2 * RIM, DK), jnp.float32)
        for tap in range(taps - 1):
            lead = RIM - taps + 1 + tap
            wrong = jnp.where(places >= taps - 1 - tap, 0.0, near)
            grads[tap] = grads[tap] - jnp.sum(
                wrong * around[lead : lead + RIM], axis=0, keepdims=True
            )
            wrong_rows = wrong_rows + jnp.concatenate(
                [
                    jnp.zeros((lead, DK), jnp.float32),
                    wrong * weight[tap : tap + 1, :],
                    jnp.zeros((RIM - lead, DK), jnp.float32),
                ],
                axis=0,
            )
        d_ext[pl.ds(reset, 2 * RIM), :] = d_ext[pl.ds(reset, 2 * RIM), :] - wrong_rows
        d_weight_ref[:, cols] = jnp.concatenate(grads, axis=0)
        rim_ref[:, cols] = d_ext[0:RIM, :]
        out_ref[:, cols] = low(d_ext[RIM : RIM + count, :])
        end_ref[:, cols] = d_ext[count : count + RIM, :]

    for j in range(per_step):
        cols = slice(j * DK, (j + 1) * DK)

        def unit_back(piece, d_unit, factor):
            u = total[j, piece]
            sig = sigmoid(u)
            c = u * sig
            scale = unit_scale(c)
            unit = c * scale
            d_unit = d_unit * factor
            d_c = scale * (d_unit - unit * jnp.sum(d_unit * unit, axis=-1, keepdims=True))
            d_total[RIM : RIM + count, :] = d_c * (sig * (1.0 + u * (1.0 - sig)))

        unit_back(0, query[j], DK**-0.5)
        conv_back(ext.at[j, 0], conv_q[:, cols], dq_ref, dq_rim, dq_end, d_conv_q, cols)
        unit_back(1, key[j], 1.0)
        conv_back(ext.at[j, 1], conv_k[:, cols], dk_ref, dk_rim, dk_end, d_conv_k, cols)
        for half in range(DV // DK):
            begin = j * DV + half * DK
            cut = slice(begin, begin + DK)
            u = total[j, 2 + half]
            sig = sigmoid(u)
            d_total[RIM : RIM + count, :] = d_value[j, :, half * DK : (half + 1) * DK] * (
                sig * (1.0 + u * (1.0 - sig))
            )
            conv_back(ext.at[j, 2 + half], conv_v[:, cut], dv_ref, dv_rim, dv_end, d_conv_v, cut)

    @pl.when(step == pl.num_programs(0) - 1)
    def _():
        shifted_in = decay_ref[...] + bias_ref[...]
        soft = jnp.maximum(shifted_in, 0.0) + jnp.log1p(jnp.exp(-jnp.abs(shifted_in)))
        speed = -jnp.exp(log_ref[...])
        after = jnp.where(within, 1.0, 0.0)
        d_log = jnp.zeros_like(d_log_ref)
        d_bias = jnp.zeros_like(d_bias_ref)
        for pair in range(pairs):
            rows = slice(pair * PAIR, (pair + 1) * PAIR)
            d_decay = lax.dot_general(
                after,
                d_cum[rows, :],
                (((0,), (0,)), ((), ())),
                precision=lax.Precision.HIGHEST,
                preferred_element_type=jnp.float32,
            )
            d_log = d_log + jnp.sum(d_decay * (speed * soft[rows]), axis=0, keepdims=True)
            d_in = d_decay * speed * jax.nn.sigmoid(shifted_in[rows])
            d_bias = d_bias + jnp.sum(d_in, axis=0, keepdims=True)
            d_decay_ref[rows, :] = d_in
        d_log_ref[...] = d_log
        d_bias_ref[...] = d_bias
        rates = rate_ref[...]
        d_beta_ref[...] = d_rate[...] * rates * (1.0 - rates)


def state_backward(
    q, k, v, rims, convs, decay, decay_log, decay_bias, cum, rate, saved, start, d_mixed, near, near_map, far, spot, per_step, offset, held, after
):
    count = q.shape[0]
    heads = decay.shape[1]
    taps = convs[0].shape[0]
    n = per_step
    blocks = count // GROUP
    skip = offset // n
    along = lambda i: (0, i + skip)
    fixed = lambda i: (0, 0)
    lead = lambda i: (i + skip, 0, 0)
    lead4 = lambda i: (i + skip, 0, 0, 0)
    out_along = lambda i: (0, i)
    f32, bf16 = jnp.float32, jnp.bfloat16
    shape = jax.ShapeDtypeStruct
    vm = pltpu.VMEM
    thin = [(RIM, DK), (RIM, DK), (RIM, DV)]
    out_blocks = [(count, DK), (count, DK), (count, DV)] + thin + thin
    out_blocks += [(taps, DK), (taps, DK), (taps, DV)]
    tables = [(count, heads), (count, heads), (1, heads), (1, heads)]
    return pl.pallas_call(
        functools.partial(state_back_kernel, taps, n, offset, len(after)),
        grid=(held // n,),
        in_specs=[
            pl.BlockSpec(memory_space=pltpu.SMEM),
            spec((count, n * DK), along),
            spec((count, n * DK), along),
            spec((count, n * DV), along),
            spec((RIM, n * DK), along),
            spec((RIM, n * DK), along),
            spec((RIM, n * DV), along),
            spec((taps, n * DK), along),
            spec((taps, n * DK), along),
            spec((taps, n * DV), along),
            spec((count, heads), fixed),
            spec((1, heads), fixed),
            spec((1, heads), fixed),
            spec((count, heads), fixed),
            spec((count, heads), fixed),
            spec((n, count, PAIR), lead),
            spec((count, n * DK), along),
            spec((n, blocks, DK, DK), lead4),
            spec((n, blocks, DK, DV), lead4),
            spec((n, DK, DV), lead),
            spec((count, n * DV), along),
            spec((n, DK, DV), lead),
            spec((n, DK, DK), lead),
            spec((n, DK, DV), lead),
        ]
        + [pl.BlockSpec(memory_space=pl.ANY) for _ in after],
        out_specs=[spec((rows, n * width), out_along) for rows, width in out_blocks]
        + [spec(block, fixed) for block in tables],
        out_shape=[
            shape((rows, held * width), bf16 if i < 3 else f32)
            for i, (rows, width) in enumerate(out_blocks)
        ]
        + [shape(block, f32) for block in tables],
        scratch_shapes=[
            vm((n, 4, count + RIM, DK), f32),
            vm((n, 4, count, DK), f32),
            vm((n, count, DK), f32),
            vm((n, count, DK), f32),
            vm((n, count, DV), f32),
            vm((n, count, DK), f32),
            vm((n, count, DK), f32),
            vm((n, blocks, DK, DV), bf16),
            vm((n, blocks, DK, DV), bf16),
            vm((n, DK, DV), f32),
            vm((n, DK, DV), f32),
            vm((count + 2 * RIM, DK), f32),
            vm((count + RIM, DK), f32),
            vm((count, heads), f32),
            vm((count, heads), f32),
        ],
        compiler_params=pltpu.CompilerParams(
            dimension_semantics=("arbitrary",), vmem_limit_bytes=VMEM_BYTES
        ),
        cost_estimate=LITTLE,
    )(
        spot,
        q,
        k,
        v,
        *rims,
        *convs,
        decay,
        decay_log,
        decay_bias,
        cum,
        rate,
        *saved,
        start,
        d_mixed,
        near,
        near_map,
        far,
        *after,
    )


def shifted(value, axis, steps):
    count = lax.axis_size(axis)
    leading, last = (max(0, -steps), min(count, count - steps))
    return lax.ppermute(value, axis, [(source, source + steps) for source in range(leading, last)])


def rms_scale(values, gain):
    return values * lax.rsqrt(jnp.mean(values * values, axis=-1, keepdims=True) + EPS) * gain


def swish_product(gate_ffn, up_ffn):
    return jax.nn.silu(gate_ffn) * up_ffn


def project(rows, weight):
    return jnp.dot(rows, weight, preferred_element_type=jnp.float32)


def rows_product(left, right):
    return jnp.dot(left, right, preferred_element_type=jnp.float32)


def rows_back(left, weight):
    return jnp.einsum("tc,dc->td", left, weight, preferred_element_type=jnp.float32)


def weight_grad(rows, grads):
    return jnp.einsum("td,tc->dc", rows, grads, preferred_element_type=jnp.float32)


STAGES = {"x": ("seq", 0, 1), "y": ("seq", 1, 2), "l": ("dp", 0, 4), "h": ("dp", 1, 8)}


def trade(value, stage):
    axis, bit, _ = STAGES[stage]
    count = lax.axis_size(axis)
    return lax.ppermute(value, axis, [(place, place ^ (1 << bit)) for place in range(count)])


def arrange_kernel(per_head, picks, full_ref, mine_ref, other_ref, *rest):
    out_ref = rest[-1]
    width = full_ref.shape[1] // 16
    mine = (pl.program_id(0) // per_head) == picks[16]
    for place in range(16):
        source = pl.ds(pl.multiple_of(picks[place] * width, width), width)
        target = slice(place * width, (place + 1) * width)
        out_ref[0, :, target] = full_ref[:, source]

    def fill(part_ref):
        for place in range(16):
            source = pl.ds(pl.multiple_of(picks[place] * width, width), width)
            out_ref[1, :, place * width : (place + 1) * width] = part_ref[:, source]

    @pl.when(mine)
    def _():
        fill(mine_ref)

    @pl.when(jnp.logical_not(mine))
    def _():
        fill(other_ref)


def with_other(got):
    if lax.axis_size("heads") == 2:
        return got, lax.ppermute(got, "heads", [(0, 1), (1, 0)])
    whole = heads_gather(got)
    return whole, whole


def paired_rows(full, got, order, *after):
    order = order[1:] + order[:1]
    own = lax.axis_index("dp") * lax.axis_size("seq") + lax.axis_index("seq")
    masks = [
        sum(STAGES[stage][2] for k, stage in enumerate(order) if place >> (3 - k) & 1)
        for place in range(16)
    ]
    picks = jnp.concatenate(
        [own ^ jnp.array(masks, jnp.int32), lax.axis_index("heads").astype(jnp.int32)[None]]
    )
    got, other = got
    count, width = full.shape
    size = 192 if got.shape[0] % 192 == 0 else 96
    blocks = got.shape[0] // size
    piece = pl.BlockSpec((size, width), lambda i: (i, 0))
    part = pl.BlockSpec((size, width), lambda i: (lax.rem(i, blocks), 0))
    both = pl.pallas_call(
        functools.partial(arrange_kernel, blocks),
        grid=(count // size,),
        in_specs=[pl.BlockSpec(memory_space=pltpu.SMEM), piece, part, part]
        + [pl.BlockSpec(memory_space=pl.ANY) for _ in after],
        out_specs=pl.BlockSpec((2, size, width), lambda i: (0, i, 0)),
        out_shape=jax.ShapeDtypeStruct((2, count, width), full.dtype),
        compiler_params=pltpu.CompilerParams(
            dimension_semantics=("arbitrary",), vmem_limit_bytes=VMEM_BYTES
        ),
        cost_estimate=LITTLE,
    )(picks, full, got, other, *after)
    return both.reshape(-1, width)


def own_side(stage):
    axis, bit, _ = STAGES[stage]
    return lax.rem(lax.axis_index(axis) // (1 << bit), 2)


def pick_half(grads, order, which):
    half = grads.shape[1] // 2
    side = own_side(order[0])
    return lax.dynamic_slice_in_dim(grads, (side if which else 1 - side) * half, half, 1)


def join_halves(grads, got, order):
    return jnp.concatenate([pick_half(grads, order, 1), got], axis=0)


def trade_halves(grads, order):
    return join_halves(grads, trade(pick_half(grads, order, 0), order[0]), order)


def pair_grad(rows, grads, begin, end):
    width = rows.shape[1] // 16
    return weight_grad(rows[:, begin * width : end * width], grads)


def grad_open(rows, grads, order):
    sent = low(pair_grad(rows, grads, 8, 16))
    return rows, grads, sent, trade(sent, order[1])


def grad_next(opened, order):
    rows, grads, _, first = opened
    middle = first.shape[0] // 2
    sent = low(pair_grad(rows, grads, 4, 8) + high(first[middle:]))
    rest = pair_grad(rows, grads, 0, 4) + high(first[:middle])
    return rest, sent, trade(sent, order[2])


def grad_last(moved):
    rest, _, second = moved
    return low(rest + high(second))


def finish_kernel(plan, head_steps, *refs):
    groups = len(plan)
    grads, small_ref = refs[:groups], refs[groups]
    outs, small_out = refs[groups + 1 : 2 * groups + 1], refs[2 * groups + 1]
    scratch = refs[2 * groups + 2 :]
    buffers = []
    for stages, _ in plan:
        buffers.append(scratch[: len(stages)])
        scratch = scratch[len(stages) :]
    small_sum, small_got, send_sem, recv_sem, small_send, small_recv = scratch

    def side(stage):
        axis, bit, _ = STAGES[stage]
        return lax.rem(lax.axis_index(axis) // (1 << bit), 2)

    def partner(stage):
        axis, bit, _ = STAGES[stage]
        return {axis: lax.axis_index(axis) + (1 - 2 * side(stage)) * (1 << bit)}

    def head_partner(step):
        me = lax.axis_index("heads")
        return {"heads": me + (1 - 2 * lax.rem(me // step, 2)) * step}

    barrier = pltpu.get_barrier_semaphore()
    targets = [partner(stage) for stage in "xylh"] + [head_partner(step) for step in head_steps]
    for target in targets:
        pl.semaphore_signal(
            barrier, inc=1, device_id=target, device_id_type=pl.DeviceIdType.MESH
        )
    pl.semaphore_wait(barrier, len(targets))

    started = []

    def send(source, target, sems, device):
        copy = pltpu.make_async_remote_copy(
            src_ref=source,
            dst_ref=target,
            send_sem=sems[0],
            recv_sem=sems[1],
            device_id=device,
            device_id_type=pl.DeviceIdType.MESH,
        )
        copy.start()
        started.append(copy)
        return copy

    most = max(len(cuts) for _, cuts in plan)
    longest = max(len(stages) for stages, _ in plan)
    chunks, number = [], 0
    rounds = [[] for _ in range(most)]
    for g, (stages, cuts) in enumerate(plan):
        for k, cut in enumerate(cuts):
            chunks.append((g, stages, slice(*cut)))
            rounds[k].append(number)
            number += 1
    copies = {}

    def advance(index, step):
        g, stages, cut = chunks[index]
        if step > len(stages):
            return
        if step > 0:
            copies[index, step - 1].wait_recv()
        full = grads[g].shape[0]
        here = buffers[g]
        if step == len(stages):
            there = 1 - side(stages[-1])
            outs[g][pl.ds(there, 1), :, cut] = here[-1][:, cut][None]
            return
        rows = slice(full >> (step + 1), full >> step)
        if step == 0:
            source = grads[g].at[rows, cut]
            if len(stages) == 1:
                outs[g][pl.ds(side(stages[0]), 1), :, cut] = grads[g][: rows.start, cut][None]
        else:
            last = step == len(stages) - 1
            begin = 0 if last else rows.start
            value = high(grads[g][begin : rows.stop, cut])
            for got in here[:step]:
                value = value + high(got[begin : rows.stop, cut])
            if last:
                outs[g][pl.ds(side(stages[-1]), 1), :, cut] = low(value[: rows.start])[None]
                value = value[rows.start :]
            here[0][rows, cut] = low(value)
            source = here[0].at[rows, cut]
        place = 4 * index + step
        copies[index, step] = send(
            source,
            here[step].at[:, cut],
            (send_sem.at[place], recv_sem.at[place]),
            partner(stages[step]),
        )

    small_copies = []
    names = "xylh"

    def small_step(step):
        if step >= 1 and step <= 4:
            small_copies[step - 1].wait_recv()
            small_sum[step] = small_sum[step - 1] + small_got[step - 1]
        if step == 4:
            small_out[pl.ds(lax.axis_index("heads"), 1)] = small_sum[4:5]
        if step < 4:
            if step == 0:
                small_sum[0] = small_ref[...]
            sems = (small_send.at[step], small_recv.at[step])
            small_copies.append(
                send(small_sum.at[step], small_got.at[step], sems, partner(names[step]))
            )
        elif step - 4 <= len(head_steps):
            k = step - 4
            if k >= 1:
                small_copies[step - 1].wait_recv()
            if k < len(head_steps):
                size = head_steps[k]
                begin = lax.axis_index("heads") // size * size
                block = small_out.at[pl.ds(begin, size)]
                sems = (small_send.at[step], small_recv.at[step])
                small_copies.append(send(block, block, sems, head_partner(size)))

    total_small = 5 + len(head_steps)
    small_step(0)
    for ahead in range(min(2, most)):
        for index in rounds[ahead]:
            advance(index, 0)
    for t in range(max(most + longest, total_small - 1)):
        for lag in range(longest):
            if lag == 1 and t + 2 < most:
                for index in rounds[t + 2]:
                    advance(index, 0)
            if 0 <= t - lag < most:
                for index in rounds[t - lag]:
                    advance(index, lag + 1)
        if t + 1 < total_small:
            small_step(t + 1)
    for copy in started:
        copy.wait_send()


def finish(grads, orders, small):
    count = lax.axis_size("heads")
    head_steps = []
    while 1 << len(head_steps) < count:
        head_steps.append(1 << len(head_steps))
    plan, scratch, outs = [], [], []
    for array, order in zip(grads, orders):
        full, half = array.shape
        step = min(256 if len(order) == 4 else 512, half) if half % 128 == 0 else half
        cuts = [(at, min(at + step, half)) for at in range(0, half, step)]
        plan.append((order[1:] + order[:1], cuts))
        for level in range(len(order)):
            scratch.append(pltpu.VMEM((full >> (level + 1), half), jnp.bfloat16))
        outs.append(jax.ShapeDtypeStruct((2, full >> len(order), half), jnp.bfloat16))
    pieces = sum(len(cuts) for _, cuts in plan)
    inside = pl.BlockSpec(memory_space=pltpu.VMEM)
    f32 = jnp.float32
    return pl.pallas_call(
        functools.partial(finish_kernel, tuple(plan), tuple(head_steps)),
        in_specs=[inside] * (len(grads) + 1),
        out_specs=[inside] * (len(grads) + 1),
        out_shape=outs + [jax.ShapeDtypeStruct((count,) + small.shape, f32)],
        scratch_shapes=scratch
        + [
            pltpu.VMEM((5,) + small.shape, f32),
            pltpu.VMEM((4,) + small.shape, f32),
            pltpu.SemaphoreType.DMA((4 * pieces,)),
            pltpu.SemaphoreType.DMA((4 * pieces,)),
            pltpu.SemaphoreType.DMA((8,)),
            pltpu.SemaphoreType.DMA((8,)),
        ],
        compiler_params=pltpu.CompilerParams(
            collective_id=0, has_side_effects=True, vmem_limit_bytes=60 * 1024 * 1024
        ),
        cost_estimate=LITTLE,
    )(*grads, small)


def fence(one, *after):
    return pl.pallas_call(
        lambda one_ref, *rest: rest[-1].__setitem__(..., one_ref[...]),
        in_specs=[pl.BlockSpec(memory_space=pltpu.VMEM)]
        + [pl.BlockSpec(memory_space=pl.ANY) for _ in after],
        out_specs=pl.BlockSpec(memory_space=pltpu.VMEM),
        out_shape=jax.ShapeDtypeStruct(one.shape, one.dtype),
        compiler_params=pltpu.CompilerParams(vmem_limit_bytes=VMEM_BYTES),
        cost_estimate=LITTLE,
    )(one, *after)


def order_kernel(*refs):
    pass


def ordered(values, *after):
    anywhere = pl.BlockSpec(memory_space=pl.ANY)
    return pl.pallas_call(
        order_kernel,
        in_specs=[anywhere] * (len(values) + len(after)),
        out_specs=[anywhere] * len(values),
        out_shape=[jax.ShapeDtypeStruct(part.shape, part.dtype) for part in values],
        input_output_aliases={k: k for k in range(len(values))},
        cost_estimate=LITTLE,
    )(*values, *after)


def heads_gather(rows, axis=0):
    count = lax.axis_size("heads")
    own = lax.axis_index("heads")
    step = 1
    while step < count:
        other = lax.ppermute(rows, "heads", [(place, place ^ step) for place in range(count)])
        upper = lax.rem(own // step, 2) == 1
        rows = jnp.concatenate(
            [jnp.where(upper, other, rows), jnp.where(upper, rows, other)], axis=axis
        )
        step *= 2
    return rows


def heads_sum(compute, count, kind):
    if lax.axis_size("heads") != 2:
        whole = compute(lambda rows: rows).astype(kind)
        return high(lax.psum_scatter(whole, "heads", scatter_dimension=0, tiled=True))
    own = lax.axis_index("heads")
    half = count // 2

    def part(which):
        return compute(lambda rows: lax.dynamic_slice_in_dim(rows, which * half, half, 0))

    got = lax.ppermute(part(1 - own).astype(kind), "heads", [(0, 1), (1, 0)])
    return part(own) + high(got)


ORDERS = ("xylh", "yxlh", "lxyh")
FFN_ORDERS = ("xlyh", "yxlh", "lyhx")


def body(
    hidden_in,
    out_cotangent,
    lengths,
    norm_gain,
    q_weight,
    k_weight,
    v_weight,
    gate_weight,
    decay_weight,
    beta_weight,
    conv_q,
    conv_k,
    conv_v,
    decay_log,
    decay_bias,
    out_gain,
    out_weight,
    ffn_gain,
    ffn_gate,
    ffn_up,
    ffn_down,
):
    resid = hidden_in[0].astype(jnp.float32)
    normed_own = rms_scale(resid, norm_gain).astype(jnp.bfloat16)
    normed, cotangent = (
        heads_gather(normed_own),
        heads_gather(out_cotangent[0]),
    )
    span = normed.shape[0]
    normed_got = {order: trade(normed_own, order[0]) for order in ORDERS[:2]}
    cotangent_got = trade(out_cotangent[0], FFN_ORDERS[2][0])
    taps = conv_q.shape[0]
    q_proj = project(normed, q_weight)
    k_proj = project(normed, k_weight)
    v_proj = project(normed, v_weight)
    gate_proj = project(normed, gate_weight)
    heads = decay_weight.shape[1]
    per_step = min(2, heads)
    narrow = project(normed, jnp.concatenate([decay_weight, beta_weight], axis=1))
    decay_proj, beta_proj = narrow[:, :heads], narrow[:, heads:]
    seq_index = lax.axis_index("seq")
    spot = jnp.stack([lengths[0, 0], seq_index * span]).astype(jnp.int32)
    ends = [part[span - RIM :] for part in (q_proj, k_proj, v_proj)]
    rims = jnp.split(
        shifted(jnp.concatenate(ends, axis=1), "seq", 1), (heads * DK, 2 * heads * DK), axis=1
    )
    convs = (conv_q, conv_k, conv_v)
    log_row, bias_row, gain_row = decay_log[None], decay_bias[None], out_gain[None]
    mixed_local, reach, span_map, span_add, *saved, cum, rate = state_forward(
        q_proj, k_proj, v_proj, rims, convs, decay_proj, beta_proj, log_row, bias_row, spot, per_step
    )
    span_map, span_add = ordered((span_map, span_add), cotangent_got, *normed_got.values())
    normed_got = {order: with_other(got) for order, got in normed_got.items()}
    cotangent_got = with_other(cotangent_got)
    near_map, near_add = shifted((span_map, span_add), "seq", 1)
    far_add = shifted(span_add, "seq", 2)
    next_map = shifted(span_map, "seq", -1)
    (mixed_local,) = ordered((mixed_local,), next_map)
    gated_low, mixed_low, start_state = gate_forward(
        mixed_local, reach, near_map, near_add, far_add, gate_proj, gain_row, per_step
    )
    (gated_low,) = ordered(
        (gated_low,), cotangent_got[1], *(got[1] for got in normed_got.values())
    )
    mixer = heads_sum(
        lambda pick: rows_product(pick(gated_low), out_weight), span, jnp.bfloat16
    )
    resid_mid = resid + mixer
    ffn_own = rms_scale(resid_mid, ffn_gain).astype(jnp.bfloat16)
    ffn_in = heads_gather(ffn_own)
    ffn_got = {order: trade(ffn_own, order[0]) for order in FFN_ORDERS[:2]}
    gate_ffn = project(ffn_in, ffn_gate)
    up_ffn = project(ffn_in, ffn_up)
    act, act_pull = jax.vjp(swish_product, gate_ffn, up_ffn)
    act_low = act.astype(jnp.bfloat16)
    d_act = jnp.einsum("td,fd->tf", cotangent, ffn_down, preferred_element_type=jnp.float32)
    d_gate_ffn, d_up_ffn = act_pull(d_act)
    d_gate_low = d_gate_ffn.astype(jnp.bfloat16)
    d_up_low = d_up_ffn.astype(jnp.bfloat16)
    ffn_low = (d_gate_low, d_up_low, act_low)
    theirs = [pick_half(part, order, 0) for part, order in zip(ffn_low, FFN_ORDERS)]
    ffn_traded = [trade(part, order[0]) for part, order in zip(theirs, FFN_ORDERS)]
    ffn_low = ordered(ffn_low, *ffn_got.values(), *theirs)
    d_gate_low, d_up_low, act_low = ffn_low
    ffn_got = {order: with_other(got) for order, got in ffn_got.items()}
    gate_halves, up_halves, down_halves = (
        join_halves(part, got, order)
        for part, got, order in zip(ffn_low, ffn_traded, FFN_ORDERS)
    )
    ffn_out = heads_sum(lambda pick: rows_product(pick(act_low), ffn_down), span, jnp.bfloat16)
    output = (resid_mid + ffn_out).astype(jnp.bfloat16)
    cotangent_rel = paired_rows(cotangent, cotangent_got, FFN_ORDERS[2], act_low)
    ffn_rel = [
        paired_rows(ffn_in, ffn_got[order], order, d_gate_low) for order in FFN_ORDERS[:2]
    ]
    gate_open = grad_open(ffn_rel[0], gate_halves, FFN_ORDERS[0])
    up_open = grad_open(ffn_rel[1], up_halves, FFN_ORDERS[1])
    down_open = grad_open(cotangent_rel, down_halves, FFN_ORDERS[2])
    d_ffn = heads_sum(
        lambda pick: rows_back(pick(d_gate_low), ffn_gate) + rows_back(pick(d_up_low), ffn_up),
        span,
        jnp.bfloat16,
    )
    _, ffn_norm_pull = jax.vjp(rms_scale, resid_mid, ffn_gain)
    d_mid_norm, d_ffn_gain = ffn_norm_pull(d_ffn)
    d_mid = out_cotangent[0].astype(jnp.float32) + d_mid_norm
    d_mid_low = low(d_mid)
    d_mid_all = heads_gather(d_mid_low)
    d_mid_got = with_other(trade(d_mid_low, ORDERS[2][0]))
    d_gated = jnp.einsum("td,cd->tc", d_mid_all, out_weight, preferred_element_type=jnp.float32)
    d_mixed, d_gate_low_mix, d_start, d_out_gain = gate_backward(
        d_gated, mixed_low, reach, gate_proj, gain_row, per_step
    )
    next_start = shifted(d_start, "seq", -1)
    beyond_start = shifted(d_start, "seq", -2)
    mix_halves = trade_halves(d_gate_low_mix, ORDERS[0])
    (gated_low,) = ordered((gated_low,), d_gate_low_mix)
    out_halves = trade_halves(gated_low, ORDERS[2])
    normed_rel = [
        paired_rows(normed, normed_got[order], order, up_open[2]) for order in ORDERS[:2]
    ]
    d_mid_rel = paired_rows(d_mid_all, d_mid_got, ORDERS[2], up_open[2])
    moved = [
        grad_next(opened, order)
        for opened, order in zip((gate_open, up_open, down_open), FFN_ORDERS)
    ]
    back = state_backward(
        q_proj,
        k_proj,
        v_proj,
        rims,
        convs,
        decay_proj,
        log_row,
        bias_row,
        cum,
        rate,
        saved,
        start_state,
        d_mixed,
        next_start,
        next_map,
        beyond_start,
        spot,
        per_step,
        0,
        heads,
        [part[1] for part in moved] + [d_mid_rel, *normed_rel],
    )
    rim = jnp.concatenate(back[3:6], axis=1)
    (rim,) = ordered((rim,), *(part[2] for part in moved))
    rim = shifted(rim, "seq", -1)
    passed = jnp.split(rim, (heads * DK, 2 * heads * DK), axis=1)
    d_q_low, d_k_low, d_v_low = (
        lax.dynamic_update_slice_in_dim(whole, low(end + more), span - RIM, 0)
        for whole, end, more in zip(back[0:3], back[6:9], passed)
    )
    d_decay_low, d_beta_low = low(back[12]), low(back[13])
    flat_lows = (jnp.concatenate([d_q_low, d_k_low], axis=1), d_v_low)
    late = [pick_half(part, order, 0) for part, order in zip(flat_lows, ORDERS)]
    late_got = [trade(part, order[0]) for part, order in zip(late, ORDERS)]
    d_gate_low_mix, d_mid_rel, *normed_rel = ordered(
        (d_gate_low_mix, d_mid_rel, *normed_rel), *late
    )
    tails = [
        grad_last(moved[0]),
        grad_last(moved[1]),
        grad_last(moved[2]),
        low(pair_grad(normed_rel[0], mix_halves, 0, 16)),
        low(pair_grad(d_mid_rel, out_halves, 0, 16)),
    ]
    tail_orders = [order[:1] + order[3:] for order in FFN_ORDERS] + [ORDERS[0], ORDERS[2]]
    for flat_low, got, rows, order in zip(flat_lows, late_got, normed_rel, ORDERS):
        tails.append(low(pair_grad(rows, join_halves(flat_low, got, order), 0, 16)))
        tail_orders.append(order)
    narrow_grad = weight_grad(jnp.concatenate([d_decay_low, d_beta_low], axis=1), normed)
    pairs = (
        (d_q_low, q_weight),
        (d_k_low, k_weight),
        (d_v_low, v_weight),
        (d_gate_low_mix, gate_weight),
        (d_decay_low, decay_weight),
        (d_beta_low, beta_weight),
    )
    d_normed = heads_sum(
        lambda pick: sum(rows_back(pick(rows), weight) for rows, weight in pairs),
        span,
        jnp.bfloat16,
    )
    _, in_norm_pull = jax.vjp(rms_scale, resid, norm_gain)
    d_in_norm, d_norm_gain = in_norm_pull(d_normed)
    input_grad = d_mid + d_in_norm
    wide = normed.shape[1]
    conv_all = jnp.concatenate(back[9:12], axis=1)

    def full_rows(part):
        return jnp.pad(part, ((0, 0), (0, wide - part.shape[1])))

    conv_rows = [full_rows(conv_all[:, at : at + wide]) for at in range(0, conv_all.shape[1], wide)]
    last_row = full_rows(jnp.concatenate([d_out_gain, back[14], back[15]], axis=1))
    stacked = [narrow_grad] + conv_rows + [d_norm_gain[None], d_ffn_gain[None], last_row]
    flat = jnp.concatenate(stacked, axis=0)
    flat = jnp.pad(flat, ((0, -flat.shape[0] % 8), (0, 0)))
    *sums, everyone = finish(tails, tail_orders, flat)
    grad_gate, grad_up, grad_down, grad_gate_mix, grad_out, grad_qk, grad_v = (
        high(jnp.concatenate([part[0], part[1]], axis=1)) for part in sums
    )
    grad_down, grad_out = grad_down.T, grad_out.T
    grad_q, grad_k = jnp.split(grad_qk, 2, axis=1)
    shard = lax.axis_index("dp") * lax.axis_size("seq") + lax.axis_index("seq")
    size = wide // 16
    narrow_sum = lax.dynamic_slice(
        everyone, (lax.axis_index("heads"), 0, shard * size), (1, 2 * heads, size)
    )[0].T
    grad_decay, grad_beta = narrow_sum[:, :heads], narrow_sum[:, heads:]
    at = 2 * heads
    conv_sum = jnp.concatenate(
        [everyone[:, at + taps * k : at + taps * (k + 1)] for k in range(len(conv_rows))], axis=2
    )
    at += taps * len(conv_rows)
    width_k = heads * DK

    def by_head(part):
        return jnp.swapaxes(part, 0, 1).reshape(part.shape[1], -1)

    width_v = out_gain.shape[0]
    small = [
        everyone[:, at].sum(0),
        everyone[:, at + 1].sum(0),
        everyone[:, at + 2, :width_v].sum(0),
        everyone[:, at + 2, width_v : width_v + heads].reshape(-1),
        everyone[:, at + 2, width_v + heads : width_v + 2 * heads].reshape(-1),
        by_head(conv_sum[:, :, :width_k]),
        by_head(conv_sum[:, :, width_k : 2 * width_k]),
        by_head(conv_sum[:, :, 2 * width_k : 2 * width_k + heads * DV]),
    ]
    return (
        output[None],
        input_grad[None],
        small[0],
        grad_q,
        grad_k,
        grad_v,
        grad_gate_mix,
        grad_decay,
        grad_beta,
        small[5],
        small[6],
        small[7],
        small[3],
        small[4],
        small[2],
        grad_out,
        small[1],
        grad_gate,
        grad_up,
        grad_down,
    )


def solution(mesh):
    in_specs = (
        P("dp", ("seq", "heads"), None),
        P("dp", ("seq", "heads"), None),
        P("dp", None),
        P(),
        P(None, "heads"),
        P(None, "heads"),
        P(None, "heads"),
        P(None, "heads"),
        P(None, "heads"),
        P(None, "heads"),
        P(None, "heads"),
        P(None, "heads"),
        P(None, "heads"),
        P("heads"),
        P("heads"),
        P(),
        P("heads", None),
        P(),
        P(None, "heads"),
        P(None, "heads"),
        P("heads", None),
    )
    out_specs = (
        P("dp", ("seq", "heads"), None),
        P("dp", ("seq", "heads"), None),
        P(),
        P(("dp", "seq"), "heads"),
        P(("dp", "seq"), "heads"),
        P(("dp", "seq"), "heads"),
        P(("dp", "seq"), "heads"),
        P(("dp", "seq"), "heads"),
        P(("dp", "seq"), "heads"),
        P(),
        P(),
        P(),
        P(),
        P(),
        P(),
        P("heads", ("dp", "seq")),
        P(),
        P(("dp", "seq"), "heads"),
        P(("dp", "seq"), "heads"),
        P("heads", ("dp", "seq")),
    )
    return jax.shard_map(body, mesh=mesh, in_specs=in_specs, out_specs=out_specs, check_vma=False)
```

```python
import functools

import jax
import jax.numpy as jnp
from jax import lax
from jax.experimental import pallas as pl
from jax.experimental.pallas import tpu as pltpu
from jax.sharding import PartitionSpec as P

HEADS = 16
DK = 128
DV = 256
GROUP = 64
EPS = 1e-06
PAIR = 2 * GROUP
RIM = 8
VMEM_BYTES = 56 * 1024 * 1024
LITTLE = pl.CostEstimate(flops=0, bytes_accessed=0, transcendentals=0)


def mm(left, right):
    return lax.dot_general(
        left, right, (((1,), (0,)), ((), ())), preferred_element_type=jnp.float32
    )


def mm_nt(left, right):
    return lax.dot_general(
        left, right, (((1,), (1,)), ((), ())), preferred_element_type=jnp.float32
    )


def mm_tn(left, right):
    return lax.dot_general(
        left, right, (((0,), (0,)), ((), ())), preferred_element_type=jnp.float32
    )


def low(value):
    return value.astype(jnp.bfloat16)


def high(value):
    return value.astype(jnp.float32)


def grid_masks():
    row = lax.broadcasted_iota(jnp.int32, (PAIR, PAIR), 0)
    col = lax.broadcasted_iota(jnp.int32, (PAIR, PAIR), 1)
    same = (row // GROUP) == (col // GROUP)
    return row, col, same & (row >= col), same & (row > col)


def masks_low(row, col):
    sizes, masks = [], []
    size = 1
    while size < GROUP:
        here = ((row // (2 * size)) == (col // (2 * size))) & ((row // size) > (col // size))
        masks.append(low(jnp.where(here, 1.0, 0.0)))
        sizes.append(size)
        size *= 2
    return masks


def sigmoid(value):
    return 0.5 * jnp.tanh(0.5 * value) + 0.5


def unit_scale(value):
    return lax.rsqrt(jnp.sum(value * value, axis=-1, keepdims=True) + EPS)


def column(table, head):
    lane = lax.broadcasted_iota(jnp.int32, table.shape, 1)
    return jnp.sum(jnp.where(lane == head, table, 0.0), axis=1, keepdims=True)


def reset_row(first, base, count):
    inside = (first > base) & (first < base + count)
    return pl.multiple_of(jnp.where(inside, first - base, 0), GROUP)


def reset_places(first, base, reset):
    token = base + reset + lax.broadcasted_iota(jnp.int32, (RIM, 1), 0)
    return token - jnp.where(token >= first, first, 0)


def conv_total(ext, total, weight, reset, places):
    count, taps = total.shape[0], weight.shape[0]
    lead = RIM - taps + 1
    whole = ext[lead : lead + count, :] * weight[0:1, :]
    for tap in range(1, taps):
        whole = whole + ext[lead + tap : lead + tap + count, :] * weight[tap : tap + 1, :]
    total[...] = whole
    near = ext[pl.ds(reset, 2 * RIM), :]
    fixed = near[RIM : 2 * RIM] * weight[taps - 1 : taps, :]
    for tap in range(taps - 1):
        rows = jnp.where(places >= taps - 1 - tap, near[lead + tap : lead + tap + RIM], 0.0)
        fixed = fixed + rows * weight[tap : tap + 1, :]
    total[pl.ds(reset, RIM), :] = fixed


def load_ext(ext, rim, body):
    ext[0:RIM, :] = rim
    ext[RIM : RIM + body.shape[0], :] = body


def load_features(taps, j, refs, ext, total, reset, places):
    q_ref, k_ref, v_ref, q_rim, k_rim, v_rim, conv_q, conv_k, conv_v = refs
    cols = slice(j * DK, (j + 1) * DK)
    sources = [(q_ref, q_rim, conv_q, cols), (k_ref, k_rim, conv_k, cols)]
    for half in range(DV // DK):
        begin = j * DV + half * DK
        sources.append((v_ref, v_rim, conv_v, slice(begin, begin + DK)))
    for piece, (body, rim, weight, cut) in enumerate(sources):
        load_ext(ext.at[j, piece], rim[:, cut], body[:, cut])
        conv_total(ext.at[j, piece], total.at[j, piece], weight[:, cut], reset, places)


def block_ends(g):
    return jnp.concatenate(
        [
            jnp.broadcast_to(g[GROUP - 1 : GROUP], (GROUP, DK)),
            jnp.broadcast_to(g[PAIR - 1 : PAIR], (GROUP, DK)),
        ],
        axis=0,
    )


def decay_tables(decay_ref, beta_ref, log_ref, bias_ref, cum_ref, rate_ref):
    count = decay_ref.shape[0]
    shifted_in = decay_ref[...] + bias_ref[...]
    soft = jnp.maximum(shifted_in, 0.0) + jnp.log1p(jnp.exp(-jnp.abs(shifted_in)))
    log_decay = -jnp.exp(log_ref[...]) * soft
    _, _, within, _ = grid_masks()
    ones = jnp.where(within, 1.0, 0.0)
    for pair in range(count // PAIR):
        rows = slice(pair * PAIR, (pair + 1) * PAIR)
        cum_ref[rows, :] = lax.dot_general(
            ones,
            log_decay[rows, :],
            (((1,), (0,)), ((), ())),
            precision=lax.Precision.HIGHEST,
            preferred_element_type=jnp.float32,
        )
    rate_ref[...] = jax.nn.sigmoid(beta_ref[...])


def state_kernel(
    taps,
    per_step,
    spot,
    q_ref,
    k_ref,
    v_ref,
    q_rim,
    k_rim,
    v_rim,
    conv_q,
    conv_k,
    conv_v,
    decay_ref,
    beta_ref,
    log_ref,
    bias_ref,
    mixed_ref,
    reach_ref,
    map_ref,
    add_ref,
    inverse_ref,
    pass_ref,
    turn_ref,
    gain_ref,
    cum_ref,
    rate_ref,
    ext,
    total,
    cum,
    lower,
    halfway,
    score,
    grown_q,
    grown_k,
    scaled_v,
    tail,
    states,
    starts,
):
    step = pl.program_id(0)
    count = q_ref.shape[0]
    pairs = count // PAIR
    blocks = count // GROUP
    first, base = spot[0], spot[1]
    reset = reset_row(first, base, count)
    places = reset_places(first, base, reset)

    @pl.when(step == 0)
    def _():
        decay_tables(decay_ref, beta_ref, log_ref, bias_ref, cum_ref, rate_ref)

    row, col, within, below = grid_masks()
    refs = (q_ref, k_ref, v_ref, q_rim, k_rim, v_rim, conv_q, conv_k, conv_v)
    for j in range(per_step):
        load_features(taps, j, refs, ext, total, reset, places)
        head = step * per_step + j
        cum[j] = jnp.broadcast_to(column(cum_ref[...], head), (count, DK))
        halfway[j] = jnp.broadcast_to(column(rate_ref[...], head), (count, DK))

    def local(pair, carry):
        at = pl.ds(pl.multiple_of(pair * PAIR, PAIR), PAIR)
        for j in range(per_step):
            g = cum[j, at, :]
            b = halfway[j, at, :]
            u = total[j, 0, at, :]
            c = u * sigmoid(u)
            q = c * (unit_scale(c) * DK**-0.5)
            u = total[j, 1, at, :]
            c = u * sigmoid(u)
            k = c * unit_scale(c)
            k_low = low(k)
            spread = jnp.where(within, jnp.exp(jnp.where(within, g - g.T, 0.0)), 0.0)
            keys = mm_nt(k_low, k_low)
            lower[j, at, :] = low(jnp.where(below, b * keys * spread, 0.0))
            score[j, at, :] = low(mm_nt(low(q), k_low) * spread)
            grown = jnp.exp(g)
            for half in range(DV // DK):
                u = total[j, 2 + half, at, :]
                scaled_v[j, at, half * DK : (half + 1) * DK] = low(b * (u * sigmoid(u)))
            grown_k[j, at, :] = low(b * grown * k)
            tail[j, at, :] = low(jnp.exp(block_ends(g) - g) * k)
            grown_q[j, at, :] = grown * q
        return carry

    lax.fori_loop(0, pairs, local, 0, unroll=3)

    masks = masks_low(row, col)
    spots = [
        (j, slice(pair * PAIR, (pair + 1) * PAIR))
        for pair in range(pairs)
        for j in range(per_step)
    ]
    eye = low(jnp.where(row == col, 1.0, 0.0))
    for j, at in spots:
        inverse_ref[j, at, :] = eye - lower[j, at, :] * masks[0]
    for mask in masks[1:]:
        for j, at in spots:
            halfway[j, at, :] = mm(lower[j, at, :] * mask, inverse_ref[j, at, :])
        for j, at in spots:
            inverse = inverse_ref[j, at, :]
            inverse_ref[j, at, :] = inverse - low(mm(inverse, low(halfway[j, at, :])))

    def combine(pair, carry):
        at = pl.ds(pl.multiple_of(pair * PAIR, PAIR), PAIR)
        for j in range(per_step):
            cols = slice(j * DK, (j + 1) * DK)
            wide = slice(j * DV, (j + 1) * DV)
            inverse = inverse_ref[j, at, :]
            scored = score[j, at, :]
            u_low = low(mm(inverse, scaled_v[j, at, :]))
            w_low = low(mm(inverse, grown_k[j, at, :]))
            mixed_ref[at, wide] = mm(scored, u_low)
            pass_ref[at, cols] = low(grown_q[j, at, :] - mm(scored, w_low))
            falls = tail[j, at, :]
            for half in range(2):
                part = slice(half * GROUP, (half + 1) * GROUP)
                turn_ref[j, 2 * pair + half] = low(mm_tn(falls[part], w_low[part]))
                gain_ref[j, 2 * pair + half] = low(mm_tn(falls[part], u_low[part]))
        return carry

    lax.fori_loop(0, pairs, combine, 0, unroll=3)

    for j in range(per_step):
        states[j] = jnp.concatenate(
            [jnp.where(row == col, 1.0, 0.0), jnp.zeros((DK, DV), jnp.float32)], axis=1
        )

    def advance(block, carry):
        begin = base + block * GROUP
        keep = jnp.where((begin != 0) & (begin != first), 1.0, 0.0)
        for j in range(per_step):
            state = states[j] * keep
            state_low = low(state)
            starts[j, block] = state_low
            last = jnp.exp(cum[j, pl.ds(block * GROUP + GROUP - 1, 1), :])
            last = jnp.concatenate([last] * 3, axis=1)
            moved = last * state - mm(turn_ref[j, block], state_low)
            states[j, :, :DK] = moved[:, :DK]
            states[j, :, DK:] = moved[:, DK:] + high(gain_ref[j, block])
        return carry

    lax.fori_loop(0, blocks, advance, 0, unroll=4)

    def close(block, carry):
        at = pl.ds(pl.multiple_of(block * GROUP, GROUP), GROUP)
        for j in range(per_step):
            cols = slice(j * DK, (j + 1) * DK)
            wide = slice(j * DV, (j + 1) * DV)
            out = mm(pass_ref[at, cols], starts[j, block])
            reach_ref[at, cols] = low(out[:, :DK])
            mixed_ref[at, wide] = mixed_ref[at, wide] + out[:, DK:]
        return carry

    lax.fori_loop(0, blocks, close, 0, unroll=6)
    for j in range(per_step):
        map_ref[j] = low(states[j, :, :DK])
        add_ref[j] = low(states[j, :, DK:])


def spec(shape, index):
    return pl.BlockSpec(shape, index)


def state_forward(q, k, v, rims, convs, decay, beta, decay_log, decay_bias, spot, per_step):
    count = q.shape[0]
    heads = decay.shape[1]
    taps = convs[0].shape[0]
    n = per_step
    blocks = count // GROUP
    along = lambda i: (0, i)
    fixed = lambda i: (0, 0)
    lead = lambda i: (i, 0, 0)
    lead4 = lambda i: (i, 0, 0, 0)
    f32, bf16 = jnp.float32, jnp.bfloat16
    shape = jax.ShapeDtypeStruct
    vm = pltpu.VMEM
    return pl.pallas_call(
        functools.partial(state_kernel, taps, n),
        grid=(heads // n,),
        in_specs=[
            pl.BlockSpec(memory_space=pltpu.SMEM),
            spec((count, n * DK), along),
            spec((count, n * DK), along),
            spec((count, n * DV), along),
            spec((RIM, n * DK), along),
            spec((RIM, n * DK), along),
            spec((RIM, n * DV), along),
            spec((taps, n * DK), along),
            spec((taps, n * DK), along),
            spec((taps, n * DV), along),
            spec((count, heads), fixed),
            spec((count, heads), fixed),
            spec((1, heads), fixed),
            spec((1, heads), fixed),
        ],
        out_specs=[
            spec((count, n * DV), along),
            spec((count, n * DK), along),
            spec((n, DK, DK), lead),
            spec((n, DK, DV), lead),
            spec((n, count, PAIR), lead),
            spec((count, n * DK), along),
            spec((n, blocks, DK, DK), lead4),
            spec((n, blocks, DK, DV), lead4),
            spec((count, heads), fixed),
            spec((count, heads), fixed),
        ],
        out_shape=[
            shape((count, heads * DV), f32),
            shape((count, heads * DK), bf16),
            shape((heads, DK, DK), bf16),
            shape((heads, DK, DV), bf16),
            shape((heads, count, PAIR), bf16),
            shape((count, heads * DK), bf16),
            shape((heads, blocks, DK, DK), bf16),
            shape((heads, blocks, DK, DV), bf16),
            shape((count, heads), f32),
            shape((count, heads), f32),
        ],
        scratch_shapes=[
            vm((n, 4, count + RIM, DK), f32),
            vm((n, 4, count, DK), f32),
            vm((n, count, DK), f32),
            vm((n, count, PAIR), bf16),
            vm((n, count, PAIR), f32),
            vm((n, count, PAIR), bf16),
            vm((n, count, DK), f32),
            vm((n, count, DK), bf16),
            vm((n, count, DV), bf16),
            vm((n, count, DK), bf16),
            vm((n, DK, DK + DV), f32),
            vm((n, blocks, DK, DK + DV), bf16),
        ],
        compiler_params=pltpu.CompilerParams(
            dimension_semantics=("arbitrary",), vmem_limit_bytes=VMEM_BYTES
        ),
        cost_estimate=LITTLE,
    )(spot, q, k, v, *rims, *convs, decay, beta, decay_log, decay_bias)


def silu(value):
    return value * sigmoid(value)


def gate_kernel(per_step, mixed_ref, reach_ref, map_ref, add_ref, far_ref, gate_ref, gain_ref, gated_ref, kept_ref, start_ref):
    for j in range(per_step):
        cols = slice(j * DK, (j + 1) * DK)
        wide = slice(j * DV, (j + 1) * DV)
        start = low(high(add_ref[j]) + mm(map_ref[j], far_ref[j]))
        start_ref[j] = start
        mixed = mixed_ref[:, wide] + mm(reach_ref[:, cols], start)
        kept_ref[:, wide] = low(mixed)
        scale = lax.rsqrt(jnp.mean(mixed * mixed, axis=-1, keepdims=True) + EPS)
        gated_ref[:, wide] = low(mixed * scale * gain_ref[...] * silu(gate_ref[:, wide]))


def gate_forward(mixed, reach, near_map, near_add, far_add, gate, gain, per_step):
    count = mixed.shape[0]
    heads = near_map.shape[0]
    n = per_step
    along = lambda i: (0, i)
    lead = lambda i: (i, 0, 0)
    bf16 = jnp.bfloat16
    return pl.pallas_call(
        functools.partial(gate_kernel, n),
        grid=(heads // n,),
        in_specs=[
            spec((count, n * DV), along),
            spec((count, n * DK), along),
            spec((n, DK, DK), lead),
            spec((n, DK, DV), lead),
            spec((n, DK, DV), lead),
            spec((count, n * DV), along),
            spec((1, DV), lambda i: (0, 0)),
        ],
        out_specs=[
            spec((count, n * DV), along),
            spec((count, n * DV), along),
            spec((n, DK, DV), lead),
        ],
        out_shape=[
            jax.ShapeDtypeStruct((count, heads * DV), bf16),
            jax.ShapeDtypeStruct((count, heads * DV), bf16),
            jax.ShapeDtypeStruct((heads, DK, DV), bf16),
        ],
        compiler_params=pltpu.CompilerParams(
            dimension_semantics=("arbitrary",), vmem_limit_bytes=VMEM_BYTES
        ),
        cost_estimate=LITTLE,
    )(mixed, reach, near_map, near_add, far_add, gate, gain)


def gate_back_kernel(per_step, d_gated_ref, kept_ref, reach_ref, gate_ref, gain_ref, d_mixed_ref, d_gate_ref, d_start_ref, d_gain_ref):
    @pl.when(pl.program_id(0) == 0)
    def _():
        d_gain_ref[...] = jnp.zeros_like(d_gain_ref)

    for j in range(per_step):
        cols = slice(j * DK, (j + 1) * DK)
        wide = slice(j * DV, (j + 1) * DV)
        mixed = high(kept_ref[:, wide])
        scale = lax.rsqrt(jnp.mean(mixed * mixed, axis=-1, keepdims=True) + EPS)
        normal = mixed * scale
        gate = gate_ref[:, wide]
        sig = sigmoid(gate)
        d_gated = d_gated_ref[:, wide]
        d_scaled = d_gated * (gate * sig)
        d_gain_ref[...] += jnp.sum(d_scaled * normal, axis=0, keepdims=True)
        d_gate_ref[:, wide] = low(
            d_gated * (normal * gain_ref[...]) * (sig * (1.0 + gate * (1.0 - sig)))
        )
        d_normal = d_scaled * gain_ref[...]
        d_mixed = low(scale * (d_normal - normal * jnp.mean(d_normal * normal, axis=-1, keepdims=True)))
        d_mixed_ref[:, wide] = d_mixed
        d_start_ref[j] = low(mm_tn(reach_ref[:, cols], d_mixed))


def gate_backward(d_gated, kept, reach, gate, gain, per_step):
    count = kept.shape[0]
    heads = kept.shape[1] // DV
    n = per_step
    along = lambda i: (0, i)
    lead = lambda i: (i, 0, 0)
    bf16 = jnp.bfloat16
    return pl.pallas_call(
        functools.partial(gate_back_kernel, n),
        grid=(heads // n,),
        in_specs=[
            spec((count, n * DV), along),
            spec((count, n * DV), along),
            spec((count, n * DK), along),
            spec((count, n * DV), along),
            spec((1, DV), lambda i: (0, 0)),
        ],
        out_specs=[
            spec((count, n * DV), along),
            spec((count, n * DV), along),
            spec((n, DK, DV), lead),
            spec((1, DV), lambda i: (0, 0)),
        ],
        out_shape=[
            jax.ShapeDtypeStruct((count, heads * DV), bf16),
            jax.ShapeDtypeStruct((count, heads * DV), bf16),
            jax.ShapeDtypeStruct((heads, DK, DV), bf16),
            jax.ShapeDtypeStruct((1, DV), jnp.float32),
        ],
        compiler_params=pltpu.CompilerParams(
            dimension_semantics=("arbitrary",), vmem_limit_bytes=VMEM_BYTES
        ),
        cost_estimate=LITTLE,
    )(d_gated, kept, reach, gate, gain)


def state_back_kernel(
    taps,
    per_step,
    offset,
    extra,
    spot,
    q_ref,
    k_ref,
    v_ref,
    q_rim,
    k_rim,
    v_rim,
    conv_q,
    conv_k,
    conv_v,
    decay_ref,
    log_ref,
    bias_ref,
    cum_ref,
    rate_ref,
    inverse_ref,
    pass_ref,
    turn_ref,
    gain_ref,
    start_ref,
    d_mixed_ref,
    near_ref,
    map_ref,
    far_ref,
    *rest,
):
    (
        dq_ref,
        dk_ref,
        dv_ref,
        dq_rim,
        dk_rim,
        dv_rim,
        dq_end,
        dk_end,
        dv_end,
        d_conv_q,
        d_conv_k,
        d_conv_v,
        d_decay_ref,
        d_beta_ref,
        d_log_ref,
        d_bias_ref,
        ext,
        total,
        query,
        key,
        d_value,
        cum,
        rate,
        starts,
        ends,
        states,
        d_states,
        d_total,
        d_ext,
        d_cum,
        d_rate,
    ) = rest[extra:]
    step = pl.program_id(0)
    count = q_ref.shape[0]
    pairs = count // PAIR
    blocks = count // GROUP
    first, base = spot[0], spot[1]
    reset = reset_row(first, base, count)
    places = reset_places(first, base, reset)

    @pl.when(step == 0)
    def _():
        d_cum[...] = jnp.zeros_like(d_cum)
        d_rate[...] = jnp.zeros_like(d_rate)

    refs = (q_ref, k_ref, v_ref, q_rim, k_rim, v_rim, conv_q, conv_k, conv_v)
    for j in range(per_step):
        load_features(taps, j, refs, ext, total, reset, places)
        head = offset + step * per_step + j
        cum[j] = jnp.broadcast_to(column(cum_ref[...], head), (count, DK))
        rate[j] = jnp.broadcast_to(column(rate_ref[...], head), (count, DK))
        u = total[j, 0]
        c = u * sigmoid(u)
        query[j] = c * (unit_scale(c) * DK**-0.5)
        u = total[j, 1]
        c = u * sigmoid(u)
        key[j] = c * unit_scale(c)
        states[j] = high(start_ref[j])
        d_states[j] = high(near_ref[j]) + mm_tn(map_ref[j], far_ref[j])

    row, col, within, below = grid_masks()

    def keep_of(block):
        begin = base + block * GROUP
        return jnp.where((begin != 0) & (begin != first), 1.0, 0.0)

    def last_of(j, block):
        last = jnp.exp(cum[j, pl.ds(block * GROUP + GROUP - 1, 1), :])
        return jnp.concatenate([last, last], axis=1)

    def chain(block, carry):
        back = blocks - 1 - block
        at = pl.ds(pl.multiple_of(back * GROUP, GROUP), GROUP)
        for j in range(per_step):
            state = states[j] * keep_of(block)
            state_low = low(state)
            starts[j, block] = state_low
            states[j] = (
                last_of(j, block) * state
                - mm(turn_ref[j, block], state_low)
                + high(gain_ref[j, block])
            )
            d_state = d_states[j]
            d_low = low(d_state)
            ends[j, back] = d_low
            d_out = d_mixed_ref[at, j * DV : (j + 1) * DV]
            d_states[j] = keep_of(back) * (
                last_of(j, back) * d_state
                - mm_tn(turn_ref[j, back], d_low)
                + mm_tn(pass_ref[at, j * DK : (j + 1) * DK], d_out)
            )
        return carry

    lax.fori_loop(0, blocks, chain, 0, unroll=3)

    lane = lax.broadcasted_iota(jnp.int32, (PAIR, d_cum.shape[1]), 1)
    tall = lax.broadcasted_iota(jnp.int32, (PAIR, 1), 0)

    def assemble(pair, carry):
        at = pl.ds(pl.multiple_of(pair * PAIR, PAIR), PAIR)
        halves = [slice(half * GROUP, (half + 1) * GROUP) for half in range(2)]
        for j in range(per_step):
            g = cum[j, at, :]
            b = rate[j, at, :]
            k = key[j, at, :]
            q = query[j, at, :]
            v = []
            for half in range(DV // DK):
                u = total[j, 2 + half, at, :]
                v.append(u * sigmoid(u))
            v = jnp.concatenate(v, axis=1)
            bb = jnp.concatenate([b, b], axis=1)
            k_low, q_low = low(k), low(q)
            inverse = inverse_ref[j, at, :]
            spread = jnp.where(within, jnp.exp(jnp.where(within, g - g.T, 0.0)), 0.0)
            grown = jnp.exp(g)
            fall = jnp.exp(block_ends(g) - g)
            scores = mm_nt(q_low, k_low)
            d_out = d_mixed_ref[at, j * DV : (j + 1) * DV]
            grown_k = low(b * grown * k)
            falls = low(fall * k)
            begin = [starts[j, 2 * pair + half] for half in range(2)]
            end = [ends[j, 2 * pair + half] for half in range(2)]
            known = jnp.concatenate(
                [mm(grown_k[part], begin[half]) for half, part in enumerate(halves)], axis=0
            )
            change = low(mm(inverse, low(bb * v - known)))
            pulled = jnp.concatenate(
                [mm(falls[part], end[half]) for half, part in enumerate(halves)], axis=0
            )
            rhs = mm_tn(inverse, low(mm_tn(low(scores * spread), d_out) + pulled))
            rhs_low = low(rhs)
            d_lower = jnp.where(below, -mm_nt(rhs_low, change), 0.0)
            d_score = mm_nt(d_out, change) * spread
            d_gk = jnp.concatenate(
                [-mm_nt(rhs_low[part], begin[half]) for half, part in enumerate(halves)], axis=0
            )
            d_gq = jnp.concatenate(
                [mm_nt(d_out[part], begin[half]) for half, part in enumerate(halves)], axis=0
            )
            d_tail = jnp.concatenate(
                [mm_nt(change[part], end[half]) for half, part in enumerate(halves)], axis=0
            )
            bonus = [jnp.sum(high(begin[half]) * high(end[half])) for half in range(2)]
            d_a = d_lower * mm_nt(k_low, k_low) * spread
            cross = d_a * b + d_score * scores
            gk_k = d_gk * k
            rate_col = jnp.sum(d_a + grown * gk_k, axis=-1, keepdims=True) + jnp.sum(
                rhs * v, axis=-1, keepdims=True
            )
            tail_sum = jnp.sum(d_tail * (fall * k), axis=-1, keepdims=True)
            cum_col = (
                jnp.sum(
                    cross - cross.T + b * grown * gk_k + d_gq * (grown * q), axis=-1, keepdims=True
                )
                - tail_sum
            )
            for half, part in enumerate(halves):
                at_end = half * GROUP + GROUP - 1
                more = jnp.sum(tail_sum[part], axis=0, keepdims=True) + bonus[half] * grown[
                    at_end : at_end + 1, :1
                ]
                cum_col = cum_col + jnp.where(tall == at_end, more, 0.0)
            head = offset + step * per_step + j
            d_cum[at, :] = d_cum[at, :] + jnp.where(lane == head, cum_col, 0.0)
            d_rate[at, :] = d_rate[at, :] + jnp.where(lane == head, rate_col, 0.0)
            d_keys = d_lower * spread * b
            d_keys = low(d_keys + d_keys.T)
            d_score_low = low(d_score)
            d_query = grown * d_gq + mm(d_score_low, k_low)
            d_key = b * grown * d_gk + fall * d_tail + mm(d_keys, k_low) + mm_tn(d_score_low, q_low)
            query[j, at, :] = d_query
            key[j, at, :] = d_key
            d_value[j, at, :] = bb * rhs
        return carry

    lax.fori_loop(0, pairs, assemble, 0, unroll=6)

    d_total[0:RIM, :] = jnp.zeros((RIM, DK), jnp.float32)
    d_total[RIM + count : 2 * RIM + count, :] = jnp.zeros((RIM, DK), jnp.float32)

    def conv_back(rows, weight, out_ref, rim_ref, end_ref, d_weight_ref, cols):
        size = count + RIM
        spread_rows = None
        grads = []
        for tap in range(taps):
            moved = d_total[taps - 1 - tap : taps - 1 - tap + size, :]
            term = moved * weight[tap : tap + 1, :]
            spread_rows = term if spread_rows is None else spread_rows + term
            grads.append(jnp.sum(moved * rows[...], axis=0, keepdims=True))
        d_ext[...] = spread_rows
        near = d_total[pl.ds(reset + RIM, RIM), :]
        around = rows[pl.ds(reset, 2 * RIM), :]
        wrong_rows = jnp.zeros((2 * RIM, DK), jnp.float32)
        for tap in range(taps - 1):
            lead = RIM - taps + 1 + tap
            wrong = jnp.where(places >= taps - 1 - tap, 0.0, near)
            grads[tap] = grads[tap] - jnp.sum(
                wrong * around[lead : lead + RIM], axis=0, keepdims=True
            )
            wrong_rows = wrong_rows + jnp.concatenate(
                [
                    jnp.zeros((lead, DK), jnp.float32),
                    wrong * weight[tap : tap + 1, :],
                    jnp.zeros((RIM - lead, DK), jnp.float32),
                ],
                axis=0,
            )
        d_ext[pl.ds(reset, 2 * RIM), :] = d_ext[pl.ds(reset, 2 * RIM), :] - wrong_rows
        d_weight_ref[:, cols] = jnp.concatenate(grads, axis=0)
        rim_ref[:, cols] = d_ext[0:RIM, :]
        out_ref[:, cols] = low(d_ext[RIM : RIM + count, :])
        end_ref[:, cols] = d_ext[count : count + RIM, :]

    for j in range(per_step):
        cols = slice(j * DK, (j + 1) * DK)

        def unit_back(piece, d_unit, factor):
            u = total[j, piece]
            sig = sigmoid(u)
            c = u * sig
            scale = unit_scale(c)
            unit = c * scale
            d_unit = d_unit * factor
            d_c = scale * (d_unit - unit * jnp.sum(d_unit * unit, axis=-1, keepdims=True))
            d_total[RIM : RIM + count, :] = d_c * (sig * (1.0 + u * (1.0 - sig)))

        unit_back(0, query[j], DK**-0.5)
        conv_back(ext.at[j, 0], conv_q[:, cols], dq_ref, dq_rim, dq_end, d_conv_q, cols)
        unit_back(1, key[j], 1.0)
        conv_back(ext.at[j, 1], conv_k[:, cols], dk_ref, dk_rim, dk_end, d_conv_k, cols)
        for half in range(DV // DK):
            begin = j * DV + half * DK
            cut = slice(begin, begin + DK)
            u = total[j, 2 + half]
            sig = sigmoid(u)
            d_total[RIM : RIM + count, :] = d_value[j, :, half * DK : (half + 1) * DK] * (
                sig * (1.0 + u * (1.0 - sig))
            )
            conv_back(ext.at[j, 2 + half], conv_v[:, cut], dv_ref, dv_rim, dv_end, d_conv_v, cut)

    @pl.when(step == pl.num_programs(0) - 1)
    def _():
        shifted_in = decay_ref[...] + bias_ref[...]
        soft = jnp.maximum(shifted_in, 0.0) + jnp.log1p(jnp.exp(-jnp.abs(shifted_in)))
        speed = -jnp.exp(log_ref[...])
        after = jnp.where(within, 1.0, 0.0)
        d_log = jnp.zeros_like(d_log_ref)
        d_bias = jnp.zeros_like(d_bias_ref)
        for pair in range(pairs):
            rows = slice(pair * PAIR, (pair + 1) * PAIR)
            d_decay = lax.dot_general(
                after,
                d_cum[rows, :],
                (((0,), (0,)), ((), ())),
                precision=lax.Precision.HIGHEST,
                preferred_element_type=jnp.float32,
            )
            d_log = d_log + jnp.sum(d_decay * (speed * soft[rows]), axis=0, keepdims=True)
            d_in = d_decay * speed * jax.nn.sigmoid(shifted_in[rows])
            d_bias = d_bias + jnp.sum(d_in, axis=0, keepdims=True)
            d_decay_ref[rows, :] = d_in
        d_log_ref[...] = d_log
        d_bias_ref[...] = d_bias
        rates = rate_ref[...]
        d_beta_ref[...] = d_rate[...] * rates * (1.0 - rates)


def state_backward(
    q, k, v, rims, convs, decay, decay_log, decay_bias, cum, rate, saved, start, d_mixed, near, near_map, far, spot, per_step, offset, held, after
):
    count = q.shape[0]
    heads = decay.shape[1]
    taps = convs[0].shape[0]
    n = per_step
    blocks = count // GROUP
    skip = offset // n
    along = lambda i: (0, i + skip)
    fixed = lambda i: (0, 0)
    lead = lambda i: (i + skip, 0, 0)
    lead4 = lambda i: (i + skip, 0, 0, 0)
    out_along = lambda i: (0, i)
    f32, bf16 = jnp.float32, jnp.bfloat16
    shape = jax.ShapeDtypeStruct
    vm = pltpu.VMEM
    thin = [(RIM, DK), (RIM, DK), (RIM, DV)]
    out_blocks = [(count, DK), (count, DK), (count, DV)] + thin + thin
    out_blocks += [(taps, DK), (taps, DK), (taps, DV)]
    tables = [(count, heads), (count, heads), (1, heads), (1, heads)]
    return pl.pallas_call(
        functools.partial(state_back_kernel, taps, n, offset, len(after)),
        grid=(held // n,),
        in_specs=[
            pl.BlockSpec(memory_space=pltpu.SMEM),
            spec((count, n * DK), along),
            spec((count, n * DK), along),
            spec((count, n * DV), along),
            spec((RIM, n * DK), along),
            spec((RIM, n * DK), along),
            spec((RIM, n * DV), along),
            spec((taps, n * DK), along),
            spec((taps, n * DK), along),
            spec((taps, n * DV), along),
            spec((count, heads), fixed),
            spec((1, heads), fixed),
            spec((1, heads), fixed),
            spec((count, heads), fixed),
            spec((count, heads), fixed),
            spec((n, count, PAIR), lead),
            spec((count, n * DK), along),
            spec((n, blocks, DK, DK), lead4),
            spec((n, blocks, DK, DV), lead4),
            spec((n, DK, DV), lead),
            spec((count, n * DV), along),
            spec((n, DK, DV), lead),
            spec((n, DK, DK), lead),
            spec((n, DK, DV), lead),
        ]
        + [pl.BlockSpec(memory_space=pl.ANY) for _ in after],
        out_specs=[spec((rows, n * width), out_along) for rows, width in out_blocks]
        + [spec(block, fixed) for block in tables],
        out_shape=[
            shape((rows, held * width), bf16 if i < 3 else f32)
            for i, (rows, width) in enumerate(out_blocks)
        ]
        + [shape(block, f32) for block in tables],
        scratch_shapes=[
            vm((n, 4, count + RIM, DK), f32),
            vm((n, 4, count, DK), f32),
            vm((n, count, DK), f32),
            vm((n, count, DK), f32),
            vm((n, count, DV), f32),
            vm((n, count, DK), f32),
            vm((n, count, DK), f32),
            vm((n, blocks, DK, DV), bf16),
            vm((n, blocks, DK, DV), bf16),
            vm((n, DK, DV), f32),
            vm((n, DK, DV), f32),
            vm((count + 2 * RIM, DK), f32),
            vm((count + RIM, DK), f32),
            vm((count, heads), f32),
            vm((count, heads), f32),
        ],
        compiler_params=pltpu.CompilerParams(
            dimension_semantics=("arbitrary",), vmem_limit_bytes=VMEM_BYTES
        ),
        cost_estimate=LITTLE,
    )(
        spot,
        q,
        k,
        v,
        *rims,
        *convs,
        decay,
        decay_log,
        decay_bias,
        cum,
        rate,
        *saved,
        start,
        d_mixed,
        near,
        near_map,
        far,
        *after,
    )


def shifted(value, axis, steps):
    count = lax.axis_size(axis)
    leading, last = (max(0, -steps), min(count, count - steps))
    return lax.ppermute(value, axis, [(source, source + steps) for source in range(leading, last)])


def rms_scale(values, gain):
    return values * lax.rsqrt(jnp.mean(values * values, axis=-1, keepdims=True) + EPS) * gain


def swish_product(gate_ffn, up_ffn):
    return jax.nn.silu(gate_ffn) * up_ffn


def project(rows, weight):
    return jnp.dot(rows, weight, preferred_element_type=jnp.float32)


def rows_product(left, right):
    return jnp.dot(left, right, preferred_element_type=jnp.float32)


def rows_back(left, weight):
    return jnp.einsum("tc,dc->td", left, weight, preferred_element_type=jnp.float32)


def weight_grad(rows, grads):
    return jnp.einsum("td,tc->dc", rows, grads, preferred_element_type=jnp.float32)


STAGES = {"x": ("seq", 0, 1), "y": ("seq", 1, 2), "l": ("dp", 0, 4), "h": ("dp", 1, 8)}


def trade(value, stage):
    axis, bit, _ = STAGES[stage]
    count = lax.axis_size(axis)
    return lax.ppermute(value, axis, [(place, place ^ (1 << bit)) for place in range(count)])


def arrange_kernel(per_head, picks, full_ref, mine_ref, other_ref, *rest):
    out_ref = rest[-1]
    width = full_ref.shape[1] // 16
    mine = (pl.program_id(0) // per_head) == picks[16]
    for place in range(16):
        source = pl.ds(pl.multiple_of(picks[place] * width, width), width)
        target = slice(place * width, (place + 1) * width)
        out_ref[0, :, target] = full_ref[:, source]

    def fill(part_ref):
        for place in range(16):
            source = pl.ds(pl.multiple_of(picks[place] * width, width), width)
            out_ref[1, :, place * width : (place + 1) * width] = part_ref[:, source]

    @pl.when(mine)
    def _():
        fill(mine_ref)

    @pl.when(jnp.logical_not(mine))
    def _():
        fill(other_ref)


def with_other(got):
    if lax.axis_size("heads") == 2:
        return got, lax.ppermute(got, "heads", [(0, 1), (1, 0)])
    whole = heads_gather(got)
    return whole, whole


def paired_rows(full, got, order, *after):
    order = order[1:] + order[:1]
    own = lax.axis_index("dp") * lax.axis_size("seq") + lax.axis_index("seq")
    masks = [
        sum(STAGES[stage][2] for k, stage in enumerate(order) if place >> (3 - k) & 1)
        for place in range(16)
    ]
    picks = jnp.concatenate(
        [own ^ jnp.array(masks, jnp.int32), lax.axis_index("heads").astype(jnp.int32)[None]]
    )
    got, other = got
    count, width = full.shape
    size = 192 if got.shape[0] % 192 == 0 else 96
    blocks = got.shape[0] // size
    piece = pl.BlockSpec((size, width), lambda i: (i, 0))
    part = pl.BlockSpec((size, width), lambda i: (lax.rem(i, blocks), 0))
    both = pl.pallas_call(
        functools.partial(arrange_kernel, blocks),
        grid=(count // size,),
        in_specs=[pl.BlockSpec(memory_space=pltpu.SMEM), piece, part, part]
        + [pl.BlockSpec(memory_space=pl.ANY) for _ in after],
        out_specs=pl.BlockSpec((2, size, width), lambda i: (0, i, 0)),
        out_shape=jax.ShapeDtypeStruct((2, count, width), full.dtype),
        compiler_params=pltpu.CompilerParams(
            dimension_semantics=("arbitrary",), vmem_limit_bytes=VMEM_BYTES
        ),
        cost_estimate=LITTLE,
    )(picks, full, got, other, *after)
    return both.reshape(-1, width)


def own_side(stage):
    axis, bit, _ = STAGES[stage]
    return lax.rem(lax.axis_index(axis) // (1 << bit), 2)


def pick_half(grads, order, which):
    half = grads.shape[1] // 2
    side = own_side(order[0])
    return lax.dynamic_slice_in_dim(grads, (side if which else 1 - side) * half, half, 1)


def join_halves(grads, got, order):
    return jnp.concatenate([pick_half(grads, order, 1), got], axis=0)


def trade_halves(grads, order):
    return join_halves(grads, trade(pick_half(grads, order, 0), order[0]), order)


def pair_grad(rows, grads, begin, end):
    width = rows.shape[1] // 16
    return weight_grad(rows[:, begin * width : end * width], grads)


def grad_open(rows, grads, order):
    sent = low(pair_grad(rows, grads, 8, 16))
    return rows, grads, sent, trade(sent, order[1])


def grad_next(opened, order):
    rows, grads, _, first = opened
    middle = first.shape[0] // 2
    sent = low(pair_grad(rows, grads, 4, 8) + high(first[middle:]))
    rest = pair_grad(rows, grads, 0, 4) + high(first[:middle])
    return rest, sent, trade(sent, order[2])


def grad_last(moved):
    rest, _, second = moved
    return low(rest + high(second))


def finish_kernel(plan, head_steps, *refs):
    groups = len(plan)
    grads, small_ref = refs[:groups], refs[groups]
    outs, small_out = refs[groups + 1 : 2 * groups + 1], refs[2 * groups + 1]
    scratch = refs[2 * groups + 2 :]
    buffers = []
    for stages, _ in plan:
        buffers.append(scratch[: len(stages)])
        scratch = scratch[len(stages) :]
    small_sum, small_got, send_sem, recv_sem, small_send, small_recv = scratch

    def side(stage):
        axis, bit, _ = STAGES[stage]
        return lax.rem(lax.axis_index(axis) // (1 << bit), 2)

    def partner(stage):
        axis, bit, _ = STAGES[stage]
        return {axis: lax.axis_index(axis) + (1 - 2 * side(stage)) * (1 << bit)}

    def head_partner(step):
        me = lax.axis_index("heads")
        return {"heads": me + (1 - 2 * lax.rem(me // step, 2)) * step}

    barrier = pltpu.get_barrier_semaphore()
    targets = [partner(stage) for stage in "xylh"] + [head_partner(step) for step in head_steps]
    for target in targets:
        pl.semaphore_signal(
            barrier, inc=1, device_id=target, device_id_type=pl.DeviceIdType.MESH
        )
    pl.semaphore_wait(barrier, len(targets))

    started = []

    def send(source, target, sems, device):
        copy = pltpu.make_async_remote_copy(
            src_ref=source,
            dst_ref=target,
            send_sem=sems[0],
            recv_sem=sems[1],
            device_id=device,
            device_id_type=pl.DeviceIdType.MESH,
        )
        copy.start()
        started.append(copy)
        return copy

    most = max(len(cuts) for _, cuts in plan)
    longest = max(len(stages) for stages, _ in plan)
    chunks, number = [], 0
    rounds = [[] for _ in range(most)]
    for g, (stages, cuts) in enumerate(plan):
        for k, cut in enumerate(cuts):
            chunks.append((g, stages, slice(*cut)))
            rounds[k].append(number)
            number += 1
    copies = {}

    def advance(index, step):
        g, stages, cut = chunks[index]
        if step > len(stages):
            return
        if step > 0:
            copies[index, step - 1].wait_recv()
        full = grads[g].shape[0]
        here = buffers[g]
        if step == len(stages):
            there = 1 - side(stages[-1])
            outs[g][pl.ds(there, 1), :, cut] = here[-1][:, cut][None]
            return
        rows = slice(full >> (step + 1), full >> step)
        if step == 0:
            source = grads[g].at[rows, cut]
            if len(stages) == 1:
                outs[g][pl.ds(side(stages[0]), 1), :, cut] = grads[g][: rows.start, cut][None]
        else:
            last = step == len(stages) - 1
            begin = 0 if last else rows.start
            value = high(grads[g][begin : rows.stop, cut])
            for got in here[:step]:
                value = value + high(got[begin : rows.stop, cut])
            if last:
                outs[g][pl.ds(side(stages[-1]), 1), :, cut] = low(value[: rows.start])[None]
                value = value[rows.start :]
            here[0][rows, cut] = low(value)
            source = here[0].at[rows, cut]
        place = 4 * index + step
        copies[index, step] = send(
            source,
            here[step].at[:, cut],
            (send_sem.at[place], recv_sem.at[place]),
            partner(stages[step]),
        )

    small_copies = []
    names = "xylh"

    def small_step(step):
        if step >= 1 and step <= 4:
            small_copies[step - 1].wait_recv()
            small_sum[step] = small_sum[step - 1] + small_got[step - 1]
        if step == 4:
            small_out[pl.ds(lax.axis_index("heads"), 1)] = small_sum[4:5]
        if step < 4:
            if step == 0:
                small_sum[0] = small_ref[...]
            sems = (small_send.at[step], small_recv.at[step])
            small_copies.append(
                send(small_sum.at[step], small_got.at[step], sems, partner(names[step]))
            )
        elif step - 4 <= len(head_steps):
            k = step - 4
            if k >= 1:
                small_copies[step - 1].wait_recv()
            if k < len(head_steps):
                size = head_steps[k]
                begin = lax.axis_index("heads") // size * size
                block = small_out.at[pl.ds(begin, size)]
                sems = (small_send.at[step], small_recv.at[step])
                small_copies.append(send(block, block, sems, head_partner(size)))

    total_small = 5 + len(head_steps)
    small_step(0)
    for ahead in range(min(2, most)):
        for index in rounds[ahead]:
            advance(index, 0)
    for t in range(max(most + longest, total_small - 1)):
        for lag in range(longest):
            if lag == 1 and t + 2 < most:
                for index in rounds[t + 2]:
                    advance(index, 0)
            if 0 <= t - lag < most:
                for index in rounds[t - lag]:
                    advance(index, lag + 1)
        if t + 1 < total_small:
            small_step(t + 1)
    for copy in started:
        copy.wait_send()


def finish(grads, orders, small):
    count = lax.axis_size("heads")
    head_steps = []
    while 1 << len(head_steps) < count:
        head_steps.append(1 << len(head_steps))
    plan, scratch, outs = [], [], []
    for array, order in zip(grads, orders):
        full, half = array.shape
        step = min(256 if len(order) == 4 else 512, half) if half % 128 == 0 else half
        cuts = [(at, min(at + step, half)) for at in range(0, half, step)]
        plan.append((order[1:] + order[:1], cuts))
        for level in range(len(order)):
            scratch.append(pltpu.VMEM((full >> (level + 1), half), jnp.bfloat16))
        outs.append(jax.ShapeDtypeStruct((2, full >> len(order), half), jnp.bfloat16))
    pieces = sum(len(cuts) for _, cuts in plan)
    inside = pl.BlockSpec(memory_space=pltpu.VMEM)
    f32 = jnp.float32
    return pl.pallas_call(
        functools.partial(finish_kernel, tuple(plan), tuple(head_steps)),
        in_specs=[inside] * (len(grads) + 1),
        out_specs=[inside] * (len(grads) + 1),
        out_shape=outs + [jax.ShapeDtypeStruct((count,) + small.shape, f32)],
        scratch_shapes=scratch
        + [
            pltpu.VMEM((5,) + small.shape, f32),
            pltpu.VMEM((4,) + small.shape, f32),
            pltpu.SemaphoreType.DMA((4 * pieces,)),
            pltpu.SemaphoreType.DMA((4 * pieces,)),
            pltpu.SemaphoreType.DMA((8,)),
            pltpu.SemaphoreType.DMA((8,)),
        ],
        compiler_params=pltpu.CompilerParams(
            collective_id=0, has_side_effects=True, vmem_limit_bytes=60 * 1024 * 1024
        ),
        cost_estimate=LITTLE,
    )(*grads, small)


def fence(one, *after):
    return pl.pallas_call(
        lambda one_ref, *rest: rest[-1].__setitem__(..., one_ref[...]),
        in_specs=[pl.BlockSpec(memory_space=pltpu.VMEM)]
        + [pl.BlockSpec(memory_space=pl.ANY) for _ in after],
        out_specs=pl.BlockSpec(memory_space=pltpu.VMEM),
        out_shape=jax.ShapeDtypeStruct(one.shape, one.dtype),
        compiler_params=pltpu.CompilerParams(vmem_limit_bytes=VMEM_BYTES),
        cost_estimate=LITTLE,
    )(one, *after)


def order_kernel(*refs):
    pass


def ordered(values, *after):
    anywhere = pl.BlockSpec(memory_space=pl.ANY)
    return pl.pallas_call(
        order_kernel,
        in_specs=[anywhere] * (len(values) + len(after)),
        out_specs=[anywhere] * len(values),
        out_shape=[jax.ShapeDtypeStruct(part.shape, part.dtype) for part in values],
        input_output_aliases={k: k for k in range(len(values))},
        cost_estimate=LITTLE,
    )(*values, *after)


def heads_gather(rows, axis=0):
    count = lax.axis_size("heads")
    own = lax.axis_index("heads")
    step = 1
    while step < count:
        other = lax.ppermute(rows, "heads", [(place, place ^ step) for place in range(count)])
        upper = lax.rem(own // step, 2) == 1
        rows = jnp.concatenate(
            [jnp.where(upper, other, rows), jnp.where(upper, rows, other)], axis=axis
        )
        step *= 2
    return rows


def heads_sum(compute, count, kind):
    if lax.axis_size("heads") != 2:
        whole = compute(lambda rows: rows).astype(kind)
        return high(lax.psum_scatter(whole, "heads", scatter_dimension=0, tiled=True))
    own = lax.axis_index("heads")
    half = count // 2

    def part(which):
        return compute(lambda rows: lax.dynamic_slice_in_dim(rows, which * half, half, 0))

    got = lax.ppermute(part(1 - own).astype(kind), "heads", [(0, 1), (1, 0)])
    return part(own) + high(got)


ORDERS = ("xylh", "yxlh", "lxyh")
FFN_ORDERS = ("xlyh", "yxlh", "lyhx")


def body(
    hidden_in,
    out_cotangent,
    lengths,
    norm_gain,
    q_weight,
    k_weight,
    v_weight,
    gate_weight,
    decay_weight,
    beta_weight,
    conv_q,
    conv_k,
    conv_v,
    decay_log,
    decay_bias,
    out_gain,
    out_weight,
    ffn_gain,
    ffn_gate,
    ffn_up,
    ffn_down,
):
    resid = hidden_in[0].astype(jnp.float32)
    normed_own = rms_scale(resid, norm_gain).astype(jnp.bfloat16)
    normed, cotangent = (
        heads_gather(normed_own),
        heads_gather(out_cotangent[0]),
    )
    span = normed.shape[0]
    normed_got = {order: trade(normed_own, order[0]) for order in ORDERS[:2]}
    cotangent_got = trade(out_cotangent[0], FFN_ORDERS[2][0])
    taps = conv_q.shape[0]
    q_proj = project(normed, q_weight)
    k_proj = project(normed, k_weight)
    v_proj = project(normed, v_weight)
    gate_proj = project(normed, gate_weight)
    heads = decay_weight.shape[1]
    per_step = min(2, heads)
    narrow = project(normed, jnp.concatenate([decay_weight, beta_weight], axis=1))
    decay_proj, beta_proj = narrow[:, :heads], narrow[:, heads:]
    seq_index = lax.axis_index("seq")
    spot = jnp.stack([lengths[0, 0], seq_index * span]).astype(jnp.int32)
    ends = [part[span - RIM :] for part in (q_proj, k_proj, v_proj)]
    rims = jnp.split(
        shifted(jnp.concatenate(ends, axis=1), "seq", 1), (heads * DK, 2 * heads * DK), axis=1
    )
    convs = (conv_q, conv_k, conv_v)
    log_row, bias_row, gain_row = decay_log[None], decay_bias[None], out_gain[None]
    mixed_local, reach, span_map, span_add, *saved, cum, rate = state_forward(
        q_proj, k_proj, v_proj, rims, convs, decay_proj, beta_proj, log_row, bias_row, spot, per_step
    )
    span_map, span_add = ordered((span_map, span_add), cotangent_got, *normed_got.values())
    normed_got = {order: with_other(got) for order, got in normed_got.items()}
    cotangent_got = with_other(cotangent_got)
    near_map, near_add = shifted((span_map, span_add), "seq", 1)
    far_add = shifted(span_add, "seq", 2)
    next_map = shifted(span_map, "seq", -1)
    (mixed_local,) = ordered((mixed_local,), next_map)
    gated_low, mixed_low, start_state = gate_forward(
        mixed_local, reach, near_map, near_add, far_add, gate_proj, gain_row, per_step
    )
    (gated_low,) = ordered(
        (gated_low,), cotangent_got[1], *(got[1] for got in normed_got.values())
    )
    mixer = heads_sum(
        lambda pick: rows_product(pick(gated_low), out_weight), span, jnp.bfloat16
    )
    resid_mid = resid + mixer
    ffn_own = rms_scale(resid_mid, ffn_gain).astype(jnp.bfloat16)
    ffn_in = heads_gather(ffn_own)
    ffn_got = {order: trade(ffn_own, order[0]) for order in FFN_ORDERS[:2]}
    gate_ffn = project(ffn_in, ffn_gate)
    up_ffn = project(ffn_in, ffn_up)
    act, act_pull = jax.vjp(swish_product, gate_ffn, up_ffn)
    act_low = act.astype(jnp.bfloat16)
    d_act = jnp.einsum("td,fd->tf", cotangent, ffn_down, preferred_element_type=jnp.float32)
    d_gate_ffn, d_up_ffn = act_pull(d_act)
    d_gate_low = d_gate_ffn.astype(jnp.bfloat16)
    d_up_low = d_up_ffn.astype(jnp.bfloat16)
    ffn_low = (d_gate_low, d_up_low, act_low)
    theirs = [pick_half(part, order, 0) for part, order in zip(ffn_low, FFN_ORDERS)]
    ffn_traded = [trade(part, order[0]) for part, order in zip(theirs, FFN_ORDERS)]
    ffn_low = ordered(ffn_low, *ffn_got.values(), *theirs)
    d_gate_low, d_up_low, act_low = ffn_low
    ffn_got = {order: with_other(got) for order, got in ffn_got.items()}
    gate_halves, up_halves, down_halves = (
        join_halves(part, got, order)
        for part, got, order in zip(ffn_low, ffn_traded, FFN_ORDERS)
    )
    ffn_out = heads_sum(lambda pick: rows_product(pick(act_low), ffn_down), span, jnp.bfloat16)
    output = (resid_mid + ffn_out).astype(jnp.bfloat16)
    cotangent_rel = paired_rows(cotangent, cotangent_got, FFN_ORDERS[2], act_low)
    ffn_rel = [
        paired_rows(ffn_in, ffn_got[order], order, d_gate_low) for order in FFN_ORDERS[:2]
    ]
    gate_open = grad_open(ffn_rel[0], gate_halves, FFN_ORDERS[0])
    up_open = grad_open(ffn_rel[1], up_halves, FFN_ORDERS[1])
    down_open = grad_open(cotangent_rel, down_halves, FFN_ORDERS[2])
    d_ffn = heads_sum(
        lambda pick: rows_back(pick(d_gate_low), ffn_gate) + rows_back(pick(d_up_low), ffn_up),
        span,
        jnp.bfloat16,
    )
    _, ffn_norm_pull = jax.vjp(rms_scale, resid_mid, ffn_gain)
    d_mid_norm, d_ffn_gain = ffn_norm_pull(d_ffn)
    d_mid = out_cotangent[0].astype(jnp.float32) + d_mid_norm
    d_mid_low = low(d_mid)
    d_mid_all = heads_gather(d_mid_low)
    d_mid_got = with_other(trade(d_mid_low, ORDERS[2][0]))
    d_gated = jnp.einsum("td,cd->tc", d_mid_all, out_weight, preferred_element_type=jnp.float32)
    d_mixed, d_gate_low_mix, d_start, d_out_gain = gate_backward(
        d_gated, mixed_low, reach, gate_proj, gain_row, per_step
    )
    next_start = shifted(d_start, "seq", -1)
    beyond_start = shifted(d_start, "seq", -2)
    mix_halves = trade_halves(d_gate_low_mix, ORDERS[0])
    (gated_low,) = ordered((gated_low,), d_gate_low_mix)
    out_halves = trade_halves(gated_low, ORDERS[2])
    normed_rel = [
        paired_rows(normed, normed_got[order], order, up_open[2]) for order in ORDERS[:2]
    ]
    d_mid_rel = paired_rows(d_mid_all, d_mid_got, ORDERS[2], up_open[2])
    moved = [
        grad_next(opened, order)
        for opened, order in zip((gate_open, up_open, down_open), FFN_ORDERS)
    ]
    back = state_backward(
        q_proj,
        k_proj,
        v_proj,
        rims,
        convs,
        decay_proj,
        log_row,
        bias_row,
        cum,
        rate,
        saved,
        start_state,
        d_mixed,
        next_start,
        next_map,
        beyond_start,
        spot,
        per_step,
        0,
        heads,
        [part[1] for part in moved] + [d_mid_rel, *normed_rel],
    )
    rim = jnp.concatenate(back[3:6], axis=1)
    (rim,) = ordered((rim,), *(part[2] for part in moved))
    rim = shifted(rim, "seq", -1)
    passed = jnp.split(rim, (heads * DK, 2 * heads * DK), axis=1)
    d_q_low, d_k_low, d_v_low = (
        lax.dynamic_update_slice_in_dim(whole, low(end + more), span - RIM, 0)
        for whole, end, more in zip(back[0:3], back[6:9], passed)
    )
    d_decay_low, d_beta_low = low(back[12]), low(back[13])
    flat_lows = (jnp.concatenate([d_q_low, d_k_low], axis=1), d_v_low)
    late = [pick_half(part, order, 0) for part, order in zip(flat_lows, ORDERS)]
    late_got = [trade(part, order[0]) for part, order in zip(late, ORDERS)]
    d_gate_low_mix, d_mid_rel, *normed_rel = ordered(
        (d_gate_low_mix, d_mid_rel, *normed_rel), *late
    )
    tails = [
        grad_last(moved[0]),
        grad_last(moved[1]),
        grad_last(moved[2]),
        low(pair_grad(normed_rel[0], mix_halves, 0, 16)),
        low(pair_grad(d_mid_rel, out_halves, 0, 16)),
    ]
    tail_orders = [order[:1] + order[3:] for order in FFN_ORDERS] + [ORDERS[0], ORDERS[2]]
    for flat_low, got, rows, order in zip(flat_lows, late_got, normed_rel, ORDERS):
        tails.append(low(pair_grad(rows, join_halves(flat_low, got, order), 0, 16)))
        tail_orders.append(order)
    narrow_grad = weight_grad(jnp.concatenate([d_decay_low, d_beta_low], axis=1), normed)
    pairs = (
        (d_q_low, q_weight),
        (d_k_low, k_weight),
        (d_v_low, v_weight),
        (d_gate_low_mix, gate_weight),
        (d_decay_low, decay_weight),
        (d_beta_low, beta_weight),
    )
    d_normed = heads_sum(
        lambda pick: sum(rows_back(pick(rows), weight) for rows, weight in pairs),
        span,
        jnp.bfloat16,
    )
    _, in_norm_pull = jax.vjp(rms_scale, resid, norm_gain)
    d_in_norm, d_norm_gain = in_norm_pull(d_normed)
    input_grad = d_mid + d_in_norm
    wide = normed.shape[1]
    conv_all = jnp.concatenate(back[9:12], axis=1)

    def full_rows(part):
        return jnp.pad(part, ((0, 0), (0, wide - part.shape[1])))

    conv_rows = [full_rows(conv_all[:, at : at + wide]) for at in range(0, conv_all.shape[1], wide)]
    last_row = full_rows(jnp.concatenate([d_out_gain, back[14], back[15]], axis=1))
    stacked = [narrow_grad] + conv_rows + [d_norm_gain[None], d_ffn_gain[None], last_row]
    flat = jnp.concatenate(stacked, axis=0)
    flat = jnp.pad(flat, ((0, -flat.shape[0] % 8), (0, 0)))
    *sums, everyone = finish(tails, tail_orders, flat)
    grad_gate, grad_up, grad_down, grad_gate_mix, grad_out, grad_qk, grad_v = (
        high(jnp.concatenate([part[0], part[1]], axis=1)) for part in sums
    )
    grad_down, grad_out = grad_down.T, grad_out.T
    grad_q, grad_k = jnp.split(grad_qk, 2, axis=1)
    shard = lax.axis_index("dp") * lax.axis_size("seq") + lax.axis_index("seq")
    size = wide // 16
    narrow_sum = lax.dynamic_slice(
        everyone, (lax.axis_index("heads"), 0, shard * size), (1, 2 * heads, size)
    )[0].T
    grad_decay, grad_beta = narrow_sum[:, :heads], narrow_sum[:, heads:]
    at = 2 * heads
    conv_sum = jnp.concatenate(
        [everyone[:, at + taps * k : at + taps * (k + 1)] for k in range(len(conv_rows))], axis=2
    )
    at += taps * len(conv_rows)
    width_k = heads * DK

    def by_head(part):
        return jnp.swapaxes(part, 0, 1).reshape(part.shape[1], -1)

    width_v = out_gain.shape[0]
    small = [
        everyone[:, at].sum(0),
        everyone[:, at + 1].sum(0),
        everyone[:, at + 2, :width_v].sum(0),
        everyone[:, at + 2, width_v : width_v + heads].reshape(-1),
        everyone[:, at + 2, width_v + heads : width_v + 2 * heads].reshape(-1),
        by_head(conv_sum[:, :, :width_k]),
        by_head(conv_sum[:, :, width_k : 2 * width_k]),
        by_head(conv_sum[:, :, 2 * width_k : 2 * width_k + heads * DV]),
    ]
    return (
        output[None],
        input_grad[None],
        small[0],
        grad_q,
        grad_k,
        grad_v,
        grad_gate_mix,
        grad_decay,
        grad_beta,
        small[5],
        small[6],
        small[7],
        small[3],
        small[4],
        small[2],
        grad_out,
        small[1],
        grad_gate,
        grad_up,
        grad_down,
    )


def solution(mesh):
    in_specs = (
        P("dp", ("seq", "heads"), None),
        P("dp", ("seq", "heads"), None),
        P("dp", None),
        P(),
        P(None, "heads"),
        P(None, "heads"),
        P(None, "heads"),
        P(None, "heads"),
        P(None, "heads"),
        P(None, "heads"),
        P(None, "heads"),
        P(None, "heads"),
        P(None, "heads"),
        P("heads"),
        P("heads"),
        P(),
        P("heads", None),
        P(),
        P(None, "heads"),
        P(None, "heads"),
        P("heads", None),
    )
    out_specs = (
        P("dp", ("seq", "heads"), None),
        P("dp", ("seq", "heads"), None),
        P(),
        P(("dp", "seq"), "heads"),
        P(("dp", "seq"), "heads"),
        P(("dp", "seq"), "heads"),
        P(("dp", "seq"), "heads"),
        P(("dp", "seq"), "heads"),
        P(("dp", "seq"), "heads"),
        P(),
        P(),
        P(),
        P(),
        P(),
        P(),
        P("heads", ("dp", "seq")),
        P(),
        P(("dp", "seq"), "heads"),
        P(("dp", "seq"), "heads"),
        P("heads", ("dp", "seq")),
    )
    return jax.shard_map(body, mesh=mesh, in_specs=in_specs, out_specs=out_specs, check_vma=False)
```
